32 devices in a mesh: seq: 8 (over z, y), batch: 4 (over x, core).
Axes of the slice: x: 2, y: 2, z: 4, core: 2. Of those that a mesh axis runs over, the one named last changes fastest.
Arguments:
- inputs: float32 [8, 1024, 1024], P('batch', 'seq'), may hold values from -6 to 6
- segments: int32 [8, 1024], P('batch', 'seq'), may hold values from 0 to 15, as said below
- w_gate: bfloat16 [1024, 1536], P(('seq', 'batch')), may hold values from -0.1875 to 0.1875
- w_input: bfloat16 [1024, 1536], P(('seq', 'batch')), may hold values from -0.1875 to 0.1875
- w_recur: bfloat16 [1536, 1536], P(('seq', 'batch')), may hold values from -0.15625 to 0.15625
- w_inject: bfloat16 [1536, 1536], P(('seq', 'batch')), may hold values from -0.15625 to 0.15625
- w_output: bfloat16 [1536, 1024], P(('seq', 'batch')), may hold values from -0.15625 to 0.15625
- w_hidden: bfloat16 [1024, 3072], P(('seq', 'batch')), may hold values from -0.1875 to 0.1875
- w_upward: bfloat16 [1024, 3072], P(('seq', 'batch')), may hold values from -0.1875 to 0.1875
- w_down: bfloat16 [3072, 1024], P(('seq', 'batch')), may hold values from -0.109375 to 0.109375
- gain_one: float32 [1024], replicated, may hold values from 0.5 to 1.5
- gain_two: float32 [1024], replicated, may hold values from 0.5 to 1.5
- conv_taps: float32 [4, 1536], replicated, may hold values from -3 to 3
- conv_bias: float32 [1536], replicated, may hold values from -3 to 3
- recur_bias: float32 [1536], replicated, may hold values from -3 to 3
- inject_bias: float32 [1536], replicated, may hold values from -3 to 3
- decay_param: float32 [1536], replicated, may hold values from -13 to -4.6
- cotangent: float32 [8, 1024, 1024], P('batch', 'seq'), may hold values from -6 to 6
Outputs:
- output: float32 [8, 1024, 1024], P('batch', 'seq')
- grad_inputs: float32 [8, 1024, 1024], P('batch', 'seq')
- grad_gate: float32 [1024, 1536], P(('seq', 'batch'))
- grad_input: float32 [1024, 1536], P(('seq', 'batch'))
- grad_recur: float32 [1536, 1536], P(('seq', 'batch'))
- grad_inject: float32 [1536, 1536], P(('seq', 'batch'))
- grad_output: float32 [1536, 1024], P(('seq', 'batch'))
- grad_hidden: float32 [1024, 3072], P(('seq', 'batch'))
- grad_upward: float32 [1024, 3072], P(('seq', 'batch'))
- grad_down: float32 [3072, 1024], P(('seq', 'batch'))
- grad_gain_one: float32 [1024], P(('seq', 'batch'))
- grad_gain_two: float32 [1024], P(('seq', 'batch'))
- grad_taps: float32 [4, 1536], P(None, ('seq', 'batch'))
- grad_conv_bias: float32 [1536], P(('seq', 'batch'))
- grad_recur_bias: float32 [1536], P(('seq', 'batch'))
- grad_inject_bias: float32 [1536], P(('seq', 'batch'))
- grad_decay_param: float32 [1536], P(('seq', 'batch'))
The draws below stay inside these ranges and needn't reach their ends.
Inputs may be any that keep to these rules, and one draw needn't show every extreme that they name: `segments`: along each row the ids start at 0 and never fall, stepping by 0 or 1; in each aligned block of 2 rows one row is a single segment and every other row reaches the largest id.
All inputs are finite; a program needn't handle non-finite values.
Results may differ from the reference program's by a relative error of at most 0.0087.
Values may be sent and summed in bfloat16 or wider, within the bound.
A program may use at most 320 MiB of HBM per device.

```python
import jax
import jax.numpy as jnp
from jax import lax

D = 1024
RNN = 1536
FF = 3072
ROWS_DEV = 2
ROWS = 8
LEN = 1024


def draw_segments(key, part):
    key = jax.random.fold_in(key, 7)
    first_key, second_key = jax.random.split(key)
    column = lax.broadcasted_iota(jnp.int32, (ROWS, LEN), 1)
    random_starts = (jax.random.randint(first_key, (ROWS, LEN), 0, max(LEN // 8, 2)) == 0).astype(jnp.int32)
    forced_starts = (column % (LEN // 16) == 0).astype(jnp.int32)
    starts = jnp.maximum(random_starts, forced_starts)
    starts = jnp.where(column == 0, 0, starts)
    chosen = jax.random.randint(second_key, (ROWS // ROWS_DEV,), 0, ROWS_DEV)
    row_index = lax.broadcasted_iota(jnp.int32, (ROWS,), 0)
    whole_row = row_index % ROWS_DEV == jnp.repeat(chosen, ROWS_DEV, total_repeat_length=ROWS)
    starts = jnp.where(whole_row[:, None], 0, starts)
    return jnp.minimum(jnp.cumsum(starts, axis=1), 15).astype(jnp.int32)


def block_levels(own_key, shape, cuts, smallest, top_value):
    level, own = 1.0, jax.random.fold_in(own_key, 6)
    for dim, parts in cuts:
        draws = jnp.exp(jax.random.uniform(jax.random.fold_in(own, dim), (parts,), jnp.float32, smallest / len(cuts), top_value / len(cuts)))
        level = level * jnp.repeat(draws, shape[dim] // parts).reshape([-1 if axis == dim else 1 for axis in range(len(shape))])
    return level


def gaussian(key, shape, scale, limit, cuts=(), kind=jnp.bfloat16):
    result = scale * jax.random.normal(key, shape, jnp.float32)
    if cuts:
        result = result * block_levels(key, shape, cuts, -0.22, 0.18)
    return jnp.clip(result, -limit, limit).astype(kind)


def setup_inputs(seed: int = 0) -> dict:
    key_of = jax.random.split(jax.random.key(seed), 19)
    return {
        "inputs": gaussian(key_of[0], (ROWS, LEN, D), 1.0, 6.0, ((0, 4), (1, 8)), jnp.float32),
        "segments": draw_segments(jax.random.fold_in(key_of[18], 71), 0),
        "w_gate": gaussian(key_of[2], (D, RNN), D ** -0.5, 0.1875, ((0, 32),)),
        "w_input": gaussian(key_of[3], (D, RNN), D ** -0.5, 0.1875, ((0, 32),)),
        "w_recur": gaussian(key_of[4], (RNN, RNN), RNN ** -0.5, 0.15625, ((0, 32),)),
        "w_inject": gaussian(key_of[5], (RNN, RNN), RNN ** -0.5, 0.15625, ((0, 32),)),
        "w_output": gaussian(key_of[6], (RNN, D), RNN ** -0.5, 0.15625, ((0, 32),)),
        "w_hidden": gaussian(key_of[7], (D, FF), D ** -0.5, 0.1875, ((0, 32),)),
        "w_upward": gaussian(key_of[8], (D, FF), D ** -0.5, 0.1875, ((0, 32),)),
        "w_down": gaussian(key_of[9], (FF, D), FF ** -0.5, 0.109375, ((0, 32),)),
        "gain_one": jnp.clip(1.0 + 0.1 * jax.random.normal(key_of[10], (D,), jnp.float32), 0.5, 1.5),
        "gain_two": jnp.clip(1.0 + 0.1 * jax.random.normal(key_of[11], (D,), jnp.float32), 0.5, 1.5),
        "conv_taps": gaussian(key_of[12], (4, RNN), 0.5, 3.0, (), jnp.float32),
        "conv_bias": gaussian(key_of[13], (RNN,), 0.5, 3.0, (), jnp.float32),
        "recur_bias": gaussian(key_of[14], (RNN,), 0.5, 3.0, (), jnp.float32),
        "inject_bias": gaussian(key_of[15], (RNN,), 0.5, 3.0, (), jnp.float32),
        "decay_param": jnp.clip(jax.random.uniform(key_of[16], (RNN,), jnp.float32, -13.0, -4.6), -13.0, -4.6),
        "cotangent": gaussian(key_of[17], (ROWS, LEN, D), 1.0, 6.0, ((0, 4), (1, 8)), jnp.float32),
    }


@jax.custom_vjp
def low(v):
    return lax.optimization_barrier(v.astype(jnp.bfloat16)).astype(jnp.float32)

@jax.custom_vjp
def low_back(v):
    return v

def low_keep(v):
    return (low(v), None)

def low_pass(kept, grad):
    return (grad,)

def back_keep(v):
    return (v, None)

def back_low(kept, grad):
    return (low(grad),)
low.defvjp(low_keep, low_pass)
low_back.defvjp(back_keep, back_low)
EPSILON = 1e-06
DECAY_SCALE = 8.0
FLOOR_TERM = 0.01

def matmul_high(left, right):
    return jnp.dot(left, right, precision=lax.Precision.HIGHEST, preferred_element_type=jnp.float32)

def rms_norm(values, gain):
    return values * lax.rsqrt(lax.optimization_barrier(jnp.mean(values * values, axis=-1, keepdims=True)) + EPSILON) * gain

def combine(earlier, later):
    return (earlier[0] * later[0], later[1] + later[0] * earlier[1])

def row_forward(x_row, seg_row, weights):
    w_gate, w_input, w_recur, w_inject, w_output, w_hidden, w_upward, w_down, gain_one, gain_two, conv_taps, conv_bias, recur_bias, inject_bias, decay_param = weights
    normed = low(rms_norm(x_row, gain_one))
    gate_act = jax.nn.gelu(low_back(matmul_high(normed, w_gate)))
    branch = low_back(matmul_high(normed, w_input))
    conv_out = conv_bias + conv_taps[0] * branch
    keep_one = None
    for offset in range(1, 4):
        shifted = jnp.pad(branch, ((offset, 0), (0, 0)))[:LEN]
        before = jnp.pad(seg_row, (offset, 0), constant_values=-1)[:LEN]
        same = (seg_row == before).astype(jnp.float32)[:, None]
        if offset == 1:
            keep_one = same
        conv_out = conv_out + conv_taps[offset] * shifted * same
    conv_low = low(conv_out)
    recur_gate = jax.nn.sigmoid(low_back(matmul_high(conv_low, w_recur)) + recur_bias)
    inject_gate = jax.nn.sigmoid(low_back(matmul_high(conv_low, w_inject)) + inject_bias)
    decays = jnp.exp(-DECAY_SCALE * recur_gate * jax.nn.softplus(decay_param))
    carry_mult = decays * keep_one
    normalizer = jnp.sqrt(1.0 - decays * decays + FLOOR_TERM)
    injected = normalizer * inject_gate * conv_out
    cumul, states = lax.associative_scan(combine, (carry_mult, injected), axis=0)
    mixed = low(states * gate_act)
    resid = x_row + low_back(matmul_high(mixed, w_output))
    normed_two = low(rms_norm(resid, gain_two))
    hidden_pre = low_back(matmul_high(normed_two, w_hidden))
    upward_pre = low_back(matmul_high(normed_two, w_upward))
    product = low(jax.nn.gelu(hidden_pre) * upward_pre)
    return resid + low_back(matmul_high(product, w_down))

def reference(inputs, segments, w_gate, w_input, w_recur, w_inject, w_output, w_hidden, w_upward, w_down, gain_one, gain_two, conv_taps, conv_bias, recur_bias, inject_bias, decay_param, cotangent):
    weights = (w_gate.astype(jnp.float32), w_input.astype(jnp.float32), w_recur.astype(jnp.float32), w_inject.astype(jnp.float32), w_output.astype(jnp.float32), w_hidden.astype(jnp.float32), w_upward.astype(jnp.float32), w_down.astype(jnp.float32), gain_one, gain_two, conv_taps, conv_bias, recur_bias, inject_bias, decay_param)

    def one_row(totals, item):
        x_row, seg_row, cot_row = item
        out_row, pull = jax.vjp(lambda xr, ws: row_forward(xr, seg_row, ws), x_row, weights)
        grad_x, grad_ws = pull(cot_row)
        totals = jax.tree.map(lambda acc, new: acc + new, totals, grad_ws)
        return (totals, (out_row, grad_x))
    zeros = jax.tree.map(jnp.zeros_like, weights)
    totals, (output, grad_inputs) = lax.scan(one_row, zeros, (inputs, segments, cotangent))
    return (output, grad_inputs, totals[0], totals[1], totals[2], totals[3], totals[4], totals[5], totals[6], totals[7], totals[8], totals[9], totals[10], totals[11], totals[12], totals[13], totals[14])
```

```python
import functools

import jax
import jax.numpy as jnp
from jax import lax
from jax.experimental import pallas as pl
from jax.experimental.pallas import tpu as pltpu
from jax.sharding import PartitionSpec as P

EPSILON = 1e-06
DECAY_SCALE = 8.0
FLOOR_TERM = 0.01
SLOTS = 240
VMEM_BYTES = 62 << 20


def shifted(array, axis, by):
    peers = lax.axis_size(axis)
    pairs = [(i, i + by) for i in range(peers) if 0 <= i + by < peers]
    return lax.ppermute(array, axis, pairs)


def prefix(value, axis, join, neutral, backward):
    count, mine = (lax.axis_size(axis), lax.axis_index(axis))
    pieces = jax.tree.map(lambda part: lax.all_gather(part, axis), value)
    if backward:
        pieces = jax.tree.map(lambda part: part[::-1], pieces)
        mine = count - 1 - mine
    so_far = jax.tree.map(
        lambda part, zero: jnp.full_like(part, 0) + jnp.asarray(zero, part.dtype), value, neutral
    )

    def turn(position, so_far):
        longer = join(so_far, jax.tree.map(lambda part: part[position], pieces))
        return jax.tree.map(lambda new, old: jnp.where(position < mine, new, old), longer, so_far)

    return lax.fori_loop(0, count - 1, turn, so_far)


def shortened(array):
    return jax.tree.map(lambda a: a.astype(jnp.bfloat16) if a.dtype == jnp.float32 else a, array)


def combine(earlier, later):
    return (earlier[0] * later[0], later[1] + later[0] * earlier[1])


def matmul_plain(left, right):
    return jnp.dot(left, right, preferred_element_type=jnp.float32)


def matmul_tleft(left, right):
    return jnp.einsum("ta,tb->ab", left, right, preferred_element_type=jnp.float32)


def matmul_tright(left, right):
    return jnp.einsum("ta,ba->tb", left, right, preferred_element_type=jnp.float32)


def norm_forward(values, gain):
    scaler = lax.rsqrt(jnp.mean(values * values, axis=-1, keepdims=True) + EPSILON)
    return (values * scaler * gain, scaler)


def norm_back(values, scaler, gain, incoming):
    scaled = incoming * gain
    grad_gain = jnp.sum(incoming * values * scaler, axis=0)
    inner = jnp.mean(scaled * values, axis=-1, keepdims=True)
    return (scaler * (scaled - values * scaler * scaler * inner), grad_gain)


def gathered_block(
    inputs,
    segments,
    w_gate,
    w_input,
    w_recur,
    w_inject,
    w_output,
    w_hidden,
    w_upward,
    w_down,
    gain_one,
    gain_two,
    conv_taps,
    conv_bias,
    recur_bias,
    inject_bias,
    decay_param,
    cotangent,
):
    row_count, positions, features = inputs.shape
    (
        gate_full,
        input_full,
        recur_full,
        inject_full,
        output_full,
        hidden_full,
        upward_full,
        down_full,
    ) = (
        lax.all_gather(w_gate, ("seq", "batch"), axis=0, tiled=True),
        lax.all_gather(w_input, ("seq", "batch"), axis=0, tiled=True),
        lax.all_gather(w_recur, ("seq", "batch"), axis=0, tiled=True),
        lax.all_gather(w_inject, ("seq", "batch"), axis=0, tiled=True),
        lax.all_gather(w_output, ("seq", "batch"), axis=0, tiled=True),
        lax.all_gather(w_hidden, ("seq", "batch"), axis=0, tiled=True),
        lax.all_gather(w_upward, ("seq", "batch"), axis=0, tiled=True),
        lax.all_gather(w_down, ("seq", "batch"), axis=0, tiled=True),
    )
    channels = gate_full.shape[1]
    tokens_here = row_count * positions
    flat_in = inputs.reshape(tokens_here, features)
    normed, scale_one = norm_forward(flat_in, gain_one)
    normed_low = normed.astype(jnp.bfloat16)
    gate_pre = matmul_plain(normed_low, gate_full)
    gate_act, gate_pull = jax.vjp(jax.nn.gelu, gate_pre)
    branch = matmul_plain(normed_low, input_full).reshape(row_count, positions, channels)
    seg_marks = segments.astype(jnp.float32) + 1.0
    prior_branch, prior_marks = shifted(
        (branch[:, positions - 3 :], seg_marks[:, positions - 3 :]), "seq", 1
    )
    ext_branch = jnp.concatenate([prior_branch, branch], axis=1)
    ext_marks = jnp.concatenate([prior_marks, seg_marks], axis=1)
    sames = []
    lagged = []
    for offset in range(4):
        sames.append(
            (ext_marks[:, 3 - offset : 3 - offset + positions] == seg_marks).astype(jnp.float32)[
                :, :, None
            ]
        )
        lagged.append(ext_branch[:, 3 - offset : 3 - offset + positions])
    conv_out = conv_bias + conv_taps[0] * branch
    for offset in range(1, 4):
        conv_out = conv_out + conv_taps[offset] * lagged[offset] * sames[offset]
    conv_low = conv_out.reshape(tokens_here, channels).astype(jnp.bfloat16)
    recur_gate = jax.nn.sigmoid(matmul_plain(conv_low, recur_full) + recur_bias).reshape(
        row_count, positions, channels
    )
    inject_gate = jax.nn.sigmoid(matmul_plain(conv_low, inject_full) + inject_bias).reshape(
        row_count, positions, channels
    )
    base_rate = jax.nn.softplus(decay_param)
    decays = jnp.exp(-DECAY_SCALE * recur_gate * base_rate)
    carry_mult = decays * sames[1]
    normalizer = jnp.sqrt(1.0 - decays * decays + FLOOR_TERM)
    injected = normalizer * inject_gate * conv_out
    cumul, local_state = lax.associative_scan(combine, (carry_mult, injected), axis=1)
    ones_rows = jnp.ones((row_count, channels), jnp.float32)
    zeros_rows = jnp.zeros((row_count, channels), jnp.float32)
    entry = prefix(
        (cumul[:, -1], local_state[:, -1]), "seq", combine, (ones_rows, zeros_rows), False
    )[1]
    states = local_state + cumul * entry[:, None]
    states_before = jnp.concatenate([entry[:, None], states[:, :-1]], axis=1)
    states_flat = states.reshape(tokens_here, channels)
    mixed = (states_flat * gate_act).astype(jnp.bfloat16)
    resid = flat_in + matmul_plain(mixed, output_full)
    normed_two, scale_two = norm_forward(resid, gain_two)
    normed_two_low = normed_two.astype(jnp.bfloat16)
    hidden_pre = matmul_plain(normed_two_low, hidden_full)
    upward_pre = matmul_plain(normed_two_low, upward_full)
    hidden_act, hidden_pull = jax.vjp(jax.nn.gelu, hidden_pre)
    product = (hidden_act * upward_pre).astype(jnp.bfloat16)
    output = resid + matmul_plain(product, down_full)
    grad_out = cotangent.reshape(tokens_here, features)
    grad_out_low = grad_out.astype(jnp.bfloat16)
    grad_down = matmul_tleft(product, grad_out_low)
    grad_product = matmul_tright(grad_out_low, down_full)
    grad_hidden_pre = hidden_pull(grad_product * upward_pre)[0].astype(jnp.bfloat16)
    grad_upward_pre = (grad_product * hidden_act).astype(jnp.bfloat16)
    grad_hidden = matmul_tleft(normed_two_low, grad_hidden_pre)
    grad_upward = matmul_tleft(normed_two_low, grad_upward_pre)
    grad_normed_two = matmul_tright(grad_hidden_pre, hidden_full) + matmul_tright(
        grad_upward_pre, upward_full
    )
    grad_resid_norm, grad_gain_two = norm_back(resid, scale_two, gain_two, grad_normed_two)
    grad_resid = grad_out + grad_resid_norm
    grad_resid_low = grad_resid.astype(jnp.bfloat16)
    grad_output = matmul_tleft(mixed, grad_resid_low)
    grad_mixed = matmul_tright(grad_resid_low, output_full)
    grad_gate_pre = gate_pull(grad_mixed * states_flat)[0].astype(jnp.bfloat16)
    grad_states = (grad_mixed * gate_act).reshape(row_count, positions, channels)
    next_mult = jnp.concatenate([carry_mult[:, 1:], jnp.ones_like(carry_mult[:, :1])], axis=1)
    tail_prod, local_grad = lax.associative_scan(
        combine, (next_mult, grad_states), axis=1, reverse=True
    )
    incoming = prefix(
        (cumul[:, -1], carry_mult[:, 0] * local_grad[:, 0]),
        "seq",
        combine,
        (ones_rows, zeros_rows),
        True,
    )[1]
    total_grad = local_grad + tail_prod * incoming[:, None]
    grad_decays = (
        total_grad * states_before * sames[1]
        - total_grad * inject_gate * conv_out * decays / normalizer
    )
    grad_log = grad_decays * decays
    grad_recur_pre = grad_log * (-DECAY_SCALE * base_rate) * recur_gate * (1.0 - recur_gate)
    grad_decay_param = jnp.sum(
        grad_log * (-DECAY_SCALE * recur_gate), axis=(0, 1)
    ) * jax.nn.sigmoid(decay_param)
    grad_inject_pre = total_grad * normalizer * conv_out * inject_gate * (1.0 - inject_gate)
    grad_recur_bias = jnp.sum(grad_recur_pre, axis=(0, 1))
    grad_inject_bias = jnp.sum(grad_inject_pre, axis=(0, 1))
    grad_recur_low = grad_recur_pre.reshape(tokens_here, channels).astype(jnp.bfloat16)
    grad_inject_low = grad_inject_pre.reshape(tokens_here, channels).astype(jnp.bfloat16)
    grad_recur = matmul_tleft(conv_low, grad_recur_low)
    grad_inject = matmul_tleft(conv_low, grad_inject_low)
    through_gates = matmul_tright(grad_recur_low, recur_full) + matmul_tright(
        grad_inject_low, inject_full
    )
    grad_conv = total_grad * normalizer * inject_gate + through_gates.reshape(
        row_count, positions, channels
    )
    grad_conv_bias = jnp.sum(grad_conv, axis=(0, 1))
    taps_by_channel = jnp.stack(
        [jnp.sum(grad_conv * lagged[offset] * sames[offset], axis=(0, 1)) for offset in range(4)],
        axis=1,
    )
    later_grad, later_marks = (
        shifted(shortened(grad_conv[:, :3]), "seq", -1),
        shifted(seg_marks[:, :3].astype(jnp.bfloat16), "seq", -1).astype(jnp.float32),
    )
    ext_grad = jnp.concatenate([grad_conv, later_grad], axis=1)
    ext_after = jnp.concatenate([seg_marks, later_marks], axis=1)
    grad_branch = conv_taps[0] * grad_conv
    for offset in range(1, 4):
        match = (ext_after[:, offset : offset + positions] == seg_marks).astype(jnp.float32)[
            :, :, None
        ]
        grad_branch = (
            grad_branch + conv_taps[offset] * ext_grad[:, offset : offset + positions] * match
        )
    grad_branch_low = grad_branch.reshape(tokens_here, channels).astype(jnp.bfloat16)
    grad_input = matmul_tleft(normed_low, grad_branch_low)
    grad_gate = matmul_tleft(normed_low, grad_gate_pre)
    grad_normed = matmul_tright(grad_gate_pre, gate_full) + matmul_tright(
        grad_branch_low, input_full
    )
    grad_first_norm, grad_gain_one = norm_back(flat_in, scale_one, gain_one, grad_normed)
    grad_inputs = (grad_resid + grad_first_norm).reshape(row_count, positions, features)
    every = (
        lax.psum_scatter(grad_gate, ("seq", "batch"), scatter_dimension=0, tiled=True),
        lax.psum_scatter(grad_input, ("seq", "batch"), scatter_dimension=0, tiled=True),
        lax.psum_scatter(grad_recur, ("seq", "batch"), scatter_dimension=0, tiled=True),
        lax.psum_scatter(grad_inject, ("seq", "batch"), scatter_dimension=0, tiled=True),
        lax.psum_scatter(grad_output, ("seq", "batch"), scatter_dimension=0, tiled=True),
        lax.psum_scatter(grad_hidden, ("seq", "batch"), scatter_dimension=0, tiled=True),
        lax.psum_scatter(grad_upward, ("seq", "batch"), scatter_dimension=0, tiled=True),
        lax.psum_scatter(grad_down, ("seq", "batch"), scatter_dimension=0, tiled=True),
        lax.psum_scatter(grad_gain_one, ("seq", "batch"), scatter_dimension=0, tiled=True),
        lax.psum_scatter(grad_gain_two, ("seq", "batch"), scatter_dimension=0, tiled=True),
        lax.psum_scatter(taps_by_channel, ("seq", "batch"), scatter_dimension=0, tiled=True),
        lax.psum_scatter(grad_conv_bias, ("seq", "batch"), scatter_dimension=0, tiled=True),
        lax.psum_scatter(grad_recur_bias, ("seq", "batch"), scatter_dimension=0, tiled=True),
        lax.psum_scatter(grad_inject_bias, ("seq", "batch"), scatter_dimension=0, tiled=True),
        lax.psum_scatter(grad_decay_param, ("seq", "batch"), scatter_dimension=0, tiled=True),
    )
    summed = (
        every[0],
        every[1],
        every[2],
        every[3],
        every[4],
        every[5],
        every[6],
        every[7],
        every[8],
        every[9],
        every[10].T,
        every[11],
        every[12],
        every[13],
        every[14],
    )
    return (
        output.reshape(row_count, positions, features),
        grad_inputs,
        summed[0],
        summed[1],
        summed[2],
        summed[3],
        summed[4],
        summed[5],
        summed[6],
        summed[7],
        summed[8],
        summed[9],
        summed[10],
        summed[11],
        summed[12],
        summed[13],
        summed[14],
    )


MESH = pl.DeviceIdType.MESH
F32, BF16 = (jnp.float32, jnp.bfloat16)
LANES = 128
EDGE = 8
STEP = 32
DEPTH, PAIR, GROUP = (4, 2, 4)
RING = DEPTH * PAIR


def dot_nn(left, right):
    return lax.dot_general(left, right, (((1,), (0,)), ((), ())), preferred_element_type=F32)


def dot_nt(left, right):
    return lax.dot_general(left, right, (((1,), (1,)), ((), ())), preferred_element_type=F32)


def dot_tn(left, right):
    return lax.dot_general(left, right, (((0,), (0,)), ((), ())), preferred_element_type=F32)


def gelu_parts(value):
    rate = 0.7978845608028654
    square = value * value
    bent = jnp.tanh(rate * (value + 0.044715 * square * value))
    act = 0.5 * value * (1.0 + bent)
    slope = 0.5 * (1.0 + bent) + 0.5 * rate * value * (1.0 - bent * bent) * (1.0 + 0.134145 * square)
    return (act, slope)


def at(start, size, of):
    return pl.ds(pl.multiple_of(start, of), size)


def loop(count, body):
    def turn(i, nothing):
        body(i)
        return nothing

    lax.fori_loop(0, count, turn, 0)


class Net:
    def __init__(self, send, recv):
        self.send, self.recv, self.used, self.open = (send, recv, 0, {})

    def slots(self, count):
        first = self.used
        self.used += count
        return list(range(first, first + count))

    def put(self, src, dst, to, slot, tag=""):
        copy = pltpu.make_async_remote_copy(
            src_ref=src,
            dst_ref=dst,
            send_sem=self.send.at[slot],
            recv_sem=self.recv.at[slot],
            device_id=to,
            device_id_type=MESH,
        )
        copy.start()
        self.open.setdefault(tag, []).append(copy)

    def got(self, dst, to, slot):
        pltpu.make_async_remote_copy(
            src_ref=dst,
            dst_ref=dst,
            send_sem=self.send.at[slot],
            recv_sem=self.recv.at[slot],
            device_id=to,
            device_id_type=MESH,
        ).wait_recv()

    def flush(self, *tags):
        for tag in tags or list(self.open):
            for copy in self.open.pop(tag, []):
                copy.wait_send()


def fused(names, *refs):
    r = dict(zip(names, refs))
    x, cot, seg, xw, xhu, own_o, own_d, gains, vec = (
        r[k] for k in ("x", "cot", "seg", "xw", "xhu", "own_o", "own_d", "gains", "vec")
    )
    out, gin, fin, fin_hu, g_o, g_d, g_vec = (
        r[k] for k in ("out", "gin", "fin", "fin_hu", "g_o", "g_d", "g_vec")
    )
    w_one, w_ri, w_o, w_hu, w_d = (r[k] for k in ("w_one", "w_ri", "w_o", "w_hu", "w_d"))
    norm, gout, norm_two, gres, conv, mix = (
        r[k] for k in ("norm", "gout", "norm_two", "gres", "conv", "mix")
    )
    prod, ghu, ggb, gri, part = (r[k] for k in ("prod", "ghu", "ggb", "gri", "part"))
    brx, tgx, stx, gate_pre, conv_out = (r[k] for k in ("brx", "tgx", "stx", "gate_pre", "conv_out"))
    rgate, igate, carry, pre = (r[k] for k in ("rgate", "igate", "carry", "pre"))
    core_in, x_in, pre_f, pre_b = (r[k] for k in ("core_in", "x_in", "pre_f", "pre_b"))
    acc, gain_acc, vs, vb = (r[k] for k in ("acc", "gain_acc", "vs", "vb"))
    net = Net(r["send"], r["recv"])

    width = x.shape[1]
    here = carry.shape[1]
    chans = carry.shape[2]
    hid = prod.shape[1]
    rows = 2 * GROUP
    half = GROUP * here
    blk, cblk, fblk = (width // (RING * GROUP), chans // RING, hid // RING)
    groups = [slice(g * LANES, (g + 1) * LANES) for g in range(chans // LANES)]
    marks = slice(chans, chans + LANES)

    s = lax.axis_index("seq")
    b = lax.axis_index("batch")
    z, y = (s // PAIR, s % PAIR)
    mate, across, corner = (
        (b // 2) * 2 + (1 - b % 2),
        (1 - b // 2) * 2 + b % 2,
        (1 - b // 2) * 2 + (1 - b % 2),
    )
    to_mate, to_across, to_corner = ((s, mate), (s, across), (s, corner))
    group_peers = [(mate, to_mate), (across, to_across), (corner, to_corner)]
    to_pair = (z * PAIR + 1 - y, b)
    far = [lax.rem(z + k, DEPTH) for k in range(DEPTH)]
    near = [lax.rem(z + DEPTH - k, DEPTH) for k in range(DEPTH)]
    ring_to = [lax.rem(s + k, RING) for k in range(RING)]
    ring_from = [lax.rem(s + RING - k, RING) for k in range(RING)]

    barrier = pltpu.get_barrier_semaphore()
    for _, to in group_peers:
        pl.semaphore_signal(barrier, inc=1, device_id=to, device_id_type=MESH)
    for k in range(1, RING):
        pl.semaphore_signal(barrier, inc=1, device_id=(ring_to[k], b), device_id_type=MESH)
    pl.semaphore_wait(barrier, 3 + RING - 1)

    class Chunk:
        pass

    def chunk(block, piece, pieces, y_block, y_piece, z_block, z_piece):
        c = Chunk()
        c.block, c.piece, c.pieces = (block, piece, pieces)
        c.y_block, c.y_piece, c.z_block, c.z_piece = (y_block, y_piece, z_block, z_piece)
        c.gather_z = net.slots(DEPTH)
        c.gather_y = net.slots(DEPTH)
        c.sum_y = net.slots(DEPTH)
        c.sum_z = net.slots(DEPTH)
        c.spread = net.slots(3)
        c.home = net.slots(3)
        return c

    def flat_chunk(ref, size, step, cols, y_ref, z_ref):
        def row(base, i):
            return (at(base * size + i * step, step, 16), cols)

        return chunk(
            lambda q: ref.at[at(q * size, size, 16), cols],
            lambda q, i: ref.at[row(q, i)],
            size // step,
            lambda q: y_ref.at[at(q * size, size, 16), slice(0, cols.stop - cols.start)],
            lambda q, i: y_ref.at[at(q * size + i * step, step, 16), slice(0, cols.stop - cols.start)],
            lambda q: z_ref.at[pl.ds(q * size, size), slice(0, cols.stop - cols.start)],
            lambda q, i: z_ref.at[at(q * size + i * step, step, 16), slice(0, cols.stop - cols.start)],
        )

    two = 2 * chans
    size_one = GROUP * blk
    one = flat_chunk(
        w_one, size_one, blk, slice(0, two), norm_two, norm_two.at[pl.ds(DEPTH * size_one, (DEPTH - 1) * size_one)]
    )
    ri = chunk(
        lambda q: w_ri.at[:, q],
        lambda q, i: w_ri.at[i, q],
        GROUP,
        lambda q: r["y_ri"].at[q],
        lambda q, i: r["y_ri"].at[q, i],
        lambda q: r["z_ri"].at[q],
        lambda q, i: r["z_ri"].at[q, i],
    )
    wo = flat_chunk(w_o, cblk, 16, slice(0, width), r["y_o"], r["z_o"])
    hi = flat_chunk(w_hu, size_one, blk, slice(0, hid), r["y_h"], r["z_h"])
    up = flat_chunk(w_hu, size_one, blk, slice(hid, 2 * hid), r["y_u"], r["z_u"])
    dn = flat_chunk(w_d, fblk, 16, slice(0, width), r["y_d"], r["z_d"])

    rec = blk + cblk
    one.source = lambda q: xw.at[at(q * rec, blk, 16)]
    one.place = lambda q: w_one.at[at(s * size_one + q * blk, blk, 16)]
    one.result = lambda q: fin.at[at(q * rec, blk, 16)]
    ri.source = lambda q: xw.at[at(q * rec + blk, cblk, 16)]
    ri.place = lambda q: w_ri.at[q, s]
    ri.result = lambda q: fin.at[at(q * rec + blk, cblk, 16)]
    hi.source = lambda q: xhu.at[at(q * blk, blk, 16), slice(0, hid)]
    hi.place = lambda q: w_hu.at[at(s * size_one + q * blk, blk, 16), slice(0, hid)]
    hi.result = lambda q: fin_hu.at[at(q * blk, blk, 16), slice(0, hid)]
    up.source = lambda q: xhu.at[at(q * blk, blk, 16), slice(hid, 2 * hid)]
    up.place = lambda q: w_hu.at[at(s * size_one + q * blk, blk, 16), slice(hid, 2 * hid)]
    up.result = lambda q: fin_hu.at[at(q * blk, blk, 16), slice(hid, 2 * hid)]

    def spread(c):
        for (peer, to), slot in zip(group_peers, c.spread):
            net.put(c.source(peer), c.place(b), to, slot)
        c.place(b)[...] = c.source(b)[...]

    def spread_wait(c):
        for (peer, to), slot in zip(group_peers, c.spread):
            net.got(c.place(peer), to, slot)

    def gather(c):
        for k in (1, 3, 2):
            net.put(c.block(s), c.block(s), (far[k] * PAIR + y, b), c.gather_z[k])
        net.put(c.block(s), c.block(s), to_pair, c.gather_y[0])

    def gather_relay(c, k):
        from_z = near[k] * PAIR + y
        net.got(c.block(from_z), (from_z, b), c.gather_z[k])
        net.put(c.block(from_z), c.block(from_z), to_pair, c.gather_y[k])

    def gather_wait(c):
        for k in range(DEPTH):
            net.got(c.block(near[k] * PAIR + 1 - y), to_pair, c.gather_y[k])

    def sum_pair(c):
        for k in (1, 3, 2, 0):
            net.put(c.block(far[k] * PAIR + 1 - y), c.y_block(far[k]), to_pair, c.sum_y[k])

    def sum_pair_end(c, k):
        net.got(c.y_block(far[k]), to_pair, c.sum_y[k])
        mine = far[k] * PAIR + y

        def add(i):
            total = c.piece(mine, i)[...].astype(F32) + c.y_piece(far[k], i)[...].astype(F32)
            c.piece(mine, i)[...] = total.astype(BF16)

        loop(c.pieces, add)
        if k:
            net.put(c.block(mine), c.z_block(k - 1), (mine, b), c.sum_z[k])

    def sum_end(c, keep):
        for k in range(1, DEPTH):
            net.got(c.z_block(k - 1), (near[k] * PAIR + y, b), c.sum_z[k])

        def add(i):
            total = c.piece(s, i)[...].astype(F32)
            for k in range(DEPTH - 1):
                total = total + c.z_piece(k, i)[...].astype(F32)
            keep(i, total)

        loop(c.pieces, add)

    def sum_end_spread(c):
        def keep(i, total):
            c.piece(s, i)[...] = total.astype(BF16)

        sum_end(c, keep)
        for (peer, to), slot in zip(group_peers, c.home):
            net.put(c.place(peer), c.result(b), to, slot)
        c.result(b)[...] = c.place(b)[...]

    def home_wait(c):
        for (peer, to), slot in zip(group_peers, c.home):
            net.got(c.result(peer), to, slot)

    def share(view, slots, h):
        net.put(view(b, h), view(b, h), to_across, slots[3 * h])
        net.put(view(b, h), view(b, h), to_mate, slots[3 * h + 1])

    def share_relay(view, slots, h):
        net.got(view(across, h), to_across, slots[3 * h])
        net.put(view(across, h), view(across, h), to_mate, slots[3 * h + 2])

    def share_end(view, slots, h):
        net.got(view(mate, h), to_mate, slots[3 * h + 1])
        net.got(view(corner, h), to_mate, slots[3 * h + 2])

    def token_rows(ref):
        return lambda q, h: ref.at[at((h * GROUP + q) * here, here, 16)]

    def merge(view, first, slots, h):
        net.put(view(corner, h), first(h, 1), to_mate, slots[3 * h], "part")
        net.put(view(mate, h), first(h, 0), to_mate, slots[3 * h + 1], "part")

    def merge_relay(view, first, second, slots, h, parts, tile):
        net.got(first(h, 1), to_mate, slots[3 * h])

        def add(i):
            v = tile(view(across, h), i)
            v[...] = (v[...].astype(F32) + tile(first(h, 1), i)[...].astype(F32)).astype(BF16)

        loop(parts, add)
        net.put(view(across, h), second(h), to_across, slots[3 * h + 2], "part")

    def merge_end(first, second, slots, h):
        net.got(first(h, 0), to_mate, slots[3 * h + 1])
        net.got(second(h), to_across, slots[3 * h + 2])

    def sixteen(ref, i):
        return ref.at[at(i * 16, 16, 16)]

    first_in = lambda h, slot: core_in.at[h, slot]
    second_in = lambda h: x_in.at[h]
    part_rows = token_rows(part)

    def merged(h, i):
        total = sixteen(part_rows(b, h), i)[...].astype(F32)
        return total + core_in[h, 0, at(i * 16, 16, 16)].astype(F32) + x_in[h, at(i * 16, 16, 16)].astype(F32)

    def own(ref, h, i):
        return ref.at[at(h * here + i * 16, 16, 16)]

    tiles16 = here // 16
    gain_one, gain_two = (gains[0:1], gains[1:2])

    def rms(values):
        return lax.rsqrt(jnp.mean(values * values, axis=-1, keepdims=True) + EPSILON)

    def norm_grad(index, values, incoming, gain):
        scaler = rms(values)
        scaled = incoming * gain
        inner = jnp.mean(scaled * values, axis=-1, keepdims=True)
        term = incoming * values * scaler
        gain_acc[index] += term[0:8] + term[8:16]
        return scaler * (scaled - values * (scaler * scaler * inner))

    def over(h, body):
        def row(i):
            q = h * GROUP + i
            for start in range(0, here, STEP):
                for g, lanes in enumerate(groups):
                    body(q, start, lanes, g)

        loop(GROUP, row)

    def flat(q, start):
        return at(q * here + start, STEP, STEP)

    def add_to(index, lanes, values):
        total = values[0:8]
        for k in range(8, STEP, 8):
            total = total + values[k : k + 8]
        acc[index, :, lanes] += total

    def same(q, start, k):
        now = brx[q, pl.ds(EDGE + start, STEP), marks]
        return (now == brx[q, pl.ds(EDGE + start - k, STEP), marks]).astype(F32)

    spread(one)
    acc[...] = jnp.zeros_like(acc)
    gain_acc[...] = jnp.zeros_like(gain_acc)
    norm_slots, gout_slots, conv_slots = (net.slots(6), net.slots(6), net.slots(6))
    two_slots, gres_slots = (net.slots(6), net.slots(6))
    out_slots, gnt_slots, down_slots, thru_slots, gn_slots = (net.slots(6) for _ in range(5))
    halo_slot, halo_back = net.slots(2)
    pre_slots, back_slots, vec_slots, last_slots = (
        net.slots(RING),
        net.slots(RING),
        net.slots(RING),
        net.slots(3),
    )
    norm_rows, gout_rows, two_rows, gres_rows = (token_rows(ref) for ref in (norm, gout, norm_two, gres))

    for h in range(2):
        def norm_tile(i, h=h):
            v = own(x, h, i)[...]
            sixteen(norm_rows(b, h), i)[:, 0:width] = (v * rms(v) * gain_one).astype(BF16)
            sixteen(norm_rows(b, h), i)[:, width : width + LANES] = own(seg, h, i)[...]

        loop(tiles16, norm_tile)
        share(norm_rows, norm_slots, h)
    spread(ri)
    spread(hi)
    spread(up)
    w_o[at(s * cblk, cblk, 16), :] = own_o[...]
    w_d[at(s * fblk, fblk, 16), :] = own_d[...]
    spread_wait(one)
    gather(one)
    gather(wo)
    for h in range(2):
        share_relay(norm_rows, norm_slots, h)

    for h in range(2):
        def low_tile(i, h=h):
            sixteen(gout_rows(b, h), i)[...] = own(cot, h, i)[...].astype(BF16)

        loop(tiles16, low_tile)

    @pl.when(s == 0)
    def _():
        brx[:, 0:EDGE, :] = jnp.full((rows, EDGE, chans + LANES), -1.0, F32)

    @pl.when(s == RING - 1)
    def _():
        tgx[:, here : here + EDGE, :] = jnp.full((rows, EDGE, chans + LANES), -1.0, F32)

    for k in (1, 3, 2):
        gather_relay(one, k)
    gather_wait(one)

    for h in range(2):
        share_end(norm_rows, norm_slots, h)

        def first_mm(i, h=h):
            q = h * GROUP + i
            span = at(q * here, here, 16)
            got = dot_nn(norm[span, 0:width], w_one[...])
            gate_pre[q] = got[:, 0:chans]
            brx[q, EDGE : EDGE + here, 0:chans] = got[:, chans:two]
            ids = norm[span, width : width + LANES].astype(F32)
            brx[q, EDGE : EDGE + here, marks] = ids
            tgx[q, 0:here, marks] = ids

        loop(GROUP, first_mm)

    def halo_out():
        return pltpu.make_async_remote_copy(
            src_ref=brx.at[:, pl.ds(here, EDGE)],
            dst_ref=brx.at[:, pl.ds(0, EDGE)],
            send_sem=net.send.at[halo_slot],
            recv_sem=net.recv.at[halo_slot],
            device_id=(ring_to[1], b),
            device_id_type=MESH,
        )

    @pl.when(s < RING - 1)
    def _():
        halo_out().start()

    spread_wait(ri)
    gather(ri)
    for k in (1, 3, 2):
        gather_relay(wo, k)

    @pl.when(s > 0)
    def _():
        net.got(brx.at[:, pl.ds(0, EDGE)], (ring_from[1], b), halo_slot)

    conv_cols = lambda q, h: conv.at[pl.ds(h * half, half), at(q * chans, chans, LANES)]
    for h in range(2):
        def conv_tile(q, start, lanes, g):
            total = vec[4:5, lanes] + vec[0:1, lanes] * brx[q, pl.ds(EDGE + start, STEP), lanes]
            for k in range(1, 4):
                lag = brx[q, pl.ds(EDGE + start - k, STEP), lanes]
                total = total + vec[k : k + 1, lanes] * lag * same(q, start, k)
            conv_out[q, pl.ds(start, STEP), lanes] = total
            conv[flat(q, start), at(b * chans + g * LANES, LANES, LANES)] = total.astype(BF16)

        over(h, conv_tile)
        share(conv_cols, conv_slots, h)
    for h in range(2):
        share(gout_rows, gout_slots, h)
    for h in range(2):
        share_relay(conv_cols, conv_slots, h)
    for k in (1, 3, 2):
        gather_relay(ri, k)
    spread_wait(hi)
    gather(hi)
    gather_wait(ri)

    for h in range(2):
        share_end(conv_cols, conv_slots, h)

        def gate_mm(i, h=h):
            q = h * GROUP + i
            got = dot_nn(conv[at(q * here, here, 16), :], w_ri[...].reshape(GROUP * chans, two))
            rgate[q] = got[:, 0:chans]
            igate[q] = got[:, chans:two]

        loop(GROUP, gate_mm)

        def gate_tile(q, start, lanes, g):
            span = pl.ds(start, STEP)
            rg = jax.nn.sigmoid(rgate[q, span, lanes] + vec[5:6, lanes])
            ig = jax.nn.sigmoid(igate[q, span, lanes] + vec[6:7, lanes])
            rgate[q, span, lanes] = rg
            igate[q, span, lanes] = ig
            decay = jnp.exp(rg * vec[7:8, lanes])
            carry[q, span, lanes] = decay * same(q, start, 1)
            scale = jnp.sqrt(1.0 - decay * decay + FLOOR_TERM)
            stx[q, pl.ds(EDGE + start, STEP), lanes] = scale * ig * conv_out[q, span, lanes]

        over(h, gate_tile)

    def ends(p, state):
        mult = carry[:, p, :]
        return (state[0] * mult, mult * state[1] + stx[:, EDGE + p, :])

    begin = (jnp.ones((rows, chans), F32), jnp.zeros((rows, chans), F32))
    product, tail = lax.fori_loop(0, here, ends, begin, unroll=8)
    pre_f[s, 0:rows] = product
    pre_f[s, rows : 2 * rows] = tail
    for k in range(1, RING):
        net.put(pre_f.at[s], pre_f.at[s], (ring_to[k], b), pre_slots[k])
    for k in (1, 3, 2):
        gather_relay(hi, k)
    spread_wait(up)
    gather(up)
    for h in range(2):
        share_relay(gout_rows, gout_slots, h)
    for k in range(1, RING):
        net.got(pre_f.at[ring_from[k]], (ring_from[k], b), pre_slots[k])
    state = jnp.zeros((rows, chans), F32)
    for q in range(RING - 1):
        state = jnp.where(q < s, pre_f[q, rows : 2 * rows] + pre_f[q, 0:rows] * state, state)
    stx[:, EDGE - 1, :] = state

    def scan(p, state):
        state = carry[:, p, :] * state + stx[:, EDGE + p, :]
        stx[:, EDGE + p, :] = state
        return state

    lax.fori_loop(0, here, scan, state, unroll=8)
    gather_wait(wo)

    for h in range(2):
        def mix_tile(q, start, lanes, g):
            act, _ = gelu_parts(gate_pre[q, pl.ds(start, STEP), lanes])
            mix[flat(q, start), lanes] = (stx[q, pl.ds(EDGE + start, STEP), lanes] * act).astype(BF16)

        over(h, mix_tile)

        def out_mm(i, h=h):
            span = at((h * GROUP + i) * here, here, 16)
            part[span, :] = dot_nn(mix[span, :], w_o[...]).astype(BF16)

        loop(GROUP, out_mm)
        merge(part_rows, first_in, out_slots, h)
    for h in range(2):
        merge_relay(part_rows, first_in, second_in, out_slots, h, tiles16, sixteen)
    for k in (1, 3, 2):
        gather_relay(up, k)
    gather(dn)
    for h in range(2):
        merge_end(first_in, second_in, out_slots, h)

        def resid_tile(i, h=h):
            v = own(x, h, i)[...] + merged(h, i)
            own(out, h, i)[...] = v
            sixteen(two_rows(b, h), i)[...] = (v * rms(v) * gain_two).astype(BF16)

        loop(tiles16, resid_tile)
        share(two_rows, two_slots, h)
    for h in range(2):
        share_relay(two_rows, two_slots, h)
    gather_wait(hi)
    gather_wait(up)

    for h in range(2):
        share_end(two_rows, two_slots, h)

        def hidden_mm(i, h=h):
            span = at((h * GROUP + i) * here, here, 16)
            pre[...] = dot_nn(norm_two[span, :], w_hu[...])

            def tile(t):
                rows_t = at(t * 16, 16, 16)
                flat_t = at((h * GROUP + i) * here + t * 16, 16, 16)
                for g in range(hid // LANES):
                    lanes = slice(g * LANES, (g + 1) * LANES)
                    right = slice(hid + g * LANES, hid + (g + 1) * LANES)
                    act, slope = gelu_parts(pre[rows_t, lanes])
                    upward = pre[rows_t, right]
                    prod[flat_t, lanes] = (act * upward).astype(BF16)
                    ghu[flat_t, lanes] = (upward * slope).astype(BF16)
                    ghu[flat_t, right] = act.astype(BF16)

            loop(tiles16, tile)

        loop(GROUP, hidden_mm)
    for k in (1, 3, 2):
        gather_relay(dn, k)
    gather_wait(dn)

    net.flush()
    for h in range(2):
        share_end(gout_rows, gout_slots, h)

        def down_back(i, h=h):
            span = at((h * GROUP + i) * here, here, 16)
            back = dot_nt(gout[span, :], w_d[...])
            ghu[span, 0:hid] = (back * ghu[span, 0:hid].astype(F32)).astype(BF16)
            ghu[span, hid : 2 * hid] = (back * ghu[span, hid : 2 * hid].astype(F32)).astype(BF16)
            part[span, :] = dot_nt(ghu[span, :], w_hu[...]).astype(BF16)

        loop(GROUP, down_back)
        merge(part_rows, first_in, gnt_slots, h)
    for h in range(2):
        merge_relay(part_rows, first_in, second_in, gnt_slots, h, tiles16, sixteen)

    def grad_hu(i):
        cols = at(i * 256, 256, LANES)
        w_hu[at(i * 256, 256, 16), :] = dot_tn(norm_two[:, cols], ghu[...]).astype(BF16)

    loop(width // 256, grad_hu)
    sum_pair(hi)
    for h in range(2):
        merge_end(first_in, second_in, gnt_slots, h)

        def second_norm(i, h=h):
            back = norm_grad(1, own(out, h, i)[...], merged(h, i), gain_two)
            own(gin, h, i)[...] = own(cot, h, i)[...] + back

        loop(tiles16, second_norm)

    for h in range(2):
        def low_resid(i, h=h):
            sixteen(gres_rows(b, h), i)[...] = own(gin, h, i)[...].astype(BF16)

        loop(tiles16, low_resid)
        share(gres_rows, gres_slots, h)
    net.flush("part")

    def down_mm(i):
        span = at(i * here, here, 16)
        part[span, :] = dot_nn(prod[span, :], w_d[...]).astype(BF16)

    loop(rows, down_mm)
    for h in range(2):
        share_relay(gres_rows, gres_slots, h)

    def grad_down(i):
        cols = at(i * 256, 256, LANES)
        w_d[at(i * 256, 256, 16), :] = dot_tn(prod[:, cols], gout[...]).astype(BF16)

    loop(hid // 256, grad_down)
    sum_pair(dn)

    for h in range(2):
        share_end(gres_rows, gres_slots, h)

        def out_back(i, h=h):
            q = h * GROUP + i
            tgx[q, 0:here, 0:chans] = dot_nt(gres[at(q * here, here, 16), :], w_o[...])

        loop(GROUP, out_back)

        def mix_back(q, start, lanes, g):
            span = pl.ds(start, STEP)
            act, slope = gelu_parts(gate_pre[q, span, lanes])
            back = tgx[q, span, lanes]
            states = stx[q, pl.ds(EDGE + start, STEP), lanes]
            ggb[flat(q, start), lanes] = (back * states * slope).astype(BF16)
            tgx[q, span, lanes] = back * act

        over(h, mix_back)

    def ends_back(i, state):
        p = here - 1 - i
        mult = carry[:, p, :]
        return (state[0] * mult, mult * (tgx[:, p, 0:chans] + state[1]))

    product, tail = lax.fori_loop(0, here, ends_back, begin, unroll=8)
    pre_b[s, 0:rows] = product
    pre_b[s, rows : 2 * rows] = tail
    for k in range(1, RING):
        net.put(pre_b.at[s], pre_b.at[s], (ring_to[k], b), back_slots[k])

    for h in range(2):
        merge(part_rows, first_in, down_slots, h)

    w_o[...] = dot_tn(mix[...], gres[...]).astype(BF16)
    for h in range(2):
        merge_relay(part_rows, first_in, second_in, down_slots, h, tiles16, sixteen)

    for k in range(1, RING):
        net.got(pre_b.at[ring_from[k]], (ring_from[k], b), back_slots[k])
    state = jnp.zeros((rows, chans), F32)
    for q in range(RING - 1, 0, -1):
        state = jnp.where(q > s, pre_b[q, rows : 2 * rows] + pre_b[q, 0:rows] * state, state)

    def scan_back(i, state):
        p = here - 1 - i
        total = tgx[:, p, 0:chans] + state
        tgx[:, p, 0:chans] = total
        return carry[:, p, :] * total

    lax.fori_loop(0, here, scan_back, state, unroll=8)

    for h in range(2):
        merge_end(first_in, second_in, down_slots, h)

        def out_tile(i, h=h):
            own(out, h, i)[...] = own(out, h, i)[...] + merged(h, i)

        loop(tiles16, out_tile)

    thru_cols = lambda q, h: ghu.at[pl.ds(h * half, half), at(q * chans, chans, LANES)]
    thru_first = lambda h, slot: prod.at[pl.ds(h * half, half), pl.ds(slot * chans, chans)]
    thru_second = lambda h: gout.at[pl.ds(h * half, half), pl.ds(0, chans)]
    for h in range(2):
        def gates_back(q, start, lanes, g):
            span = pl.ds(start, STEP)
            total = tgx[q, span, lanes]
            rg, ig, co = (rgate[q, span, lanes], igate[q, span, lanes], conv_out[q, span, lanes])
            before = stx[q, pl.ds(EDGE + start - 1, STEP), lanes]
            rate = vec[7:8, lanes]
            decay = jnp.exp(rg * rate)
            scale = jnp.sqrt(1.0 - decay * decay + FLOOR_TERM)
            grad_decay = total * before * same(q, start, 1) - total * ig * co * decay / scale
            grad_log = grad_decay * decay
            grad_rg = grad_log * rate * rg * (1.0 - rg)
            scaled = total * scale
            grad_ig = scaled * co * ig * (1.0 - ig)
            tgx[q, span, lanes] = scaled * ig
            gri[flat(q, start), lanes] = grad_rg.astype(BF16)
            gri[flat(q, start), slice(chans + g * LANES, chans + (g + 1) * LANES)] = grad_ig.astype(BF16)
            add_to(5, lanes, grad_rg)
            add_to(6, lanes, grad_ig)
            add_to(7, lanes, grad_log * (-DECAY_SCALE * rg))

        over(h, gates_back)

        def thru_mm(i, h=h):
            span = at((h * GROUP + i) * here, here, 16)
            got = dot_nt(gri[span, :], w_ri[...].reshape(GROUP * chans, two))
            ghu[span, :] = got.astype(BF16)

        loop(GROUP, thru_mm)
        merge(thru_cols, thru_first, thru_slots, h)
    for h in range(2):
        merge_relay(thru_cols, thru_first, thru_second, thru_slots, h, half // 16, sixteen)

    def grad_ri(i):
        got = dot_tn(conv[:, at(i * chans, chans, LANES)], gri[...])
        w_ri[i] = got.astype(BF16).reshape(RING, cblk, two)

    loop(GROUP, grad_ri)
    for k in (1, 3, 2, 0):
        sum_pair_end(hi, k)
    for k in (1, 3, 2, 0):
        sum_pair_end(dn, k)
    sum_pair(up)

    for h in range(2):
        merge_end(thru_first, thru_second, thru_slots, h)

        def conv_grad(q, start, lanes, g, h=h):
            span = flat(q, start)
            total = ghu[span, at(b * chans + g * LANES, LANES, LANES)].astype(F32)
            total = total + prod[span, lanes].astype(F32) + gout[span, lanes].astype(F32)
            tgx[q, pl.ds(start, STEP), lanes] += total

        over(h, conv_grad)

    def halo_in():
        return pltpu.make_async_remote_copy(
            src_ref=tgx.at[:, pl.ds(0, EDGE)],
            dst_ref=tgx.at[:, pl.ds(here, EDGE)],
            send_sem=net.send.at[halo_back],
            recv_sem=net.recv.at[halo_back],
            device_id=(ring_from[1], b),
            device_id_type=MESH,
        )

    @pl.when(s > 0)
    def _():
        halo_in().start()

    sum_pair(wo)
    sum_pair(ri)

    @pl.when(s < RING - 1)
    def _():
        net.got(tgx.at[:, pl.ds(here, EDGE)], (ring_to[1], b), halo_back)

    net.flush("part")
    for h in range(2):
        def conv_back(q, start, lanes, g):
            now = tgx[q, pl.ds(start, STEP), lanes]
            ids = tgx[q, pl.ds(start, STEP), marks]
            total = vec[0:1, lanes] * now
            add_to(4, lanes, now)
            add_to(0, lanes, now * brx[q, pl.ds(EDGE + start, STEP), lanes])
            for k in range(1, 4):
                later = pl.ds(start + k, STEP)
                match = (tgx[q, later, marks] == ids).astype(F32)
                total = total + vec[k : k + 1, lanes] * tgx[q, later, lanes] * match
                lag = brx[q, pl.ds(EDGE + start - k, STEP), lanes]
                add_to(k, lanes, now * lag * same(q, start, k))
            ggb[flat(q, start), slice(chans + g * LANES, chans + (g + 1) * LANES)] = total.astype(BF16)

        over(h, conv_back)

        def first_back(i, h=h):
            span = at((h * GROUP + i) * here, here, 16)
            part[span, :] = dot_nt(ggb[span, :], w_one[...]).astype(BF16)

        loop(GROUP, first_back)
        merge(part_rows, first_in, gn_slots, h)
    for h in range(2):
        merge_relay(part_rows, first_in, second_in, gn_slots, h, tiles16, sixteen)

    def grad_one(i):
        cols = at(i * 256, 256, LANES)
        w_one[at(i * 256, 256, 16), :] = dot_tn(norm[:, cols], ggb[...]).astype(BF16)

    loop(width // 256, grad_one)
    sum_pair(one)
    for c in (up, wo, ri):
        for k in (1, 3, 2, 0):
            sum_pair_end(c, k)

    for h in range(2):
        merge_end(first_in, second_in, gn_slots, h)

        def first_norm(i, h=h):
            back = norm_grad(0, own(x, h, i)[...], merged(h, i), gain_one)
            own(gin, h, i)[...] = own(gin, h, i)[...] + back

        loop(tiles16, first_norm)

    for k in range(8):
        vs[s, k : k + 1, 0:chans] = jnp.sum(acc[k], axis=0, keepdims=True)
    piece = width // 4
    for k in range(2):
        total = jnp.sum(gain_acc[k], axis=0, keepdims=True)
        for j in range(4):
            vs[s, 4 * k + j : 4 * k + j + 1, chans : chans + piece] = total[:, j * piece : (j + 1) * piece]
    for k in range(1, RING):
        net.put(vs.at[s], vs.at[s], (ring_to[k], b), vec_slots[k])

    for k in (1, 3, 2, 0):
        sum_pair_end(one, k)

    def keep_down(i, total):
        g_d[at(i * 16, 16, 16), :] = total

    def keep_out(i, total):
        g_o[at(i * 16, 16, 16), :] = total

    sum_end(dn, keep_down)
    sum_end_spread(hi)
    sum_end_spread(up)
    sum_end(wo, keep_out)
    for k in range(1, RING):
        net.got(vs.at[ring_from[k]], (ring_from[k], b), vec_slots[k])
    total = vs[0]
    for q in range(1, RING):
        total = total + vs[q]
    vb[b] = total
    for (peer, to), slot in zip(group_peers, last_slots):
        net.put(vb.at[b], vb.at[b], to, slot)
    sum_end_spread(ri)
    sum_end_spread(one)
    for (peer, to), slot in zip(group_peers, last_slots):
        net.got(vb.at[peer], to, slot)
    g_vec[:, 0:chans] = total[:, 0:chans]
    summed = vb[0, :, chans : chans + piece]
    for q in range(1, GROUP):
        summed = summed + vb[q, :, chans : chans + piece]
    g_vec[:, chans : chans + piece] = summed
    for c in (hi, up, ri, one):
        home_wait(c)
    net.flush()

    @pl.when(s < RING - 1)
    def _():
        halo_out().wait_send()

    @pl.when(s > 0)
    def _():
        halo_in().wait_send()


def by_member(array, parts):
    lead = array.shape[:-1]
    split = array.reshape(*lead, RING, GROUP, parts)
    return jnp.moveaxis(split, -2, 0).reshape(GROUP, *lead, RING * parts)


def from_members(array, parts):
    members, count, _ = array.shape
    split = array.reshape(members, count, RING, parts)
    return jnp.moveaxis(split, 0, 2).reshape(count, RING * members * parts)


def split_block(
    inputs,
    segments,
    w_gate,
    w_input,
    w_recur,
    w_inject,
    w_output,
    w_hidden,
    w_upward,
    w_down,
    gain_one,
    gain_two,
    conv_taps,
    conv_bias,
    recur_bias,
    inject_bias,
    decay_param,
    cotangent,
):
    count, here, width = inputs.shape
    channels = w_gate.shape[1]
    chans, hid = (channels // GROUP, w_hidden.shape[1] // GROUP)
    blk, cblk, fblk = (w_gate.shape[0], w_recur.shape[0], w_down.shape[0])
    tokens = GROUP * count * here
    rows = GROUP * count
    s, b = (lax.axis_index("seq"), lax.axis_index("batch"))
    ids = jnp.broadcast_to(
        segments.astype(BF16).reshape(count * here, 1), (count * here, LANES)
    )
    first = jnp.concatenate([w_gate, w_recur], axis=0)
    second = jnp.concatenate([w_input, w_inject], axis=0)
    xw = jnp.concatenate([by_member(first, cblk), by_member(second, cblk)], axis=-1)
    xhu = jnp.concatenate([by_member(w_hidden, fblk), by_member(w_upward, fblk)], axis=-1)
    rate = -DECAY_SCALE * jax.nn.softplus(decay_param)
    vectors = jnp.concatenate(
        [conv_taps, jnp.stack([conv_bias, recur_bias, inject_bias, rate])], axis=0
    ).reshape(8, RING, GROUP, cblk)
    vec = lax.dynamic_index_in_dim(vectors, b, axis=2, keepdims=False).reshape(8, chans)
    gains = jnp.stack([gain_one, gain_two])

    wide = chans + LANES
    size_one = GROUP * blk
    operands = {
        "x": inputs.reshape(count * here, width),
        "cot": cotangent.reshape(count * here, width),
        "seg": ids,
        "xw": xw.reshape(GROUP * (blk + cblk), 2 * chans),
        "xhu": xhu.reshape(GROUP * blk, 2 * hid),
        "own_o": w_output,
        "own_d": w_down,
        "gains": gains,
        "vec": vec,
    }
    piece = width // 4
    outputs = {
        "out": ((count * here, width), F32),
        "gin": ((count * here, width), F32),
        "fin": ((GROUP * (blk + cblk), 2 * chans), BF16),
        "fin_hu": ((GROUP * blk, 2 * hid), BF16),
        "g_o": ((cblk, width), F32),
        "g_d": ((fblk, width), F32),
        "g_vec": ((8, chans + piece), F32),
    }
    scratch = {
        "w_one": ((width, 2 * chans), BF16),
        "w_ri": ((GROUP, RING, cblk, 2 * chans), BF16),
        "w_o": ((chans, width), BF16),
        "w_hu": ((width, 2 * hid), BF16),
        "w_d": ((hid, width), BF16),
        "norm": ((tokens, width + LANES), BF16),
        "gout": ((tokens, width), BF16),
        "norm_two": ((tokens, width), BF16),
        "gres": ((tokens, width), BF16),
        "conv": ((tokens, channels), BF16),
        "mix": ((tokens, chans), BF16),
        "prod": ((tokens, hid), BF16),
        "ghu": ((tokens, 2 * hid), BF16),
        "ggb": ((tokens, 2 * chans), BF16),
        "gri": ((tokens, 2 * chans), BF16),
        "part": ((tokens, width), BF16),
        "brx": ((rows, EDGE + here, wide), F32),
        "tgx": ((rows, here + EDGE, wide), F32),
        "stx": ((rows, EDGE + here, chans), F32),
        "gate_pre": ((rows, here, chans), F32),
        "conv_out": ((rows, here, chans), F32),
        "rgate": ((rows, here, chans), F32),
        "igate": ((rows, here, chans), F32),
        "carry": ((rows, here, chans), F32),
        "pre": ((here, 2 * hid), F32),
        "core_in": ((2, 2, here, width), BF16),
        "x_in": ((2, here, width), BF16),
        "pre_f": ((RING, 2 * rows, chans), F32),
        "pre_b": ((RING, 2 * rows, chans), F32),
        "y_ri": ((DEPTH, GROUP, cblk, 2 * chans), BF16),
        "z_ri": ((DEPTH - 1, GROUP, cblk, 2 * chans), BF16),
        "y_o": ((DEPTH * cblk, width), BF16),
        "z_o": (((DEPTH - 1) * cblk, width), BF16),
        "y_h": ((DEPTH * size_one, hid), BF16),
        "z_h": (((DEPTH - 1) * size_one, hid), BF16),
        "y_u": ((DEPTH * size_one, hid), BF16),
        "z_u": (((DEPTH - 1) * size_one, hid), BF16),
        "y_d": ((DEPTH * fblk, width), BF16),
        "z_d": (((DEPTH - 1) * fblk, width), BF16),
        "acc": ((8, 8, chans), F32),
        "gain_acc": ((2, 8, width), F32),
        "vs": ((RING, 8, chans + piece), F32),
        "vb": ((GROUP, 8, chans + piece), F32),
    }
    names = [*operands, *outputs, *scratch, "send", "recv"]
    in_vmem = pl.BlockSpec(memory_space=pltpu.VMEM)
    got = pl.pallas_call(
        functools.partial(fused, names),
        out_shape=[jax.ShapeDtypeStruct(shape, kind) for shape, kind in outputs.values()],
        in_specs=[in_vmem] * len(operands),
        out_specs=[in_vmem] * len(outputs),
        scratch_shapes=[pltpu.VMEM(shape, kind) for shape, kind in scratch.values()]
        + [pltpu.SemaphoreType.DMA((SLOTS,))] * 2,
        compiler_params=pltpu.CompilerParams(
            collective_id=0, has_side_effects=True, vmem_limit_bytes=VMEM_BYTES
        ),
        name="block",
    )(*operands.values())
    out, gin, fin, fin_hu, g_o, g_d, g_vec = got
    fin = fin.reshape(GROUP, blk + cblk, 2 * chans)
    fin_hu = fin_hu.reshape(GROUP, blk, 2 * hid)
    first = from_members(fin[:, :, :chans], cblk).astype(F32)
    second = from_members(fin[:, :, chans:], cblk).astype(F32)
    hidden = from_members(fin_hu[:, :, :hid], fblk).astype(F32)
    upward = from_members(fin_hu[:, :, hid:], fblk).astype(F32)
    mine = lax.dynamic_slice_in_dim(g_vec, s * cblk, cblk, axis=1)
    place = s * GROUP + b
    gain_sums = g_vec[:, chans:].reshape(2, width)
    gain_mine = lax.dynamic_slice_in_dim(gain_sums, place * blk, blk, axis=1)
    slope = jax.nn.sigmoid(lax.dynamic_slice_in_dim(decay_param, place * cblk, cblk))
    return (
        out.reshape(count, here, width),
        gin.reshape(count, here, width),
        first[:blk],
        second[:blk],
        first[blk:],
        second[blk:],
        g_o,
        hidden,
        upward,
        g_d,
        gain_mine[0],
        gain_mine[1],
        mine[0:4],
        mine[4],
        mine[5],
        mine[6],
        mine[7] * slope,
    )


def solution(mesh):
    fits = dict(mesh.shape) == {"seq": RING, "batch": GROUP}
    return jax.shard_map(
        split_block if fits else gathered_block,
        mesh=mesh,
        in_specs=(
            P("batch", "seq", None),
            P("batch", "seq"),
            P(("seq", "batch"), None),
            P(("seq", "batch"), None),
            P(("seq", "batch"), None),
            P(("seq", "batch"), None),
            P(("seq", "batch"), None),
            P(("seq", "batch"), None),
            P(("seq", "batch"), None),
            P(("seq", "batch"), None),
            P(),
            P(),
            P(),
            P(),
            P(),
            P(),
            P(),
            P("batch", "seq", None),
        ),
        out_specs=(
            P("batch", "seq", None),
            P("batch", "seq", None),
            P(("seq", "batch"), None),
            P(("seq", "batch"), None),
            P(("seq", "batch"), None),
            P(("seq", "batch"), None),
            P(("seq", "batch"), None),
            P(("seq", "batch"), None),
            P(("seq", "batch"), None),
            P(("seq", "batch"), None),
            P(("seq", "batch")),
            P(("seq", "batch")),
            P(None, ("seq", "batch")),
            P(("seq", "batch")),
            P(("seq", "batch")),
            P(("seq", "batch")),
            P(("seq", "batch")),
        ),
        check_vma=False,
    )
```

```python
import functools

import jax
import jax.numpy as jnp
from jax import lax
from jax.experimental import pallas as pl
from jax.experimental.pallas import tpu as pltpu
from jax.sharding import PartitionSpec as P

EPSILON = 1e-06
DECAY_SCALE = 8.0
FLOOR_TERM = 0.01
SLOTS = 240
VMEM_BYTES = 62 << 20


def shifted(array, axis, by):
    peers = lax.axis_size(axis)
    pairs = [(i, i + by) for i in range(peers) if 0 <= i + by < peers]
    return lax.ppermute(array, axis, pairs)


def prefix(value, axis, join, neutral, backward):
    count, mine = (lax.axis_size(axis), lax.axis_index(axis))
    pieces = jax.tree.map(lambda part: lax.all_gather(part, axis), value)
    if backward:
        pieces = jax.tree.map(lambda part: part[::-1], pieces)
        mine = count - 1 - mine
    so_far = jax.tree.map(
        lambda part, zero: jnp.full_like(part, 0) + jnp.asarray(zero, part.dtype), value, neutral
    )

    def turn(position, so_far):
        longer = join(so_far, jax.tree.map(lambda part: part[position], pieces))
        return jax.tree.map(lambda new, old: jnp.where(position < mine, new, old), longer, so_far)

    return lax.fori_loop(0, count - 1, turn, so_far)


def shortened(array):
    return jax.tree.map(lambda a: a.astype(jnp.bfloat16) if a.dtype == jnp.float32 else a, array)


def combine(earlier, later):
    return (earlier[0] * later[0], later[1] + later[0] * earlier[1])


def matmul_plain(left, right):
    return jnp.dot(left, right, preferred_element_type=jnp.float32)


def matmul_tleft(left, right):
    return jnp.einsum("ta,tb->ab", left, right, preferred_element_type=jnp.float32)


def matmul_tright(left, right):
    return jnp.einsum("ta,ba->tb", left, right, preferred_element_type=jnp.float32)


def norm_forward(values, gain):
    scaler = lax.rsqrt(jnp.mean(values * values, axis=-1, keepdims=True) + EPSILON)
    return (values * scaler * gain, scaler)


def norm_back(values, scaler, gain, incoming):
    scaled = incoming * gain
    grad_gain = jnp.sum(incoming * values * scaler, axis=0)
    inner = jnp.mean(scaled * values, axis=-1, keepdims=True)
    return (scaler * (scaled - values * scaler * scaler * inner), grad_gain)


def gathered_block(
    inputs,
    segments,
    w_gate,
    w_input,
    w_recur,
    w_inject,
    w_output,
    w_hidden,
    w_upward,
    w_down,
    gain_one,
    gain_two,
    conv_taps,
    conv_bias,
    recur_bias,
    inject_bias,
    decay_param,
    cotangent,
):
    row_count, positions, features = inputs.shape
    (
        gate_full,
        input_full,
        recur_full,
        inject_full,
        output_full,
        hidden_full,
        upward_full,
        down_full,
    ) = (
        lax.all_gather(w_gate, ("seq", "batch"), axis=0, tiled=True),
        lax.all_gather(w_input, ("seq", "batch"), axis=0, tiled=True),
        lax.all_gather(w_recur, ("seq", "batch"), axis=0, tiled=True),
        lax.all_gather(w_inject, ("seq", "batch"), axis=0, tiled=True),
        lax.all_gather(w_output, ("seq", "batch"), axis=0, tiled=True),
        lax.all_gather(w_hidden, ("seq", "batch"), axis=0, tiled=True),
        lax.all_gather(w_upward, ("seq", "batch"), axis=0, tiled=True),
        lax.all_gather(w_down, ("seq", "batch"), axis=0, tiled=True),
    )
    channels = gate_full.shape[1]
    tokens_here = row_count * positions
    flat_in = inputs.reshape(tokens_here, features)
    normed, scale_one = norm_forward(flat_in, gain_one)
    normed_low = normed.astype(jnp.bfloat16)
    gate_pre = matmul_plain(normed_low, gate_full)
    gate_act, gate_pull = jax.vjp(jax.nn.gelu, gate_pre)
    branch = matmul_plain(normed_low, input_full).reshape(row_count, positions, channels)
    seg_marks = segments.astype(jnp.float32) + 1.0
    prior_branch, prior_marks = shifted(
        (branch[:, positions - 3 :], seg_marks[:, positions - 3 :]), "seq", 1
    )
    ext_branch = jnp.concatenate([prior_branch, branch], axis=1)
    ext_marks = jnp.concatenate([prior_marks, seg_marks], axis=1)
    sames = []
    lagged = []
    for offset in range(4):
        sames.append(
            (ext_marks[:, 3 - offset : 3 - offset + positions] == seg_marks).astype(jnp.float32)[
                :, :, None
            ]
        )
        lagged.append(ext_branch[:, 3 - offset : 3 - offset + positions])
    conv_out = conv_bias + conv_taps[0] * branch
    for offset in range(1, 4):
        conv_out = conv_out + conv_taps[offset] * lagged[offset] * sames[offset]
    conv_low = conv_out.reshape(tokens_here, channels).astype(jnp.bfloat16)
    recur_gate = jax.nn.sigmoid(matmul_plain(conv_low, recur_full) + recur_bias).reshape(
        row_count, positions, channels
    )
    inject_gate = jax.nn.sigmoid(matmul_plain(conv_low, inject_full) + inject_bias).reshape(
        row_count, positions, channels
    )
    base_rate = jax.nn.softplus(decay_param)
    decays = jnp.exp(-DECAY_SCALE * recur_gate * base_rate)
    carry_mult = decays * sames[1]
    normalizer = jnp.sqrt(1.0 - decays * decays + FLOOR_TERM)
    injected = normalizer * inject_gate * conv_out
    cumul, local_state = lax.associative_scan(combine, (carry_mult, injected), axis=1)
    ones_rows = jnp.ones((row_count, channels), jnp.float32)
    zeros_rows = jnp.zeros((row_count, channels), jnp.float32)
    entry = prefix(
        (cumul[:, -1], local_state[:, -1]), "seq", combine, (ones_rows, zeros_rows), False
    )[1]
    states = local_state + cumul * entry[:, None]
    states_before = jnp.concatenate([entry[:, None], states[:, :-1]], axis=1)
    states_flat = states.reshape(tokens_here, channels)
    mixed = (states_flat * gate_act).astype(jnp.bfloat16)
    resid = flat_in + matmul_plain(mixed, output_full)
    normed_two, scale_two = norm_forward(resid, gain_two)
    normed_two_low = normed_two.astype(jnp.bfloat16)
    hidden_pre = matmul_plain(normed_two_low, hidden_full)
    upward_pre = matmul_plain(normed_two_low, upward_full)
    hidden_act, hidden_pull = jax.vjp(jax.nn.gelu, hidden_pre)
    product = (hidden_act * upward_pre).astype(jnp.bfloat16)
    output = resid + matmul_plain(product, down_full)
    grad_out = cotangent.reshape(tokens_here, features)
    grad_out_low = grad_out.astype(jnp.bfloat16)
    grad_down = matmul_tleft(product, grad_out_low)
    grad_product = matmul_tright(grad_out_low, down_full)
    grad_hidden_pre = hidden_pull(grad_product * upward_pre)[0].astype(jnp.bfloat16)
    grad_upward_pre = (grad_product * hidden_act).astype(jnp.bfloat16)
    grad_hidden = matmul_tleft(normed_two_low, grad_hidden_pre)
    grad_upward = matmul_tleft(normed_two_low, grad_upward_pre)
    grad_normed_two = matmul_tright(grad_hidden_pre, hidden_full) + matmul_tright(
        grad_upward_pre, upward_full
    )
    grad_resid_norm, grad_gain_two = norm_back(resid, scale_two, gain_two, grad_normed_two)
    grad_resid = grad_out + grad_resid_norm
    grad_resid_low = grad_resid.astype(jnp.bfloat16)
    grad_output = matmul_tleft(mixed, grad_resid_low)
    grad_mixed = matmul_tright(grad_resid_low, output_full)
    grad_gate_pre = gate_pull(grad_mixed * states_flat)[0].astype(jnp.bfloat16)
    grad_states = (grad_mixed * gate_act).reshape(row_count, positions, channels)
    next_mult = jnp.concatenate([carry_mult[:, 1:], jnp.ones_like(carry_mult[:, :1])], axis=1)
    tail_prod, local_grad = lax.associative_scan(
        combine, (next_mult, grad_states), axis=1, reverse=True
    )
    incoming = prefix(
        (cumul[:, -1], carry_mult[:, 0] * local_grad[:, 0]),
        "seq",
        combine,
        (ones_rows, zeros_rows),
        True,
    )[1]
    total_grad = local_grad + tail_prod * incoming[:, None]
    grad_decays = (
        total_grad * states_before * sames[1]
        - total_grad * inject_gate * conv_out * decays / normalizer
    )
    grad_log = grad_decays * decays
    grad_recur_pre = grad_log * (-DECAY_SCALE * base_rate) * recur_gate * (1.0 - recur_gate)
    grad_decay_param = jnp.sum(
        grad_log * (-DECAY_SCALE * recur_gate), axis=(0, 1)
    ) * jax.nn.sigmoid(decay_param)
    grad_inject_pre = total_grad * normalizer * conv_out * inject_gate * (1.0 - inject_gate)
    grad_recur_bias = jnp.sum(grad_recur_pre, axis=(0, 1))
    grad_inject_bias = jnp.sum(grad_inject_pre, axis=(0, 1))
    grad_recur_low = grad_recur_pre.reshape(tokens_here, channels).astype(jnp.bfloat16)
    grad_inject_low = grad_inject_pre.reshape(tokens_here, channels).astype(jnp.bfloat16)
    grad_recur = matmul_tleft(conv_low, grad_recur_low)
    grad_inject = matmul_tleft(conv_low, grad_inject_low)
    through_gates = matmul_tright(grad_recur_low, recur_full) + matmul_tright(
        grad_inject_low, inject_full
    )
    grad_conv = total_grad * normalizer * inject_gate + through_gates.reshape(
        row_count, positions, channels
    )
    grad_conv_bias = jnp.sum(grad_conv, axis=(0, 1))
    taps_by_channel = jnp.stack(
        [jnp.sum(grad_conv * lagged[offset] * sames[offset], axis=(0, 1)) for offset in range(4)],
        axis=1,
    )
    later_grad, later_marks = (
        shifted(shortened(grad_conv[:, :3]), "seq", -1),
        shifted(seg_marks[:, :3].astype(jnp.bfloat16), "seq", -1).astype(jnp.float32),
    )
    ext_grad = jnp.concatenate([grad_conv, later_grad], axis=1)
    ext_after = jnp.concatenate([seg_marks, later_marks], axis=1)
    grad_branch = conv_taps[0] * grad_conv
    for offset in range(1, 4):
        match = (ext_after[:, offset : offset + positions] == seg_marks).astype(jnp.float32)[
            :, :, None
        ]
        grad_branch = (
            grad_branch + conv_taps[offset] * ext_grad[:, offset : offset + positions] * match
        )
    grad_branch_low = grad_branch.reshape(tokens_here, channels).astype(jnp.bfloat16)
    grad_input = matmul_tleft(normed_low, grad_branch_low)
    grad_gate = matmul_tleft(normed_low, grad_gate_pre)
    grad_normed = matmul_tright(grad_gate_pre, gate_full) + matmul_tright(
        grad_branch_low, input_full
    )
    grad_first_norm, grad_gain_one = norm_back(flat_in, scale_one, gain_one, grad_normed)
    grad_inputs = (grad_resid + grad_first_norm).reshape(row_count, positions, features)
    every = (
        lax.psum_scatter(grad_gate, ("seq", "batch"), scatter_dimension=0, tiled=True),
        lax.psum_scatter(grad_input, ("seq", "batch"), scatter_dimension=0, tiled=True),
        lax.psum_scatter(grad_recur, ("seq", "batch"), scatter_dimension=0, tiled=True),
        lax.psum_scatter(grad_inject, ("seq", "batch"), scatter_dimension=0, tiled=True),
        lax.psum_scatter(grad_output, ("seq", "batch"), scatter_dimension=0, tiled=True),
        lax.psum_scatter(grad_hidden, ("seq", "batch"), scatter_dimension=0, tiled=True),
        lax.psum_scatter(grad_upward, ("seq", "batch"), scatter_dimension=0, tiled=True),
        lax.psum_scatter(grad_down, ("seq", "batch"), scatter_dimension=0, tiled=True),
        lax.psum_scatter(grad_gain_one, ("seq", "batch"), scatter_dimension=0, tiled=True),
        lax.psum_scatter(grad_gain_two, ("seq", "batch"), scatter_dimension=0, tiled=True),
        lax.psum_scatter(taps_by_channel, ("seq", "batch"), scatter_dimension=0, tiled=True),
        lax.psum_scatter(grad_conv_bias, ("seq", "batch"), scatter_dimension=0, tiled=True),
        lax.psum_scatter(grad_recur_bias, ("seq", "batch"), scatter_dimension=0, tiled=True),
        lax.psum_scatter(grad_inject_bias, ("seq", "batch"), scatter_dimension=0, tiled=True),
        lax.psum_scatter(grad_decay_param, ("seq", "batch"), scatter_dimension=0, tiled=True),
    )
    summed = (
        every[0],
        every[1],
        every[2],
        every[3],
        every[4],
        every[5],
        every[6],
        every[7],
        every[8],
        every[9],
        every[10].T,
        every[11],
        every[12],
        every[13],
        every[14],
    )
    return (
        output.reshape(row_count, positions, features),
        grad_inputs,
        summed[0],
        summed[1],
        summed[2],
        summed[3],
        summed[4],
        summed[5],
        summed[6],
        summed[7],
        summed[8],
        summed[9],
        summed[10],
        summed[11],
        summed[12],
        summed[13],
        summed[14],
    )


MESH = pl.DeviceIdType.MESH
F32, BF16 = (jnp.float32, jnp.bfloat16)
LANES = 128
EDGE = 8
STEP = 32
DEPTH, PAIR, GROUP = (4, 2, 4)
RING = DEPTH * PAIR


def dot_nn(left, right):
    return lax.dot_general(left, right, (((1,), (0,)), ((), ())), preferred_element_type=F32)


def dot_nt(left, right):
    return lax.dot_general(left, right, (((1,), (1,)), ((), ())), preferred_element_type=F32)


def dot_tn(left, right):
    return lax.dot_general(left, right, (((0,), (0,)), ((), ())), preferred_element_type=F32)


def gelu_parts(value):
    rate = 0.7978845608028654
    square = value * value
    bent = jnp.tanh(rate * (value + 0.044715 * square * value))
    act = 0.5 * value * (1.0 + bent)
    slope = 0.5 * (1.0 + bent) + 0.5 * rate * value * (1.0 - bent * bent) * (1.0 + 0.134145 * square)
    return (act, slope)


def at(start, size, of):
    return pl.ds(pl.multiple_of(start, of), size)


def loop(count, body):
    def turn(i, nothing):
        body(i)
        return nothing

    lax.fori_loop(0, count, turn, 0)


class Net:
    def __init__(self, send, recv):
        self.send, self.recv, self.used, self.open = (send, recv, 0, {})

    def slots(self, count):
        first = self.used
        self.used += count
        return list(range(first, first + count))

    def put(self, src, dst, to, slot, tag=""):
        copy = pltpu.make_async_remote_copy(
            src_ref=src,
            dst_ref=dst,
            send_sem=self.send.at[slot],
            recv_sem=self.recv.at[slot],
            device_id=to,
            device_id_type=MESH,
        )
        copy.start()
        self.open.setdefault(tag, []).append(copy)

    def got(self, dst, to, slot):
        pltpu.make_async_remote_copy(
            src_ref=dst,
            dst_ref=dst,
            send_sem=self.send.at[slot],
            recv_sem=self.recv.at[slot],
            device_id=to,
            device_id_type=MESH,
        ).wait_recv()

    def flush(self, *tags):
        for tag in tags or list(self.open):
            for copy in self.open.pop(tag, []):
                copy.wait_send()


def fused(names, *refs):
    r = dict(zip(names, refs))
    out_hbm, gin_hbm, fin, fin_hu, g_o, g_d, g_vec = (
        r[k] for k in ("out", "gin", "fin", "fin_hu", "g_o", "g_d", "g_vec")
    )
    x, cot, out, gin, vec, gains = (r[k] for k in ("x", "cot", "out_own", "gin_own", "vec", "gains"))
    w_one, w_ri, w_o, w_hu, w_d = (r[k] for k in ("w_one", "w_ri", "w_o", "w_hu", "w_d"))
    norm, gout, norm_two, gres, conv, mix = (
        r[k] for k in ("norm", "gout", "norm_two", "gres", "conv", "mix")
    )
    prod, ghu, ggb, gri, part = (r[k] for k in ("prod", "ghu", "ggb", "gri", "part"))
    brx, tgx, stx, gate_pre, conv_out = (r[k] for k in ("brx", "tgx", "stx", "gate_pre", "conv_out"))
    rgate, igate, carry, pre = (r[k] for k in ("rgate", "igate", "carry", "pre"))
    core_in, x_in, pre_f, pre_b = (r[k] for k in ("core_in", "x_in", "pre_f", "pre_b"))
    acc, gain_acc, vs, vb = (r[k] for k in ("acc", "gain_acc", "vs", "vb"))
    net = Net(r["send"], r["recv"])

    width = x.shape[1]
    here = carry.shape[1]
    chans = carry.shape[2]
    hid = prod.shape[1]
    rows = 2 * GROUP
    half = GROUP * here
    blk, cblk, fblk = (width // (RING * GROUP), chans // RING, hid // RING)
    groups = [slice(g * LANES, (g + 1) * LANES) for g in range(chans // LANES)]
    marks = slice(chans, chans + LANES)

    s = lax.axis_index("seq")
    b = lax.axis_index("batch")
    z, y = (s // PAIR, s % PAIR)
    mate, across, corner = (
        (b // 2) * 2 + (1 - b % 2),
        (1 - b // 2) * 2 + b % 2,
        (1 - b // 2) * 2 + (1 - b % 2),
    )
    to_mate, to_across, to_corner = ((s, mate), (s, across), (s, corner))
    group_peers = [(mate, to_mate), (across, to_across), (corner, to_corner)]
    to_pair = (z * PAIR + 1 - y, b)
    far = [lax.rem(z + k, DEPTH) for k in range(DEPTH)]
    near = [lax.rem(z + DEPTH - k, DEPTH) for k in range(DEPTH)]
    ring_to = [lax.rem(s + k, RING) for k in range(RING)]
    ring_from = [lax.rem(s + RING - k, RING) for k in range(RING)]

    def fetch(slot, src, dst):
        copy = pltpu.make_async_copy(src, dst, r["local"].at[slot])
        copy.start()
        return copy

    raw = ghu
    sides = (slice(0, raw.shape[1]), slice(raw.shape[1], 2 * raw.shape[1]))
    spots, place = ({}, 0)
    fetched = {}
    for name, tall in (("w_gate", blk), ("w_input", blk), ("w_recur", cblk), ("w_inject", cblk)):
        spots[name] = place
        fetched[name] = [fetch(len(fetched), r["hbm_" + name], raw.at[pl.ds(place, tall)])]
        place += tall
    fetched["x"] = [fetch(4, r["hbm_x"], x)]
    fetched["seg"] = [fetch(5, r["hbm_seg"], r["seg"])]
    for k, name in enumerate(("gain_one", "gain_two")):
        fetched[name] = [fetch(6 + k, r["hbm_" + name], gains.at[k])]
    for k, name in enumerate(("w_hidden", "w_upward")):
        spots[name] = place
        fetched[name] = [
            fetch(8 + 2 * k + j, r["hbm_" + name].at[:, side], raw.at[pl.ds(place + j * blk, blk)])
            for j, side in enumerate(sides)
        ]
        place += 2 * blk
    fetched["own"] = [
        fetch(12, r["hbm_w_output"], w_o.at[at(s * cblk, cblk, 16)]),
        fetch(13, r["hbm_w_down"], w_d.at[at(s * fblk, fblk, 16)]),
    ]
    fetched["vec"] = [fetch(14, r["hbm_conv_taps"], r["taps"])] + [
        fetch(15 + k, r["hbm_" + name], r["biases"].at[k])
        for k, name in enumerate(("conv_bias", "recur_bias", "inject_bias", "decay_param"))
    ]
    fetched["cot"] = [fetch(19, r["hbm_cot"], cot)]

    def fetch_wait(*which):
        for name in which:
            for copy in fetched[name]:
                copy.wait()

    barrier = pltpu.get_barrier_semaphore()
    for _, to in group_peers:
        pl.semaphore_signal(barrier, inc=1, device_id=to, device_id_type=MESH)
    for k in range(1, RING):
        pl.semaphore_signal(barrier, inc=1, device_id=(ring_to[k], b), device_id_type=MESH)

    class Chunk:
        pass

    def chunk(block, piece, pieces, y_block, y_piece, z_block, z_piece):
        c = Chunk()
        c.block, c.piece, c.pieces = (block, piece, pieces)
        c.y_block, c.y_piece, c.z_block, c.z_piece = (y_block, y_piece, z_block, z_piece)
        c.gather_z = net.slots(DEPTH)
        c.gather_y = net.slots(DEPTH)
        c.sum_y = net.slots(DEPTH)
        c.sum_z = net.slots(DEPTH)
        c.spread = net.slots(3)
        c.home = net.slots(3)
        return c

    def flat_chunk(ref, size, step, cols, y_ref, z_ref):
        def row(base, i):
            return (at(base * size + i * step, step, 16), cols)

        return chunk(
            lambda q: ref.at[at(q * size, size, 16), cols],
            lambda q, i: ref.at[row(q, i)],
            size // step,
            lambda q: y_ref.at[at(q * size, size, 16), slice(0, cols.stop - cols.start)],
            lambda q, i: y_ref.at[at(q * size + i * step, step, 16), slice(0, cols.stop - cols.start)],
            lambda q: z_ref.at[pl.ds(q * size, size), slice(0, cols.stop - cols.start)],
            lambda q, i: z_ref.at[at(q * size + i * step, step, 16), slice(0, cols.stop - cols.start)],
        )

    two = 2 * chans
    size_one = GROUP * blk
    one = flat_chunk(
        w_one, size_one, blk, slice(0, two), norm_two, norm_two.at[pl.ds(DEPTH * size_one, (DEPTH - 1) * size_one)]
    )
    ri = chunk(
        lambda q: w_ri.at[:, q],
        lambda q, i: w_ri.at[i, q],
        GROUP,
        lambda q: r["y_ri"].at[q],
        lambda q, i: r["y_ri"].at[q, i],
        lambda q: r["z_ri"].at[q],
        lambda q, i: r["z_ri"].at[q, i],
    )
    wo = flat_chunk(w_o, cblk, 16, slice(0, width), r["y_o"], r["z_o"])
    hi = flat_chunk(w_hu, size_one, blk, slice(0, hid), r["y_h"], r["z_h"])
    up = flat_chunk(w_hu, size_one, blk, slice(hid, 2 * hid), r["y_u"], r["z_u"])
    dn = flat_chunk(w_d, fblk, 16, slice(0, width), r["y_d"], r["z_d"])

    rec = blk + cblk
    xhu = gri.at[pl.ds(GROUP * rec, 2 * GROUP * blk)]
    one.source = lambda q: gri.at[at(q * rec, blk, 16)]
    one.place = lambda q: w_one.at[at(s * size_one + q * blk, blk, 16)]
    one.result = lambda q: fin.at[at(q * rec, blk, 16)]
    ri.source = lambda q: gri.at[at(q * rec + blk, cblk, 16)]
    ri.place = lambda q: w_ri.at[q, s]
    ri.result = lambda q: fin.at[at(q * rec + blk, cblk, 16)]
    hi.source = lambda q: xhu.at[at(q * blk, blk, 16)]
    hi.place = lambda q: w_hu.at[at(s * size_one + q * blk, blk, 16), slice(0, hid)]
    hi.result = lambda q: fin_hu.at[at(q * blk, blk, 16), slice(0, hid)]
    up.source = lambda q: xhu.at[at((GROUP + q) * blk, blk, 16)]
    up.place = lambda q: w_hu.at[at(s * size_one + q * blk, blk, 16), slice(hid, 2 * hid)]
    up.result = lambda q: fin_hu.at[at(q * blk, blk, 16), slice(hid, 2 * hid)]

    def member_cols(array, q, parts):
        pieces = [array[:, parts * (GROUP * k + q) : parts * (GROUP * k + q + 1)] for k in range(RING)]
        return jnp.concatenate(pieces, axis=1)

    def prepare(c, tall, parts, *names):
        for q in range(GROUP):
            for k, name in enumerate(names):
                array = raw[spots[name] : spots[name] + tall, :]
                if array.shape[1] < RING * GROUP * parts:
                    array = jnp.concatenate([array, raw[spots[name] + tall : spots[name] + 2 * tall, :]], axis=1)
                c.source(q)[:, k * RING * parts : (k + 1) * RING * parts] = member_cols(array, q, parts)

    def spread(c):
        for (peer, to), slot in zip(group_peers, c.spread):
            net.put(c.source(peer), c.place(b), to, slot)
        c.place(b)[...] = c.source(b)[...]

    def spread_wait(c):
        for (peer, to), slot in zip(group_peers, c.spread):
            net.got(c.place(peer), to, slot)

    def gz(c, *which):
        for k in which:
            net.put(c.block(s), c.block(s), (far[k] * PAIR + y, b), c.gather_z[k])

    def gy(c):
        net.put(c.block(s), c.block(s), to_pair, c.gather_y[0])

    def gr(c, *which):
        for k in which:
            from_z = near[k] * PAIR + y
            net.got(c.block(from_z), (from_z, b), c.gather_z[k])
            net.put(c.block(from_z), c.block(from_z), to_pair, c.gather_y[k])

    def gather_wait(c):
        for k in range(DEPTH):
            net.got(c.block(near[k] * PAIR + 1 - y), to_pair, c.gather_y[k])

    def sp(c, *which):
        for k in which:
            net.put(c.block(far[k] * PAIR + 1 - y), c.y_block(far[k]), to_pair, c.sum_y[k])

    def se(c, *which):
        for k in which:
            sum_pair_end(c, k)

    def sum_pair_end(c, k):
        net.got(c.y_block(far[k]), to_pair, c.sum_y[k])
        mine = far[k] * PAIR + y

        def add(i):
            total = c.piece(mine, i)[...].astype(F32) + c.y_piece(far[k], i)[...].astype(F32)
            c.piece(mine, i)[...] = total.astype(BF16)

        loop(c.pieces, add)
        if k:
            net.put(c.block(mine), c.z_block(k - 1), (mine, b), c.sum_z[k])

    def sum_end(c, keep):
        for k in range(1, DEPTH):
            net.got(c.z_block(k - 1), (near[k] * PAIR + y, b), c.sum_z[k])

        def add(i):
            total = c.piece(s, i)[...].astype(F32)
            for k in range(DEPTH - 1):
                total = total + c.z_piece(k, i)[...].astype(F32)
            keep(i, total)

        loop(c.pieces, add)

    def sum_end_spread(c):
        def keep(i, total):
            c.piece(s, i)[...] = total.astype(BF16)

        sum_end(c, keep)
        for (peer, to), slot in zip(group_peers, c.home):
            net.put(c.place(peer), c.result(b), to, slot)
        c.result(b)[...] = c.place(b)[...]

    def home_wait(c):
        for (peer, to), slot in zip(group_peers, c.home):
            net.got(c.result(peer), to, slot)

    def share(view, slots, h):
        net.put(view(b, h), view(b, h), to_across, slots[3 * h])
        net.put(view(b, h), view(b, h), to_mate, slots[3 * h + 1])

    def share_relay(view, slots, h):
        net.got(view(across, h), to_across, slots[3 * h])
        net.put(view(across, h), view(across, h), to_mate, slots[3 * h + 2])

    def share_end(view, slots, h):
        net.got(view(mate, h), to_mate, slots[3 * h + 1])
        net.got(view(corner, h), to_mate, slots[3 * h + 2])

    def token_rows(ref):
        return lambda q, h: ref.at[at((h * GROUP + q) * here, here, 16)]

    def merge(view, first, slots, h):
        net.put(view(corner, h), first(h, 1), to_mate, slots[3 * h], "part")
        net.put(view(mate, h), first(h, 0), to_mate, slots[3 * h + 1], "part")

    def merge_relay(view, first, second, slots, h, parts, tile):
        net.got(first(h, 1), to_mate, slots[3 * h])

        def add(i):
            v = tile(view(across, h), i)
            v[...] = (v[...].astype(F32) + tile(first(h, 1), i)[...].astype(F32)).astype(BF16)

        loop(parts, add)
        net.put(view(across, h), second(h), to_across, slots[3 * h + 2], "part")

    def merge_end(first, second, slots, h):
        net.got(first(h, 0), to_mate, slots[3 * h + 1])
        net.got(second(h), to_across, slots[3 * h + 2])

    def sixteen(ref, i):
        return ref.at[at(i * 16, 16, 16)]

    first_in = lambda h, slot: core_in.at[h, slot]
    second_in = lambda h: x_in.at[h]
    part_rows = token_rows(part)

    def merged(h, i):
        total = sixteen(part_rows(b, h), i)[...].astype(F32)
        return total + core_in[h, 0, at(i * 16, 16, 16)].astype(F32) + x_in[h, at(i * 16, 16, 16)].astype(F32)

    def own(ref, h, i):
        return ref.at[at(h * here + i * 16, 16, 16)]

    tiles16 = here // 16

    def rms(values):
        return lax.rsqrt(jnp.mean(values * values, axis=-1, keepdims=True) + EPSILON)

    def norm_grad(index, values, incoming, gain):
        scaler = rms(values)
        scaled = incoming * gain
        inner = jnp.mean(scaled * values, axis=-1, keepdims=True)
        term = incoming * values * scaler
        gain_acc[index] += term[0:8] + term[8:16]
        return scaler * (scaled - values * (scaler * scaler * inner))

    def over(h, body):
        def row(i):
            q = h * GROUP + i
            for start in range(0, here, STEP):
                for g, lanes in enumerate(groups):
                    body(q, start, lanes, g)

        loop(GROUP, row)

    def flat(q, start):
        return at(q * here + start, STEP, STEP)

    def add_to(index, lanes, values):
        total = values[0:8]
        for k in range(8, STEP, 8):
            total = total + values[k : k + 8]
        acc[index, :, lanes] += total

    def same(q, start, k):
        now = brx[q, pl.ds(EDGE + start, STEP), marks]
        return (now == brx[q, pl.ds(EDGE + start - k, STEP), marks]).astype(F32)

    norm_slots, gout_slots, conv_slots = (net.slots(6), net.slots(6), net.slots(6))
    two_slots, gres_slots = (net.slots(6), net.slots(6))
    out_slots, gnt_slots, down_slots, thru_slots, gn_slots = (net.slots(6) for _ in range(5))
    halo_slot, halo_back = net.slots(2)
    pre_slots, back_slots, vec_slots, last_slots = (
        net.slots(RING),
        net.slots(RING),
        net.slots(RING),
        net.slots(3),
    )
    norm_rows, gout_rows, two_rows, gres_rows = (token_rows(ref) for ref in (norm, gout, norm_two, gres))
    conv_cols = lambda q, h: conv.at[pl.ds(h * half, half), at(q * chans, chans, LANES)]

    fetch_wait("w_gate", "w_input")
    prepare(one, blk, cblk, "w_gate", "w_input")
    fetch_wait("x", "seg", "gain_one", "gain_two")
    gain_one, gain_two = (gains[0:1], gains[1:2])
    pl.semaphore_wait(barrier, 3 + RING - 1)
    spread(one)
    for h in range(2):
        ids = r["seg"][h : h + 1, :].astype(F32)
        norm[at((h * GROUP + b) * here, here, 16), width : width + LANES] = jnp.transpose(
            jnp.broadcast_to(ids, (here, here))
        ).astype(BF16)

        def norm_tile(i, h=h):
            v = own(x, h, i)[...]
            sixteen(norm_rows(b, h), i)[:, 0:width] = (v * rms(v) * gain_one).astype(BF16)

        loop(tiles16, norm_tile)
        share(norm_rows, norm_slots, h)
    fetch_wait("w_recur", "w_inject")
    prepare(ri, cblk, cblk, "w_recur", "w_inject")
    spread(ri)
    spread_wait(one)
    gz(one, 1, 3, 2)
    gy(one)
    fetch_wait("w_hidden")
    prepare(hi, blk, fblk, "w_hidden")
    spread(hi)
    fetch_wait("w_upward")
    prepare(up, blk, fblk, "w_upward")
    spread(up)

    fetch_wait("vec")
    log_of = lambda grown: jnp.log(grown)
    biases = jnp.concatenate([r["biases"][k].reshape(1, -1) for k in range(4)], axis=0)
    small = jnp.exp(biases[3:4])
    grown = 1.0 + small
    rate = jnp.where(grown == 1.0, small, log_of(grown) * small / jnp.where(grown == 1.0, 1.0, grown - 1.0))
    sources = jnp.concatenate([r["taps"][...], biases[0:3], -DECAY_SCALE * rate], axis=0)
    for q in range(GROUP):
        r["vecs"][q, 0:8] = member_cols(sources, q, cblk)
        r["vecs"][q, 8:16] = member_cols(jnp.broadcast_to(jax.nn.sigmoid(biases[3:4]), (8, GROUP * chans)), q, cblk)
    vec[...] = r["vecs"][b]
    acc[...] = jnp.zeros_like(acc)
    gain_acc[...] = jnp.zeros_like(gain_acc)

    @pl.when(s == 0)
    def _():
        brx[:, 0:EDGE, :] = jnp.full((rows, EDGE, chans + LANES), -1.0, F32)

    @pl.when(s == RING - 1)
    def _():
        tgx[:, here : here + EDGE, :] = jnp.full((rows, EDGE, chans + LANES), -1.0, F32)

    gr(one, 1)
    share_relay(norm_rows, norm_slots, 0)
    gr(one, 3)
    fetch_wait("cot")
    for h in range(2):
        def low_tile(i, h=h):
            sixteen(gout_rows(b, h), i)[...] = own(cot, h, i)[...].astype(BF16)

        loop(tiles16, low_tile)
    share_relay(norm_rows, norm_slots, 1)
    gr(one, 2)
    spread_wait(ri)
    gy(ri)
    gz(ri, 1)
    share_end(norm_rows, norm_slots, 0)
    gather_wait(one)

    for h in range(2):
        if h:
            share_end(norm_rows, norm_slots, h)
        span = pl.ds(h * half, half)
        block = slice(h * GROUP, (h + 1) * GROUP)
        got = dot_nn(norm[span, 0:width], w_one[...]).reshape(GROUP, here, two)
        gate_pre[block] = got[:, :, 0:chans]
        brx[block, EDGE : EDGE + here, 0:chans] = got[:, :, chans:two]
        ids = norm[span, width : width + LANES].astype(F32).reshape(GROUP, here, LANES)
        brx[block, EDGE : EDGE + here, marks] = ids
        tgx[block, 0:here, marks] = ids

    def halo_out():
        return pltpu.make_async_remote_copy(
            src_ref=brx.at[:, pl.ds(here, EDGE)],
            dst_ref=brx.at[:, pl.ds(0, EDGE)],
            send_sem=net.send.at[halo_slot],
            recv_sem=net.recv.at[halo_slot],
            device_id=(ring_to[1], b),
            device_id_type=MESH,
        )

    @pl.when(s < RING - 1)
    def _():
        halo_out().start()

    gz(ri, 3, 2)
    gr(ri, 1)

    @pl.when(s > 0)
    def _():
        net.got(brx.at[:, pl.ds(0, EDGE)], (ring_from[1], b), halo_slot)

    for h in range(2):
        def conv_tile(q, start, lanes, g):
            total = vec[4:5, lanes] + vec[0:1, lanes] * brx[q, pl.ds(EDGE + start, STEP), lanes]
            for k in range(1, 4):
                lag = brx[q, pl.ds(EDGE + start - k, STEP), lanes]
                total = total + vec[k : k + 1, lanes] * lag * same(q, start, k)
            conv_out[q, pl.ds(start, STEP), lanes] = total
            conv[flat(q, start), at(b * chans + g * LANES, LANES, LANES)] = total.astype(BF16)

        over(h, conv_tile)
        share(conv_cols, conv_slots, h)
    for h in range(2):
        share(gout_rows, gout_slots, h)
    gr(ri, 3)
    fetch_wait("own")
    gy(wo)
    gz(wo, 1, 3, 2)
    share_relay(conv_cols, conv_slots, 0)
    spread_wait(hi)
    gy(hi)
    gr(ri, 2)
    share_relay(conv_cols, conv_slots, 1)
    gr(wo, 1, 3, 2)
    gz(hi, 1, 3)
    spread_wait(up)
    share_end(conv_cols, conv_slots, 0)
    gather_wait(ri)

    for h in range(2):
        if h:
            share_end(conv_cols, conv_slots, h)
        block = slice(h * GROUP, (h + 1) * GROUP)
        got = dot_nn(conv[pl.ds(h * half, half), :], w_ri[...].reshape(GROUP * chans, two))
        got = got.reshape(GROUP, here, two)
        rgate[block] = got[:, :, 0:chans]
        igate[block] = got[:, :, chans:two]

        def gate_tile(q, start, lanes, g):
            span = pl.ds(start, STEP)
            rg = jax.nn.sigmoid(rgate[q, span, lanes] + vec[5:6, lanes])
            ig = jax.nn.sigmoid(igate[q, span, lanes] + vec[6:7, lanes])
            rgate[q, span, lanes] = rg
            igate[q, span, lanes] = ig
            decay = jnp.exp(rg * vec[7:8, lanes])
            carry[q, span, lanes] = decay * same(q, start, 1)
            scale = jnp.sqrt(1.0 - decay * decay + FLOOR_TERM)
            stx[q, pl.ds(EDGE + start, STEP), lanes] = scale * ig * conv_out[q, span, lanes]

        over(h, gate_tile)

    def ends(p, state):
        mult = carry[:, p, :]
        return (state[0] * mult, mult * state[1] + stx[:, EDGE + p, :])

    begin = (jnp.ones((rows, chans), F32), jnp.zeros((rows, chans), F32))
    product, tail = lax.fori_loop(0, here, ends, begin, unroll=8)
    pre_f[s, 0:rows] = product
    pre_f[s, rows : 2 * rows] = tail
    for k in range(1, RING):
        net.put(pre_f.at[s], pre_f.at[s], (ring_to[k], b), pre_slots[k])
    gr(hi, 1, 3)
    gz(hi, 2)
    gy(up)
    gz(up, 1)

    for h in range(2):
        def act_tile(q, start, lanes, g):
            span = pl.ds(start, STEP)
            tgx[q, span, lanes] = gelu_parts(gate_pre[q, span, lanes])[0]

        over(h, act_tile)
    for k in range(1, RING):
        net.got(pre_f.at[ring_from[k]], (ring_from[k], b), pre_slots[k])
    state = jnp.zeros((rows, chans), F32)
    for q in range(RING - 1):
        state = jnp.where(q < s, pre_f[q, rows : 2 * rows] + pre_f[q, 0:rows] * state, state)
    stx[:, EDGE - 1, :] = state

    def scan(p, state):
        state = carry[:, p, :] * state + stx[:, EDGE + p, :]
        stx[:, EDGE + p, :] = state
        return state

    lax.fori_loop(0, here, scan, state, unroll=8)
    gather_wait(wo)

    for h in range(2):
        def mix_tile(q, start, lanes, g):
            act = tgx[q, pl.ds(start, STEP), lanes]
            mix[flat(q, start), lanes] = (stx[q, pl.ds(EDGE + start, STEP), lanes] * act).astype(BF16)

        over(h, mix_tile)
        span = pl.ds(h * half, half)
        part[span, :] = dot_nn(mix[span, :], w_o[...]).astype(BF16)
        merge(part_rows, first_in, out_slots, h)
    gr(hi, 2)
    gr(up, 1)
    gz(up, 3, 2)
    for h in range(2):
        share_relay(gout_rows, gout_slots, h)
    for h in range(2):
        merge_relay(part_rows, first_in, second_in, out_slots, h, tiles16, sixteen)
    gr(up, 3)
    gy(dn)
    gz(dn, 1, 3, 2)
    for h in range(2):
        merge_end(first_in, second_in, out_slots, h)

        def resid_tile(i, h=h):
            v = own(x, h, i)[...] + merged(h, i)
            own(out, h, i)[...] = v
            sixteen(two_rows(b, h), i)[...] = (v * rms(v) * gain_two).astype(BF16)

        loop(tiles16, resid_tile)
        share(two_rows, two_slots, h)
        if h == 0:
            gr(up, 2)
    share_relay(two_rows, two_slots, 0)
    gr(dn, 1)
    share_relay(two_rows, two_slots, 1)
    gather_wait(hi)
    gather_wait(up)

    for h in range(2):
        share_end(two_rows, two_slots, h)
        span = pl.ds(h * half, half)
        for j in range(hid // 256):
            left = slice(j * 256, j * 256 + 256)
            right = slice(hid + j * 256, hid + j * 256 + 256)
            pre[:, 0:256] = dot_nn(norm_two[span, :], w_hu[:, left])
            pre[:, 256:512] = dot_nn(norm_two[span, :], w_hu[:, right])

            def tile(i, h=h, j=j):
                rows_t = at(i * STEP, STEP, STEP)
                flat_t = at(h * half + i * STEP, STEP, STEP)
                for g in range(2):
                    first = slice(j * 256 + g * LANES, j * 256 + (g + 1) * LANES)
                    second = slice(hid + j * 256 + g * LANES, hid + j * 256 + (g + 1) * LANES)
                    act, slope = gelu_parts(pre[rows_t, g * LANES : (g + 1) * LANES])
                    upward = pre[rows_t, 256 + g * LANES : 256 + (g + 1) * LANES]
                    prod[flat_t, first] = (act * upward).astype(BF16)
                    ghu[flat_t, first] = (upward * slope).astype(BF16)
                    ghu[flat_t, second] = act.astype(BF16)

            loop(half // STEP, tile)
        if h == 0:
            gr(dn, 3)
    gr(dn, 2)
    for h in range(2):
        share_end(gout_rows, gout_slots, h)
    gather_wait(dn)

    net.flush()
    for h in range(2):
        span = pl.ds(h * half, half)
        for j in range(hid // 256):
            left = slice(j * 256, j * 256 + 256)
            right = slice(hid + j * 256, hid + j * 256 + 256)
            back = dot_nt(gout[span, :], w_d[left, :])
            ghu[span, left] = (back * ghu[span, left].astype(F32)).astype(BF16)
            ghu[span, right] = (back * ghu[span, right].astype(F32)).astype(BF16)
        for j in range(2):
            cols = slice(j * width // 2, (j + 1) * width // 2)
            part[span, cols] = dot_nt(ghu[span, :], w_hu[cols, :]).astype(BF16)
        merge(part_rows, first_in, gnt_slots, h)
    for h in range(2):
        merge_relay(part_rows, first_in, second_in, gnt_slots, h, tiles16, sixteen)

    for j in range(2):
        def grad_hu(i, j=j):
            cols = at(i * 256, 256, LANES)
            side = slice(j * hid, (j + 1) * hid)
            w_hu[at(i * 256, 256, 16), side] = dot_tn(norm_two[:, cols], ghu[:, side]).astype(BF16)

        loop(width // 256, grad_hu)
        sp(up if j else hi, 1, 3, 2, 0) if j == 0 else sp(up, 1, 3)

    for h in range(2):
        merge_end(first_in, second_in, gnt_slots, h)

        def second_norm(i, h=h):
            back = norm_grad(1, own(out, h, i)[...], merged(h, i), gain_two)
            total = own(cot, h, i)[...] + back
            own(gin, h, i)[...] = total
            sixteen(gres_rows(b, h), i)[...] = total.astype(BF16)

        loop(tiles16, second_norm)
        share(gres_rows, gres_slots, h)
        if h == 0:
            se(hi, 1, 3)
    net.flush("part")
    for h in range(2):
        span = pl.ds(h * half, half)
        part[span, :] = dot_nn(prod[span, :], w_d[...]).astype(BF16)
    share_relay(gres_rows, gres_slots, 0)
    for j in range(2):
        cols = slice(j * hid // 2, (j + 1) * hid // 2)
        w_d[cols, :] = dot_tn(prod[:, cols], gout[...]).astype(BF16)
    se(hi, 2, 0)
    share_relay(gres_rows, gres_slots, 1)

    for h in range(2):
        share_end(gres_rows, gres_slots, h)
        block = slice(h * GROUP, (h + 1) * GROUP)
        got = dot_nt(gres[pl.ds(h * half, half), :], w_o[...])
        tgx[block, 0:here, 0:chans] = got.reshape(GROUP, here, chans)

        def mix_back(q, start, lanes, g):
            span = pl.ds(start, STEP)
            act, slope = gelu_parts(gate_pre[q, span, lanes])
            back = tgx[q, span, lanes]
            states = stx[q, pl.ds(EDGE + start, STEP), lanes]
            ggb[flat(q, start), lanes] = (back * states * slope).astype(BF16)
            tgx[q, span, lanes] = back * act

        over(h, mix_back)

    def ends_back(i, state):
        p = here - 1 - i
        mult = carry[:, p, :]
        return (state[0] * mult, mult * (tgx[:, p, 0:chans] + state[1]))

    product, tail = lax.fori_loop(0, here, ends_back, begin, unroll=8)
    pre_b[s, 0:rows] = product
    pre_b[s, rows : 2 * rows] = tail
    for k in range(1, RING):
        net.put(pre_b.at[s], pre_b.at[s], (ring_to[k], b), back_slots[k])
    sp(up, 2, 0)
    sp(dn, 1, 3)

    for h in range(2):
        merge(part_rows, first_in, down_slots, h)

    w_o[...] = dot_tn(mix[...], gres[...]).astype(BF16)
    for h in range(2):
        merge_relay(part_rows, first_in, second_in, down_slots, h, tiles16, sixteen)
    se(up, 1, 3)

    for k in range(1, RING):
        net.got(pre_b.at[ring_from[k]], (ring_from[k], b), back_slots[k])
    state = jnp.zeros((rows, chans), F32)
    for q in range(RING - 1, 0, -1):
        state = jnp.where(q > s, pre_b[q, rows : 2 * rows] + pre_b[q, 0:rows] * state, state)

    def scan_back(i, state):
        p = here - 1 - i
        total = tgx[:, p, 0:chans] + state
        tgx[:, p, 0:chans] = total
        return carry[:, p, :] * total

    lax.fori_loop(0, here, scan_back, state, unroll=8)

    thru_cols = lambda q, h: ghu.at[pl.ds(h * half, half), at(q * chans, chans, LANES)]
    thru_first = lambda h, slot: prod.at[pl.ds(h * half, half), pl.ds(slot * chans, chans)]
    thru_second = lambda h: gout.at[pl.ds(h * half, half), pl.ds(0, chans)]
    for h in range(2):
        def gates_back(q, start, lanes, g):
            span = pl.ds(start, STEP)
            total = tgx[q, span, lanes]
            rg, ig, co = (rgate[q, span, lanes], igate[q, span, lanes], conv_out[q, span, lanes])
            before = stx[q, pl.ds(EDGE + start - 1, STEP), lanes]
            rate = vec[7:8, lanes]
            decay = jnp.exp(rg * rate)
            scale = jnp.sqrt(1.0 - decay * decay + FLOOR_TERM)
            grad_decay = total * before * same(q, start, 1) - total * ig * co * decay / scale
            grad_log = grad_decay * decay
            grad_rg = grad_log * rate * rg * (1.0 - rg)
            scaled = total * scale
            grad_ig = scaled * co * ig * (1.0 - ig)
            tgx[q, span, lanes] = scaled * ig
            gri[flat(q, start), lanes] = grad_rg.astype(BF16)
            gri[flat(q, start), slice(chans + g * LANES, chans + (g + 1) * LANES)] = grad_ig.astype(BF16)
            add_to(5, lanes, grad_rg)
            add_to(6, lanes, grad_ig)
            add_to(7, lanes, grad_log * (-DECAY_SCALE * rg))

        over(h, gates_back)
        span = pl.ds(h * half, half)
        for j in range(2):
            pair = slice(2 * j, 2 * j + 2)
            got = dot_nt(gri[span, :], w_ri[pair].reshape(2 * chans, two))
            ghu[span, 2 * j * chans : 2 * (j + 1) * chans] = got.astype(BF16)
        if h:
            for k in range(2):
                merge_end(first_in, second_in, down_slots, k)

                def out_tile(i, k=k):
                    own(out, k, i)[...] = own(out, k, i)[...] + merged(k, i)

                loop(tiles16, out_tile)
        merge(thru_cols, thru_first, thru_slots, h)
        if h == 0:
            se(up, 2, 0)
            sp(dn, 2, 0)
    leave_out = fetch(0, out, out_hbm)
    for h in range(2):
        merge_relay(thru_cols, thru_first, thru_second, thru_slots, h, half // 16, sixteen)

    def grad_ri(i):
        got = dot_tn(conv[:, at(i * chans, chans, LANES)], gri[...])
        w_ri[i] = got.astype(BF16).reshape(RING, cblk, two)

    loop(GROUP, grad_ri)
    se(dn, 1, 3)
    sp(ri, 1)
    se(dn, 2, 0)

    for h in range(2):
        merge_end(thru_first, thru_second, thru_slots, h)

        def conv_grad(q, start, lanes, g, h=h):
            span = flat(q, start)
            total = ghu[span, at(b * chans + g * LANES, LANES, LANES)].astype(F32)
            total = total + prod[span, lanes].astype(F32) + gout[span, lanes].astype(F32)
            tgx[q, pl.ds(start, STEP), lanes] += total

        over(h, conv_grad)

    def halo_in():
        return pltpu.make_async_remote_copy(
            src_ref=tgx.at[:, pl.ds(0, EDGE)],
            dst_ref=tgx.at[:, pl.ds(here, EDGE)],
            send_sem=net.send.at[halo_back],
            recv_sem=net.recv.at[halo_back],
            device_id=(ring_from[1], b),
            device_id_type=MESH,
        )

    @pl.when(s > 0)
    def _():
        halo_in().start()

    sp(ri, 3, 2, 0)
    sp(wo, 1, 3, 2, 0)

    @pl.when(s < RING - 1)
    def _():
        net.got(tgx.at[:, pl.ds(here, EDGE)], (ring_to[1], b), halo_back)

    net.flush("part")
    for h in range(2):
        def conv_back(q, start, lanes, g):
            now = tgx[q, pl.ds(start, STEP), lanes]
            ids = tgx[q, pl.ds(start, STEP), marks]
            total = vec[0:1, lanes] * now
            add_to(4, lanes, now)
            add_to(0, lanes, now * brx[q, pl.ds(EDGE + start, STEP), lanes])
            for k in range(1, 4):
                later = pl.ds(start + k, STEP)
                match = (tgx[q, later, marks] == ids).astype(F32)
                total = total + vec[k : k + 1, lanes] * tgx[q, later, lanes] * match
                lag = brx[q, pl.ds(EDGE + start - k, STEP), lanes]
                add_to(k, lanes, now * lag * same(q, start, k))
            ggb[flat(q, start), slice(chans + g * LANES, chans + (g + 1) * LANES)] = total.astype(BF16)

        over(h, conv_back)
        span = pl.ds(h * half, half)
        for j in range(2):
            cols = slice(j * width // 2, (j + 1) * width // 2)
            part[span, cols] = dot_nt(ggb[span, :], w_one[cols, :]).astype(BF16)
        merge(part_rows, first_in, gn_slots, h)
    for h in range(2):
        merge_relay(part_rows, first_in, second_in, gn_slots, h, tiles16, sixteen)

    def grad_one(i):
        cols = at(i * 256, 256, LANES)
        w_one[at(i * 256, 256, 16), :] = dot_tn(norm[:, cols], ggb[...]).astype(BF16)

    loop(width // 256, grad_one)
    sp(one, 1, 3, 2, 0)
    se(ri, 1, 3)

    for h in range(2):
        merge_end(first_in, second_in, gn_slots, h)

        def first_norm(i, h=h):
            back = norm_grad(0, own(x, h, i)[...], merged(h, i), gain_one)
            own(gin, h, i)[...] = own(gin, h, i)[...] + back

        loop(tiles16, first_norm)
        if h == 0:
            se(ri, 2, 0)
    leave_gin = fetch(1, gin, gin_hbm)

    for k in range(8):
        total = jnp.sum(acc[k], axis=0, keepdims=True)
        vs[s, k : k + 1, 0:chans] = total * vec[8:9, :] if k == 7 else total
    piece = width // 4
    for k in range(2):
        total = jnp.sum(gain_acc[k], axis=0, keepdims=True)
        for j in range(4):
            vs[s, 4 * k + j : 4 * k + j + 1, chans : chans + piece] = total[:, j * piece : (j + 1) * piece]
    for k in range(1, RING):
        net.put(vs.at[s], vs.at[s], (ring_to[k], b), vec_slots[k])

    def keep_down(i, total):
        g_d[at(i * 16, 16, 16), :] = total

    def keep_out(i, total):
        g_o[at(i * 16, 16, 16), :] = total

    sum_end_spread(hi)
    sum_end_spread(up)
    se(wo, 1, 3, 2, 0)
    sum_end(dn, keep_down)
    se(one, 1, 3, 2, 0)
    sum_end_spread(ri)
    sum_end(wo, keep_out)
    for k in range(1, RING):
        net.got(vs.at[ring_from[k]], (ring_from[k], b), vec_slots[k])
    total = vs[0]
    for q in range(1, RING):
        total = total + vs[q]
    vb[b] = total
    for (peer, to), slot in zip(group_peers, last_slots):
        net.put(vb.at[b], vb.at[b], to, slot)
    sum_end_spread(one)
    for (peer, to), slot in zip(group_peers, last_slots):
        net.got(vb.at[peer], to, slot)
    g_vec[:, 0:chans] = total[:, 0:chans]
    summed = vb[0, :, chans : chans + piece]
    for q in range(1, GROUP):
        summed = summed + vb[q, :, chans : chans + piece]
    g_vec[:, chans : chans + piece] = summed
    for c in (hi, up, ri, one):
        home_wait(c)
    net.flush()
    leave_out.wait()
    leave_gin.wait()

    @pl.when(s < RING - 1)
    def _():
        halo_out().wait_send()

    @pl.when(s > 0)
    def _():
        halo_in().wait_send()


def finish(names, *refs):
    r = dict(zip(names, refs))
    r["to_o"][...] = r["g_o"][...]
    r["to_d"][...] = r["g_d"][...]
    place = lax.axis_index("seq") * GROUP + lax.axis_index("batch")
    s = lax.axis_index("seq")
    blk, cblk, fblk = (r["to_gate"].shape[0], r["to_recur"].shape[0], r["to_d"].shape[0])
    chans, hid = (RING * cblk, RING * fblk)
    rec = blk + cblk

    def joined(pieces, parts):
        pieces = [piece.astype(F32) for piece in pieces]
        return jnp.concatenate(
            [pieces[q][:, k * parts : (k + 1) * parts] for k in range(RING) for q in range(GROUP)], axis=1
        )

    fin, fin_hu, g_vec = (r["fin"], r["fin_hu"], r["g_vec"])
    for name, first, tall, left in (
        ("to_gate", 0, blk, 0),
        ("to_input", 0, blk, chans),
        ("to_recur", blk, cblk, 0),
        ("to_inject", blk, cblk, chans),
    ):
        spans = [slice(q * rec + first, q * rec + first + tall) for q in range(GROUP)]
        r[name][...] = joined([fin[span, left : left + chans] for span in spans], cblk)
    for name, left in (("to_hidden", 0), ("to_upward", hid)):
        spans = [slice(q * blk, (q + 1) * blk) for q in range(GROUP)]
        r[name][...] = joined([fin_hu[span, left : left + hid] for span in spans], fblk)
    vectors = g_vec[:, 0:chans]
    mine = vectors[:, 0:cblk]
    for k in range(1, RING):
        mine = jnp.where(k == s, vectors[:, k * cblk : (k + 1) * cblk], mine)
    r["to_taps"][...] = mine[0:4]
    for k, name in enumerate(("to_cbias", "to_rbias", "to_ibias", "to_decay")):
        r[name][...] = mine[4 + k]
    piece = g_vec.shape[1] - chans
    for k, name in enumerate(("to_gain_one", "to_gain_two")):
        total = jnp.zeros((1, blk), F32)
        for j in range(4):
            for m in range(piece // blk):
                part = g_vec[4 * k + j : 4 * k + j + 1, chans + m * blk : chans + (m + 1) * blk]
                total = jnp.where(j * (piece // blk) + m == place, part, total)
        r[name][...] = total[0]


def split_block(
    inputs,
    segments,
    w_gate,
    w_input,
    w_recur,
    w_inject,
    w_output,
    w_hidden,
    w_upward,
    w_down,
    gain_one,
    gain_two,
    conv_taps,
    conv_bias,
    recur_bias,
    inject_bias,
    decay_param,
    cotangent,
):
    count, here, width = inputs.shape
    channels = w_gate.shape[1]
    chans, hid = (channels // GROUP, w_hidden.shape[1] // GROUP)
    blk, cblk, fblk = (w_gate.shape[0], w_recur.shape[0], w_down.shape[0])
    tokens = GROUP * count * here
    rows = GROUP * count
    wide = chans + LANES
    size_one = GROUP * blk
    operands = {
        "hbm_x": inputs.reshape(count * here, width),
        "hbm_cot": cotangent.reshape(count * here, width),
        "hbm_seg": segments,
        "hbm_w_gate": w_gate,
        "hbm_w_input": w_input,
        "hbm_w_recur": w_recur,
        "hbm_w_inject": w_inject,
        "hbm_w_output": w_output,
        "hbm_w_hidden": w_hidden,
        "hbm_w_upward": w_upward,
        "hbm_w_down": w_down,
        "hbm_gain_one": gain_one,
        "hbm_gain_two": gain_two,
        "hbm_conv_taps": conv_taps,
        "hbm_conv_bias": conv_bias,
        "hbm_recur_bias": recur_bias,
        "hbm_inject_bias": inject_bias,
        "hbm_decay_param": decay_param,
    }
    piece = width // 4
    outputs = {
        "out": ((count * here, width), F32),
        "gin": ((count * here, width), F32),
        "fin": ((GROUP * (blk + cblk), 2 * chans), BF16),
        "fin_hu": ((GROUP * blk, 2 * hid), BF16),
        "g_o": ((cblk, width), F32),
        "g_d": ((fblk, width), F32),
        "g_vec": ((8, chans + piece), F32),
    }
    scratch = {
        "x": ((count * here, width), F32),
        "cot": ((count * here, width), F32),
        "out_own": ((count * here, width), F32),
        "gin_own": ((count * here, width), F32),
        "seg": (segments.shape, jnp.int32),
        "gains": ((2, width), F32),
        "taps": (conv_taps.shape, F32),
        "biases": ((4, channels), F32),
        "vecs": ((GROUP, 16, chans), F32),
        "vec": ((16, chans), F32),
        "w_one": ((width, 2 * chans), BF16),
        "w_ri": ((GROUP, RING, cblk, 2 * chans), BF16),
        "w_o": ((chans, width), BF16),
        "w_hu": ((width, 2 * hid), BF16),
        "w_d": ((hid, width), BF16),
        "norm": ((tokens, width + LANES), BF16),
        "gout": ((tokens, width), BF16),
        "norm_two": ((tokens, width), BF16),
        "gres": ((tokens, width), BF16),
        "conv": ((tokens, channels), BF16),
        "mix": ((tokens, chans), BF16),
        "prod": ((tokens, hid), BF16),
        "ghu": ((tokens, 2 * hid), BF16),
        "ggb": ((tokens, 2 * chans), BF16),
        "gri": ((tokens, 2 * chans), BF16),
        "part": ((tokens, width), BF16),
        "brx": ((rows, EDGE + here, wide), F32),
        "tgx": ((rows, here + EDGE, wide), F32),
        "stx": ((rows, EDGE + here, chans), F32),
        "gate_pre": ((rows, here, chans), F32),
        "conv_out": ((rows, here, chans), F32),
        "rgate": ((rows, here, chans), F32),
        "igate": ((rows, here, chans), F32),
        "carry": ((rows, here, chans), F32),
        "pre": ((GROUP * here, 512), F32),
        "core_in": ((2, 2, here, width), BF16),
        "x_in": ((2, here, width), BF16),
        "pre_f": ((RING, 2 * rows, chans), F32),
        "pre_b": ((RING, 2 * rows, chans), F32),
        "y_ri": ((DEPTH, GROUP, cblk, 2 * chans), BF16),
        "z_ri": ((DEPTH - 1, GROUP, cblk, 2 * chans), BF16),
        "y_o": ((DEPTH * cblk, width), BF16),
        "z_o": (((DEPTH - 1) * cblk, width), BF16),
        "y_h": ((DEPTH * size_one, hid), BF16),
        "z_h": (((DEPTH - 1) * size_one, hid), BF16),
        "y_u": ((DEPTH * size_one, hid), BF16),
        "z_u": (((DEPTH - 1) * size_one, hid), BF16),
        "y_d": ((DEPTH * fblk, width), BF16),
        "z_d": (((DEPTH - 1) * fblk, width), BF16),
        "acc": ((8, 8, chans), F32),
        "gain_acc": ((2, 8, width), F32),
        "vs": ((RING, 8, chans + piece), F32),
        "vb": ((GROUP, 8, chans + piece), F32),
    }
    names = [*operands, *outputs, *scratch, "send", "recv", "local"]
    in_vmem = pl.BlockSpec(memory_space=pltpu.VMEM)
    in_hbm = pl.BlockSpec(memory_space=pl.ANY)
    shapes = lambda specs: [jax.ShapeDtypeStruct(shape, kind) for shape, kind in specs.values()]
    got = pl.pallas_call(
        functools.partial(fused, names),
        out_shape=shapes(outputs),
        in_specs=[in_hbm] * len(operands),
        out_specs=[in_hbm] * 2 + [in_vmem] * (len(outputs) - 2),
        scratch_shapes=[pltpu.VMEM(shape, kind) for shape, kind in scratch.values()]
        + [pltpu.SemaphoreType.DMA((SLOTS,))] * 2
        + [pltpu.SemaphoreType.DMA((20,))],
        compiler_params=pltpu.CompilerParams(
            collective_id=0, has_side_effects=True, vmem_limit_bytes=VMEM_BYTES
        ),
        name="block",
    )(*operands.values())
    finals = {
        "to_gate": ((blk, channels), F32),
        "to_input": ((blk, channels), F32),
        "to_recur": ((cblk, channels), F32),
        "to_inject": ((cblk, channels), F32),
        "to_o": ((cblk, width), F32),
        "to_hidden": ((blk, GROUP * hid), F32),
        "to_upward": ((blk, GROUP * hid), F32),
        "to_d": ((fblk, width), F32),
        "to_gain_one": ((blk,), F32),
        "to_gain_two": ((blk,), F32),
        "to_taps": ((4, cblk), F32),
        "to_cbias": ((cblk,), F32),
        "to_rbias": ((cblk,), F32),
        "to_ibias": ((cblk,), F32),
        "to_decay": ((cblk,), F32),
    }
    done = pl.pallas_call(
        functools.partial(finish, [*list(outputs)[2:], *finals]),
        out_shape=shapes(finals),
        in_specs=[in_vmem] * (len(outputs) - 2),
        out_specs=[in_vmem] * len(finals),
        name="finish",
    )(*got[2:])
    return (
        got[0].reshape(count, here, width),
        got[1].reshape(count, here, width),
        *done,
    )


def solution(mesh):
    fits = dict(mesh.shape) == {"seq": RING, "batch": GROUP}
    return jax.shard_map(
        split_block if fits else gathered_block,
        mesh=mesh,
        in_specs=(
            P("batch", "seq", None),
            P("batch", "seq"),
            P(("seq", "batch"), None),
            P(("seq", "batch"), None),
            P(("seq", "batch"), None),
            P(("seq", "batch"), None),
            P(("seq", "batch"), None),
            P(("seq", "batch"), None),
            P(("seq", "batch"), None),
            P(("seq", "batch"), None),
            P(),
            P(),
            P(),
            P(),
            P(),
            P(),
            P(),
            P("batch", "seq", None),
        ),
        out_specs=(
            P("batch", "seq", None),
            P("batch", "seq", None),
            P(("seq", "batch"), None),
            P(("seq", "batch"), None),
            P(("seq", "batch"), None),
            P(("seq", "batch"), None),
            P(("seq", "batch"), None),
            P(("seq", "batch"), None),
            P(("seq", "batch"), None),
            P(("seq", "batch"), None),
            P(("seq", "batch")),
            P(("seq", "batch")),
            P(None, ("seq", "batch")),
            P(("seq", "batch")),
            P(("seq", "batch")),
            P(("seq", "batch")),
            P(("seq", "batch")),
        ),
        check_vma=False,
    )
```

```python
import functools

import jax
import jax.numpy as jnp
from jax import lax
from jax.experimental import pallas as pl
from jax.experimental.pallas import tpu as pltpu
from jax.sharding import PartitionSpec as P

EPSILON = 1e-06
DECAY_SCALE = 8.0
FLOOR_TERM = 0.01
SLOTS = 360
VMEM_BYTES = 63 << 20


def shifted(array, axis, by):
    peers = lax.axis_size(axis)
    pairs = [(i, i + by) for i in range(peers) if 0 <= i + by < peers]
    return lax.ppermute(array, axis, pairs)


def prefix(value, axis, join, neutral, backward):
    count, mine = (lax.axis_size(axis), lax.axis_index(axis))
    pieces = jax.tree.map(lambda part: lax.all_gather(part, axis), value)
    if backward:
        pieces = jax.tree.map(lambda part: part[::-1], pieces)
        mine = count - 1 - mine
    so_far = jax.tree.map(
        lambda part, zero: jnp.full_like(part, 0) + jnp.asarray(zero, part.dtype), value, neutral
    )

    def turn(position, so_far):
        longer = join(so_far, jax.tree.map(lambda part: part[position], pieces))
        return jax.tree.map(lambda new, old: jnp.where(position < mine, new, old), longer, so_far)

    return lax.fori_loop(0, count - 1, turn, so_far)


def shortened(array):
    return jax.tree.map(lambda a: a.astype(jnp.bfloat16) if a.dtype == jnp.float32 else a, array)


def combine(earlier, later):
    return (earlier[0] * later[0], later[1] + later[0] * earlier[1])


def matmul_plain(left, right):
    return jnp.dot(left, right, preferred_element_type=jnp.float32)


def matmul_tleft(left, right):
    return jnp.einsum("ta,tb->ab", left, right, preferred_element_type=jnp.float32)


def matmul_tright(left, right):
    return jnp.einsum("ta,ba->tb", left, right, preferred_element_type=jnp.float32)


def norm_forward(values, gain):
    scaler = lax.rsqrt(jnp.mean(values * values, axis=-1, keepdims=True) + EPSILON)
    return (values * scaler * gain, scaler)


def norm_back(values, scaler, gain, incoming):
    scaled = incoming * gain
    grad_gain = jnp.sum(incoming * values * scaler, axis=0)
    inner = jnp.mean(scaled * values, axis=-1, keepdims=True)
    return (scaler * (scaled - values * scaler * scaler * inner), grad_gain)


def gathered_block(
    inputs,
    segments,
    w_gate,
    w_input,
    w_recur,
    w_inject,
    w_output,
    w_hidden,
    w_upward,
    w_down,
    gain_one,
    gain_two,
    conv_taps,
    conv_bias,
    recur_bias,
    inject_bias,
    decay_param,
    cotangent,
):
    row_count, positions, features = inputs.shape
    (
        gate_full,
        input_full,
        recur_full,
        inject_full,
        output_full,
        hidden_full,
        upward_full,
        down_full,
    ) = (
        lax.all_gather(w_gate, ("seq", "batch"), axis=0, tiled=True),
        lax.all_gather(w_input, ("seq", "batch"), axis=0, tiled=True),
        lax.all_gather(w_recur, ("seq", "batch"), axis=0, tiled=True),
        lax.all_gather(w_inject, ("seq", "batch"), axis=0, tiled=True),
        lax.all_gather(w_output, ("seq", "batch"), axis=0, tiled=True),
        lax.all_gather(w_hidden, ("seq", "batch"), axis=0, tiled=True),
        lax.all_gather(w_upward, ("seq", "batch"), axis=0, tiled=True),
        lax.all_gather(w_down, ("seq", "batch"), axis=0, tiled=True),
    )
    channels = gate_full.shape[1]
    tokens_here = row_count * positions
    flat_in = inputs.reshape(tokens_here, features)
    normed, scale_one = norm_forward(flat_in, gain_one)
    normed_low = normed.astype(jnp.bfloat16)
    gate_pre = matmul_plain(normed_low, gate_full)
    gate_act, gate_pull = jax.vjp(jax.nn.gelu, gate_pre)
    branch = matmul_plain(normed_low, input_full).reshape(row_count, positions, channels)
    seg_marks = segments.astype(jnp.float32) + 1.0
    prior_branch, prior_marks = shifted(
        (branch[:, positions - 3 :], seg_marks[:, positions - 3 :]), "seq", 1
    )
    ext_branch = jnp.concatenate([prior_branch, branch], axis=1)
    ext_marks = jnp.concatenate([prior_marks, seg_marks], axis=1)
    sames = []
    lagged = []
    for offset in range(4):
        sames.append(
            (ext_marks[:, 3 - offset : 3 - offset + positions] == seg_marks).astype(jnp.float32)[
                :, :, None
            ]
        )
        lagged.append(ext_branch[:, 3 - offset : 3 - offset + positions])
    conv_out = conv_bias + conv_taps[0] * branch
    for offset in range(1, 4):
        conv_out = conv_out + conv_taps[offset] * lagged[offset] * sames[offset]
    conv_low = conv_out.reshape(tokens_here, channels).astype(jnp.bfloat16)
    recur_gate = jax.nn.sigmoid(matmul_plain(conv_low, recur_full) + recur_bias).reshape(
        row_count, positions, channels
    )
    inject_gate = jax.nn.sigmoid(matmul_plain(conv_low, inject_full) + inject_bias).reshape(
        row_count, positions, channels
    )
    base_rate = jax.nn.softplus(decay_param)
    decays = jnp.exp(-DECAY_SCALE * recur_gate * base_rate)
    carry_mult = decays * sames[1]
    normalizer = jnp.sqrt(1.0 - decays * decays + FLOOR_TERM)
    injected = normalizer * inject_gate * conv_out
    cumul, local_state = lax.associative_scan(combine, (carry_mult, injected), axis=1)
    ones_rows = jnp.ones((row_count, channels), jnp.float32)
    zeros_rows = jnp.zeros((row_count, channels), jnp.float32)
    entry = prefix(
        (cumul[:, -1], local_state[:, -1]), "seq", combine, (ones_rows, zeros_rows), False
    )[1]
    states = local_state + cumul * entry[:, None]
    states_before = jnp.concatenate([entry[:, None], states[:, :-1]], axis=1)
    states_flat = states.reshape(tokens_here, channels)
    mixed = (states_flat * gate_act).astype(jnp.bfloat16)
    resid = flat_in + matmul_plain(mixed, output_full)
    normed_two, scale_two = norm_forward(resid, gain_two)
    normed_two_low = normed_two.astype(jnp.bfloat16)
    hidden_pre = matmul_plain(normed_two_low, hidden_full)
    upward_pre = matmul_plain(normed_two_low, upward_full)
    hidden_act, hidden_pull = jax.vjp(jax.nn.gelu, hidden_pre)
    product = (hidden_act * upward_pre).astype(jnp.bfloat16)
    output = resid + matmul_plain(product, down_full)
    grad_out = cotangent.reshape(tokens_here, features)
    grad_out_low = grad_out.astype(jnp.bfloat16)
    grad_down = matmul_tleft(product, grad_out_low)
    grad_product = matmul_tright(grad_out_low, down_full)
    grad_hidden_pre = hidden_pull(grad_product * upward_pre)[0].astype(jnp.bfloat16)
    grad_upward_pre = (grad_product * hidden_act).astype(jnp.bfloat16)
    grad_hidden = matmul_tleft(normed_two_low, grad_hidden_pre)
    grad_upward = matmul_tleft(normed_two_low, grad_upward_pre)
    grad_normed_two = matmul_tright(grad_hidden_pre, hidden_full) + matmul_tright(
        grad_upward_pre, upward_full
    )
    grad_resid_norm, grad_gain_two = norm_back(resid, scale_two, gain_two, grad_normed_two)
    grad_resid = grad_out + grad_resid_norm
    grad_resid_low = grad_resid.astype(jnp.bfloat16)
    grad_output = matmul_tleft(mixed, grad_resid_low)
    grad_mixed = matmul_tright(grad_resid_low, output_full)
    grad_gate_pre = gate_pull(grad_mixed * states_flat)[0].astype(jnp.bfloat16)
    grad_states = (grad_mixed * gate_act).reshape(row_count, positions, channels)
    next_mult = jnp.concatenate([carry_mult[:, 1:], jnp.ones_like(carry_mult[:, :1])], axis=1)
    tail_prod, local_grad = lax.associative_scan(
        combine, (next_mult, grad_states), axis=1, reverse=True
    )
    incoming = prefix(
        (cumul[:, -1], carry_mult[:, 0] * local_grad[:, 0]),
        "seq",
        combine,
        (ones_rows, zeros_rows),
        True,
    )[1]
    total_grad = local_grad + tail_prod * incoming[:, None]
    grad_decays = (
        total_grad * states_before * sames[1]
        - total_grad * inject_gate * conv_out * decays / normalizer
    )
    grad_log = grad_decays * decays
    grad_recur_pre = grad_log * (-DECAY_SCALE * base_rate) * recur_gate * (1.0 - recur_gate)
    grad_decay_param = jnp.sum(
        grad_log * (-DECAY_SCALE * recur_gate), axis=(0, 1)
    ) * jax.nn.sigmoid(decay_param)
    grad_inject_pre = total_grad * normalizer * conv_out * inject_gate * (1.0 - inject_gate)
    grad_recur_bias = jnp.sum(grad_recur_pre, axis=(0, 1))
    grad_inject_bias = jnp.sum(grad_inject_pre, axis=(0, 1))
    grad_recur_low = grad_recur_pre.reshape(tokens_here, channels).astype(jnp.bfloat16)
    grad_inject_low = grad_inject_pre.reshape(tokens_here, channels).astype(jnp.bfloat16)
    grad_recur = matmul_tleft(conv_low, grad_recur_low)
    grad_inject = matmul_tleft(conv_low, grad_inject_low)
    through_gates = matmul_tright(grad_recur_low, recur_full) + matmul_tright(
        grad_inject_low, inject_full
    )
    grad_conv = total_grad * normalizer * inject_gate + through_gates.reshape(
        row_count, positions, channels
    )
    grad_conv_bias = jnp.sum(grad_conv, axis=(0, 1))
    taps_by_channel = jnp.stack(
        [jnp.sum(grad_conv * lagged[offset] * sames[offset], axis=(0, 1)) for offset in range(4)],
        axis=1,
    )
    later_grad, later_marks = (
        shifted(shortened(grad_conv[:, :3]), "seq", -1),
        shifted(seg_marks[:, :3].astype(jnp.bfloat16), "seq", -1).astype(jnp.float32),
    )
    ext_grad = jnp.concatenate([grad_conv, later_grad], axis=1)
    ext_after = jnp.concatenate([seg_marks, later_marks], axis=1)
    grad_branch = conv_taps[0] * grad_conv
    for offset in range(1, 4):
        match = (ext_after[:, offset : offset + positions] == seg_marks).astype(jnp.float32)[
            :, :, None
        ]
        grad_branch = (
            grad_branch + conv_taps[offset] * ext_grad[:, offset : offset + positions] * match
        )
    grad_branch_low = grad_branch.reshape(tokens_here, channels).astype(jnp.bfloat16)
    grad_input = matmul_tleft(normed_low, grad_branch_low)
    grad_gate = matmul_tleft(normed_low, grad_gate_pre)
    grad_normed = matmul_tright(grad_gate_pre, gate_full) + matmul_tright(
        grad_branch_low, input_full
    )
    grad_first_norm, grad_gain_one = norm_back(flat_in, scale_one, gain_one, grad_normed)
    grad_inputs = (grad_resid + grad_first_norm).reshape(row_count, positions, features)
    every = (
        lax.psum_scatter(grad_gate, ("seq", "batch"), scatter_dimension=0, tiled=True),
        lax.psum_scatter(grad_input, ("seq", "batch"), scatter_dimension=0, tiled=True),
        lax.psum_scatter(grad_recur, ("seq", "batch"), scatter_dimension=0, tiled=True),
        lax.psum_scatter(grad_inject, ("seq", "batch"), scatter_dimension=0, tiled=True),
        lax.psum_scatter(grad_output, ("seq", "batch"), scatter_dimension=0, tiled=True),
        lax.psum_scatter(grad_hidden, ("seq", "batch"), scatter_dimension=0, tiled=True),
        lax.psum_scatter(grad_upward, ("seq", "batch"), scatter_dimension=0, tiled=True),
        lax.psum_scatter(grad_down, ("seq", "batch"), scatter_dimension=0, tiled=True),
        lax.psum_scatter(grad_gain_one, ("seq", "batch"), scatter_dimension=0, tiled=True),
        lax.psum_scatter(grad_gain_two, ("seq", "batch"), scatter_dimension=0, tiled=True),
        lax.psum_scatter(taps_by_channel, ("seq", "batch"), scatter_dimension=0, tiled=True),
        lax.psum_scatter(grad_conv_bias, ("seq", "batch"), scatter_dimension=0, tiled=True),
        lax.psum_scatter(grad_recur_bias, ("seq", "batch"), scatter_dimension=0, tiled=True),
        lax.psum_scatter(grad_inject_bias, ("seq", "batch"), scatter_dimension=0, tiled=True),
        lax.psum_scatter(grad_decay_param, ("seq", "batch"), scatter_dimension=0, tiled=True),
    )
    summed = (
        every[0],
        every[1],
        every[2],
        every[3],
        every[4],
        every[5],
        every[6],
        every[7],
        every[8],
        every[9],
        every[10].T,
        every[11],
        every[12],
        every[13],
        every[14],
    )
    return (
        output.reshape(row_count, positions, features),
        grad_inputs,
        summed[0],
        summed[1],
        summed[2],
        summed[3],
        summed[4],
        summed[5],
        summed[6],
        summed[7],
        summed[8],
        summed[9],
        summed[10],
        summed[11],
        summed[12],
        summed[13],
        summed[14],
    )


MESH = pl.DeviceIdType.MESH
F32, BF16 = (jnp.float32, jnp.bfloat16)
LANES = 128
EDGE = 8
STEP = 32
GROUP, RING = (4, 8)


def dot_nn(left, right):
    return lax.dot_general(left, right, (((1,), (0,)), ((), ())), preferred_element_type=F32)


def dot_nt(left, right):
    return lax.dot_general(left, right, (((1,), (1,)), ((), ())), preferred_element_type=F32)


def dot_tn(left, right):
    return lax.dot_general(left, right, (((0,), (0,)), ((), ())), preferred_element_type=F32)


def gelu_parts(value):
    rate = 0.7978845608028654
    square = value * value
    bent = jnp.tanh(rate * (value + 0.044715 * square * value))
    act = 0.5 * value * (1.0 + bent)
    slope = 0.5 * (1.0 + bent) + 0.5 * rate * value * (1.0 - bent * bent) * (1.0 + 0.134145 * square)
    return (act, slope)


def at(start, size, of):
    return pl.ds(pl.multiple_of(start, of), size)


def loop(count, body):
    def turn(i, nothing):
        body(i)
        return nothing

    lax.fori_loop(0, count, turn, 0)


class Net:
    def __init__(self, send, recv):
        self.send, self.recv, self.used, self.open = (send, recv, 0, {})

    def slots(self, count):
        first = self.used
        self.used += count
        return list(range(first, first + count))

    def put(self, src, dst, to, slot, tag=""):
        copy = pltpu.make_async_remote_copy(
            src_ref=src,
            dst_ref=dst,
            send_sem=self.send.at[slot],
            recv_sem=self.recv.at[slot],
            device_id=to,
            device_id_type=MESH,
        )
        copy.start()
        self.open.setdefault(tag, []).append(copy)

    def got(self, dst, to, slot):
        pltpu.make_async_remote_copy(
            src_ref=dst,
            dst_ref=dst,
            send_sem=self.send.at[slot],
            recv_sem=self.recv.at[slot],
            device_id=to,
            device_id_type=MESH,
        ).wait_recv()

    def flush(self, *tags):
        for tag in tags or list(self.open):
            for copy in self.open.pop(tag, []):
                copy.wait_send()


def fused(names, *refs):
    r = dict(zip(names, refs))
    out_hbm, gin_hbm, fin, fin_hu, g_o, g_d, g_vec = (
        r[k] for k in ("out", "gin", "fin", "fin_hu", "g_o", "g_d", "g_vec")
    )
    x, cot, out, gin, vec, gains = (r[k] for k in ("x", "cot", "out_own", "cot", "vec", "gains"))
    w_one, w_ri, w_o, w_hu, w_d = (r[k] for k in ("w_one", "w_ri", "w_o", "w_hu", "w_d"))
    norm, gout, norm_two, gres, conv, mix = (
        r[k] for k in ("norm", "gout", "norm_two", "gres", "conv", "mix")
    )
    prod, ghu, ggb, gri, part = (r[k] for k in ("prod", "ghu", "ggb", "gri", "part"))
    brx, tgx, stx, gate_pre, conv_out = (r[k] for k in ("brx", "tgx", "stx", "gate_pre", "conv_out"))
    rgate, igate, carry, pre = (r[k] for k in ("rgate", "igate", "carry", "pre"))
    core_in, x_in, pre_f, pre_b = (r[k] for k in ("core_in", "x_in", "pre_f", "pre_b"))
    acc, gain_acc, vs, vb = (r[k] for k in ("acc", "gain_acc", "vs", "vb"))
    net = Net(r["send"], r["recv"])

    width = x.shape[1]
    here = carry.shape[1]
    chans = carry.shape[2]
    hid = prod.shape[1]
    rows = 2 * GROUP
    half = GROUP * here
    blk, cblk, fblk = (width // (RING * GROUP), chans // RING, hid // RING)
    groups = [slice(g * LANES, (g + 1) * LANES) for g in range(chans // LANES)]
    marks = slice(chans, chans + LANES)

    s, b = (lax.axis_index("seq"), lax.axis_index("batch"))
    mate, across = (b + 1 - 2 * (b % 2), b + 2 - 4 * (b // 2))
    corner = across + 1 - 2 * (b % 2)
    to_mate, to_across, to_corner = ((s, mate), (s, across), (s, corner))
    group_peers = [(mate, to_mate), (across, to_across), (corner, to_corner)]
    flips = {"h": 4 - 8 * (s // 4), "l": 2 - 4 * (s // 2 % 2), "y": 1 - 2 * (s % 2)}

    def turned(axes):
        place = s
        for axis in axes:
            place = place + flips[axis]
        return place

    def reach(axes):
        return (turned(axes), b)

    ring_to = [lax.rem(s + k, RING) for k in range(RING)]
    ring_from = [lax.rem(s + RING - k, RING) for k in range(RING)]

    def ring_device(q):
        return (q, b)

    def fetch(slot, src, dst):
        copy = pltpu.make_async_copy(src, dst, r["local"].at[slot])
        copy.start()
        return copy

    raw = ghu
    sides = (slice(0, raw.shape[1]), slice(raw.shape[1], 2 * raw.shape[1]))
    spots, place = ({}, 0)
    fetched = {}
    for name, tall in (("w_gate", blk), ("w_input", blk), ("w_recur", cblk), ("w_inject", cblk)):
        spots[name] = place
        fetched[name] = [fetch(len(fetched), r["hbm_" + name], raw.at[pl.ds(place, tall)])]
        place += tall
    fetched["x"] = [fetch(4, r["hbm_x"], x)]
    fetched["seg"] = [fetch(5, r["hbm_seg"], r["seg"])]
    for k, name in enumerate(("gain_one", "gain_two")):
        fetched[name] = [fetch(6 + k, r["hbm_" + name], gains.at[k])]
    for k, name in enumerate(("w_hidden", "w_upward")):
        spots[name] = place
        fetched[name] = [
            fetch(8 + 2 * k + j, r["hbm_" + name].at[:, side], raw.at[pl.ds(place + j * blk, blk)])
            for j, side in enumerate(sides)
        ]
        place += 2 * blk
    fetched["own_o"] = [fetch(12, r["hbm_w_output"], w_o.at[at(s * cblk, cblk, 16)])]
    fetched["own_d"] = [fetch(13, r["hbm_w_down"], w_d.at[at(s * fblk, fblk, 16)])]
    fetched["vec"] = [fetch(14, r["hbm_conv_taps"], r["taps"])] + [
        fetch(15 + k, r["hbm_" + name], r["biases"].at[k])
        for k, name in enumerate(("conv_bias", "recur_bias", "inject_bias", "decay_param"))
    ]
    fetched["cot"] = [fetch(19, r["hbm_cot"], cot)]

    def fetch_wait(*which):
        for name in which:
            for copy in fetched[name]:
                copy.wait()

    barrier = pltpu.get_barrier_semaphore()
    for _, to in group_peers:
        pl.semaphore_signal(barrier, inc=1, device_id=to, device_id_type=MESH)
    for k in range(1, RING):
        pl.semaphore_signal(barrier, inc=1, device_id=ring_device(ring_to[k]), device_id_type=MESH)

    class Chunk:
        pass

    def chunk(axes, block, piece, pieces, first_sum, later_sum):
        c = Chunk()
        c.axes, c.back, c.block, c.piece, c.pieces = (axes[:3], axes[-3:], block, piece, pieces)
        c.first_sum, c.later_sum = (first_sum, later_sum)
        c.gather, c.sums = (net.slots(7), net.slots(7))
        c.spread, c.home = (net.slots(3), net.slots(3))
        return c

    def tall_chunk(axes, ref, size, first_ref, later_ref):
        return chunk(
            axes,
            lambda q: ref.at[at(q * size, size, 16)],
            lambda q, i: ref.at[at(q * size + i * 16, 16, 16)],
            size // 16,
            lambda k: first_ref.at[pl.ds(k * size, size)],
            lambda k: later_ref.at[pl.ds(k * size, size)],
        )

    def wide_chunk(axes, ref, cols, first_ref, later_ref):
        return chunk(
            axes,
            lambda q: ref.at[q, :, cols],
            lambda q, i: ref.at[q, at(i * 16, 16, 16), cols],
            GROUP * blk // 16,
            lambda k: first_ref.at[k],
            lambda k: later_ref.at[k],
        )

    class Late:
        def __init__(self, first, cols):
            self.first, self.cols, self.at = (first, cols, self)

        def __getitem__(self, k):
            size = GROUP * blk
            return norm_two.at[pl.ds((self.first + k) * size, size), self.cols]

    tokens = rows * here
    two = 2 * chans
    gate_side, in_side = (slice(0, chans), slice(chans, two))
    gat = wide_chunk("hly", w_one, gate_side, None, None)
    gat_sum = wide_chunk("hly", r["dw_gate"], gate_side, Late(0, gate_side), Late(4, gate_side))
    inp = wide_chunk("hly", w_one, in_side, None, None)
    inp_sum = wide_chunk("hly", r["dw_in"], gate_side, Late(0, in_side), Late(4, in_side))
    ri = chunk(
        "hly hyl",
        lambda q: w_ri.at[:, q],
        lambda q, i: w_ri.at[i, q],
        GROUP,
        lambda k: r["y_ri"].at[k],
        lambda k: r["z_ri"].at[k],
    )
    wo = tall_chunk("hly", w_o, cblk, r["y_o"], r["z_o"])
    hi = wide_chunk("hly", w_hu, slice(0, hid), r["y_h"], r["z_h"])
    up = wide_chunk("hly", w_hu, slice(hid, 2 * hid), r["y_u"], r["z_u"])
    dn = tall_chunk("hyl", w_d, fblk, None, None)
    dn_sum = tall_chunk("hyl", r["dw_d"], fblk, r["y_d"], r["z_d"])

    def cube_place(ref, cols):
        return lambda q: ref.at[s, at(q * blk, blk, 16), cols]

    rec = blk + cblk
    xhu = gri.at[pl.ds(GROUP * rec, 2 * GROUP * blk)]
    gat.source = lambda q: gri.at[at(q * rec, blk, 16), gate_side]
    gat.place = cube_place(w_one, gate_side)
    gat_sum.place = cube_place(r["dw_gate"], gate_side)
    gat_sum.result = lambda q: fin.at[at(q * rec, blk, 16), gate_side]
    inp.source = lambda q: gri.at[at(q * rec, blk, 16), in_side]
    inp.place = cube_place(w_one, in_side)
    inp_sum.place = cube_place(r["dw_in"], gate_side)
    inp_sum.result = lambda q: fin.at[at(q * rec, blk, 16), in_side]
    ri.source = lambda q: gri.at[at(q * rec + blk, cblk, 16)]
    ri.place = lambda q: w_ri.at[q, s]
    ri.result = lambda q: fin.at[at(q * rec + blk, cblk, 16)]
    hi.source = lambda q: xhu.at[at(q * blk, blk, 16)]
    hi.place = cube_place(w_hu, slice(0, hid))
    hi.result = lambda q: fin_hu.at[at(q * blk, blk, 16), slice(0, hid)]
    up.source = lambda q: xhu.at[at((GROUP + q) * blk, blk, 16)]
    up.place = cube_place(w_hu, slice(hid, 2 * hid))
    up.result = lambda q: fin_hu.at[at(q * blk, blk, 16), slice(hid, 2 * hid)]

    def member_cols(array, q, parts):
        pieces = [array[:, parts * (GROUP * k + q) : parts * (GROUP * k + q + 1)] for k in range(RING)]
        return jnp.concatenate(pieces, axis=1)

    def prepare(c, tall, parts, *names):
        for q in range(GROUP):
            for k, name in enumerate(names):
                array = raw[spots[name] : spots[name] + tall, :]
                if array.shape[1] < RING * GROUP * parts:
                    array = jnp.concatenate([array, raw[spots[name] + tall : spots[name] + 2 * tall, :]], axis=1)
                c.source(q)[:, k * RING * parts : (k + 1) * RING * parts] = member_cols(array, q, parts)

    def spread(c):
        for (peer, to), slot in zip(group_peers, c.spread):
            net.put(c.source(peer), c.place(b), to, slot)
        c.place(b)[...] = c.source(b)[...]

    def spread_wait(c):
        for (peer, to), slot in zip(group_peers, c.spread):
            net.got(c.place(peer), to, slot)

    def g0(c, *which):
        for slot in which or range(3):
            axis = c.axes[slot]
            net.put(c.block(s), c.block(s), reach(axis), c.gather[slot])

    def g1(c):
        i, j, k = c.axes
        net.got(c.block(turned(i)), reach(i), c.gather[0])
        net.put(c.block(turned(i)), c.block(turned(i)), reach(j), c.gather[3])
        net.put(c.block(turned(i)), c.block(turned(i)), reach(k), c.gather[4])

    def g2(c):
        i, j, k = c.axes
        net.got(c.block(turned(j)), reach(j), c.gather[1])
        net.put(c.block(turned(j)), c.block(turned(j)), reach(k), c.gather[5])

    def g3(c):
        i, j, k = c.axes
        net.got(c.block(turned(i + j)), reach(j), c.gather[3])
        net.put(c.block(turned(i + j)), c.block(turned(i + j)), reach(k), c.gather[6])

    def gather_wait(c):
        i, j, k = c.axes
        for slot, axes in ((2, k), (4, i + k), (5, j + k), (6, i + j + k)):
            net.got(c.block(turned(axes)), reach(k), c.gather[slot])

    def sp(c, *which):
        i, j, k = c.back
        for slot in which:
            axes = ("", i, j, i + j)[slot]
            net.put(c.block(turned(axes + k)), c.first_sum(slot), reach(k), c.sums[slot], "sum")

    def added(c, axes, parts, keep):
        def add(i):
            total = c.piece(turned(axes), i)[...].astype(F32)
            for ref in parts:
                total = total + part_of(c, ref, i).astype(F32)
            keep(i, total)

        loop(c.pieces, add)

    def part_of(c, ref, i):
        if len(ref.shape) == 2:
            return ref[at(i * 16, 16, 16), :]
        return ref[i]

    def back_to(c, axes):
        def keep(i, total):
            c.piece(turned(axes), i)[...] = total.astype(BF16)

        return keep

    def se(c, *which):
        i, j, k = c.back
        for slot in which:
            axes = {2: j, 3: i + j}[slot]
            net.got(c.first_sum(slot), reach(k), c.sums[slot])
            added(c, axes, [c.first_sum(slot)], back_to(c, axes))
            net.put(c.block(turned(axes)), c.later_sum(slot - 2), reach(j), c.sums[slot + 2], "sum")

    def sf(c):
        i, j, k = c.back
        net.got(c.first_sum(1), reach(k), c.sums[1])
        net.got(c.later_sum(1), reach(j), c.sums[5])
        added(c, i, [c.first_sum(1), c.later_sum(1)], back_to(c, i))
        net.put(c.block(turned(i)), c.later_sum(2), reach(i), c.sums[6], "sum")

    def sum_end(c, keep):
        i, j, k = c.back
        net.got(c.first_sum(0), reach(k), c.sums[0])
        net.got(c.later_sum(0), reach(j), c.sums[4])
        net.got(c.later_sum(2), reach(i), c.sums[6])
        added(c, "", [c.first_sum(0), c.later_sum(0), c.later_sum(2)], keep)

    def sum_end_spread(c):
        sum_end(c, back_to(c, ""))
        for (peer, to), slot in zip(group_peers, c.home):
            net.put(c.place(peer), c.result(b), to, slot)
        c.result(b)[...] = c.place(b)[...]

    def home_wait(c):
        for (peer, to), slot in zip(group_peers, c.home):
            net.got(c.result(peer), to, slot)

    def share(view, slots, h):
        net.put(view(b, h), view(b, h), to_across, slots[3 * h])
        net.put(view(b, h), view(b, h), to_mate, slots[3 * h + 1])

    def share_relay(view, slots, h):
        net.got(view(across, h), to_across, slots[3 * h])
        net.put(view(across, h), view(across, h), to_mate, slots[3 * h + 2])

    def share_end(view, slots, h):
        net.got(view(mate, h), to_mate, slots[3 * h + 1])
        net.got(view(corner, h), to_mate, slots[3 * h + 2])

    def token_rows(ref):
        return lambda q, h: ref.at[at((h * GROUP + q) * here, here, 16)]

    def merge(view, first, slots, h):
        net.put(view(corner, h), first(h, 1), to_mate, slots[3 * h], "part")
        net.put(view(mate, h), first(h, 0), to_mate, slots[3 * h + 1], "part")

    def merge_relay(view, first, second, slots, h, parts, tile):
        net.got(first(h, 1), to_mate, slots[3 * h])

        def add(i):
            v = tile(view(across, h), i)
            v[...] = (v[...].astype(F32) + tile(first(h, 1), i)[...].astype(F32)).astype(BF16)

        loop(parts, add)
        net.put(view(across, h), second(h), to_across, slots[3 * h + 2], "part")

    def merge_end(first, second, slots, h):
        net.got(first(h, 0), to_mate, slots[3 * h + 1])
        net.got(second(h), to_across, slots[3 * h + 2])

    def sixteen(ref, i):
        return ref.at[at(i * 16, 16, 16)]

    first_in = lambda h, slot: core_in.at[h, slot]
    second_in = lambda h: x_in.at[h]
    part_rows = token_rows(part)

    def merged(h, i):
        total = sixteen(part_rows(b, h), i)[...].astype(F32)
        return total + core_in[h, 0, at(i * 16, 16, 16)].astype(F32) + x_in[h, at(i * 16, 16, 16)].astype(F32)

    def own(ref, h, i):
        return ref.at[at(h * here + i * 16, 16, 16)]

    tiles16 = here // 16

    def rms(values):
        return lax.rsqrt(jnp.mean(values * values, axis=-1, keepdims=True) + EPSILON)

    def norm_grad(index, values, incoming, gain):
        scaler = rms(values)
        scaled = incoming * gain
        inner = jnp.mean(scaled * values, axis=-1, keepdims=True)
        term = incoming * values * scaler
        gain_acc[index] += term[0:8] + term[8:16]
        return scaler * (scaled - values * (scaler * scaler * inner))

    def over(h, body):
        def row(i):
            q = h * GROUP + i
            for start in range(0, here, STEP):
                for g, lanes in enumerate(groups):
                    body(q, start, lanes, g)

        loop(GROUP, row)

    def flat(q, start):
        return at(q * here + start, STEP, STEP)

    def add_to(index, lanes, values):
        total = values[0:8]
        for k in range(8, STEP, 8):
            total = total + values[k : k + 8]
        acc[index, :, lanes] += total

    def same(q, start, k):
        now = brx[q, pl.ds(EDGE + start, STEP), marks]
        return (now == brx[q, pl.ds(EDGE + start - k, STEP), marks]).astype(F32)

    norm_slots, gout_slots, conv_slots = (net.slots(6), net.slots(6), net.slots(6))
    two_slots, gres_slots = (net.slots(6), net.slots(6))
    out_slots, gnt_slots, down_slots, thru_slots, gn_slots = (net.slots(6) for _ in range(5))
    halo_slot, halo_back = net.slots(2)
    pre_slots, back_slots, vec_slots, last_slots = (
        net.slots(RING),
        net.slots(RING),
        net.slots(RING),
        net.slots(3),
    )
    norm_rows, gout_rows, two_rows, gres_rows = (token_rows(ref) for ref in (norm, gout, norm_two, gres))
    conv_cols = lambda q, h: conv.at[pl.ds(h * half, half), at(q * chans, chans, LANES)]

    fetch_wait("w_input", "own_o")
    prepare(inp, blk, cblk, "w_input")
    fetch_wait("x", "seg", "gain_one", "gain_two")
    gain_one, gain_two = (gains[0:1], gains[1:2])
    pl.semaphore_wait(barrier, 3 + RING - 1)
    spread(inp)

    def norm_half(h):
        ids = r["seg"][h : h + 1, :].astype(F32)
        norm[at((h * GROUP + b) * here, here, 16), width : width + LANES] = jnp.transpose(
            jnp.broadcast_to(ids, (here, here))
        ).astype(BF16)

        def norm_tile(i):
            v = own(x, h, i)[...]
            sixteen(norm_rows(b, h), i)[:, 0:width] = (v * rms(v) * gain_one).astype(BF16)

        loop(tiles16, norm_tile)

    fetch_wait("w_gate")
    prepare(gat, blk, cblk, "w_gate")
    spread(gat)
    fetch_wait("w_recur", "w_inject")
    prepare(ri, cblk, cblk, "w_recur", "w_inject")
    spread(ri)
    spread_wait(inp)
    g0(inp)
    norm_half(0)
    share(norm_rows, norm_slots, 0)
    spread_wait(gat)
    g0(gat)
    norm_half(1)
    share(norm_rows, norm_slots, 1)
    g1(inp)
    g2(inp)
    fetch_wait("w_hidden")
    prepare(hi, blk, fblk, "w_hidden")
    g1(gat)
    g3(inp)
    spread(hi)
    spread_wait(ri)
    g0(ri)
    g2(gat)
    fetch_wait("w_upward")
    prepare(up, blk, fblk, "w_upward")
    spread(up)

    fetch_wait("vec")
    log_of = lambda grown: jnp.log(grown)
    biases = jnp.concatenate([r["biases"][k].reshape(1, -1) for k in range(4)], axis=0)
    small = jnp.exp(biases[3:4])
    grown = 1.0 + small
    rate = jnp.where(grown == 1.0, small, log_of(grown) * small / jnp.where(grown == 1.0, 1.0, grown - 1.0))
    sources = jnp.concatenate([r["taps"][...], biases[0:3], -DECAY_SCALE * rate], axis=0)
    for q in range(GROUP):
        r["vecs"][q, 0:8] = member_cols(sources, q, cblk)
        r["vecs"][q, 8:16] = member_cols(jnp.broadcast_to(jax.nn.sigmoid(biases[3:4]), (8, GROUP * chans)), q, cblk)
    vec[...] = r["vecs"][b]
    acc[...] = jnp.zeros_like(acc)
    gain_acc[...] = jnp.zeros_like(gain_acc)

    @pl.when(s == 0)
    def _():
        brx[:, 0:EDGE, :] = jnp.full((rows, EDGE, chans + LANES), -1.0, F32)

    @pl.when(s == RING - 1)
    def _():
        tgx[:, here : here + EDGE, :] = jnp.full((rows, EDGE, chans + LANES), -1.0, F32)

    share_relay(norm_rows, norm_slots, 0)
    fetch_wait("cot")
    for h in range(2):
        def low_tile(i, h=h):
            sixteen(gout_rows(b, h), i)[...] = own(cot, h, i)[...].astype(BF16)

        loop(tiles16, low_tile)
    gather_wait(inp)
    share_end(norm_rows, norm_slots, 0)

    for h in range(2):
        if h:
            share_relay(norm_rows, norm_slots, h)
            share_end(norm_rows, norm_slots, h)
        span = pl.ds(h * half, half)
        block = slice(h * GROUP, (h + 1) * GROUP)
        got = dot_nn(norm[span, 0:width], w_one[:, :, in_side].reshape(width, chans))
        brx[block, EDGE : EDGE + here, 0:chans] = got.reshape(GROUP, here, chans)
        ids = norm[span, width : width + LANES].astype(F32).reshape(GROUP, here, LANES)
        brx[block, EDGE : EDGE + here, marks] = ids
        tgx[block, 0:here, marks] = ids

    def edge_copies(ref, src, dst, slot, step, gives, takes):
        def copy(where):
            return pltpu.make_async_remote_copy(
                src_ref=ref.at[:, pl.ds(src, EDGE)],
                dst_ref=ref.at[:, pl.ds(dst, EDGE)],
                send_sem=net.send.at[slot],
                recv_sem=net.recv.at[slot],
                device_id=(where, b),
                device_id_type=MESH,
            )

        def out(act):
            @pl.when(gives)
            def _():
                act(copy(lax.rem(s + step, RING)))

        def arrive():
            @pl.when(takes)
            def _():
                copy(lax.rem(s + RING - step, RING)).wait_recv()

        return (out, arrive)

    edge_out, edge_in = edge_copies(brx, here, 0, halo_slot, 1, s < RING - 1, s > 0)
    edge_out(lambda one: one.start())
    g3(gat)
    edge_in()

    for h in range(2):
        def conv_tile(q, start, lanes, g):
            total = vec[4:5, lanes] + vec[0:1, lanes] * brx[q, pl.ds(EDGE + start, STEP), lanes]
            for k in range(1, 4):
                lag = brx[q, pl.ds(EDGE + start - k, STEP), lanes]
                total = total + vec[k : k + 1, lanes] * lag * same(q, start, k)
            conv_out[q, pl.ds(start, STEP), lanes] = total
            conv[flat(q, start), at(b * chans + g * LANES, LANES, LANES)] = total.astype(BF16)

        over(h, conv_tile)
        share(conv_cols, conv_slots, h)
        g2(ri) if h else g1(ri)
    g3(ri)
    g0(wo)
    spread_wait(hi)
    g0(hi)
    share_relay(conv_cols, conv_slots, 0)
    g1(wo)
    g2(wo)
    share_relay(conv_cols, conv_slots, 1)
    share_end(conv_cols, conv_slots, 0)
    gather_wait(ri)

    for h in range(2):
        if h:
            share_end(conv_cols, conv_slots, h)
        block = slice(h * GROUP, (h + 1) * GROUP)
        got = dot_nn(conv[pl.ds(h * half, half), :], w_ri[...].reshape(GROUP * chans, two))
        got = got.reshape(GROUP, here, two)
        rgate[block] = got[:, :, 0:chans]
        igate[block] = got[:, :, chans:two]

        def gate_tile(q, start, lanes, g):
            span = pl.ds(start, STEP)
            rg = jax.nn.sigmoid(rgate[q, span, lanes] + vec[5:6, lanes])
            ig = jax.nn.sigmoid(igate[q, span, lanes] + vec[6:7, lanes])
            rgate[q, span, lanes] = rg
            igate[q, span, lanes] = ig
            decay = jnp.exp(rg * vec[7:8, lanes])
            carry[q, span, lanes] = decay * same(q, start, 1)
            scale = jnp.sqrt(1.0 - decay * decay + FLOOR_TERM)
            stx[q, pl.ds(EDGE + start, STEP), lanes] = scale * ig * conv_out[q, span, lanes]

        over(h, gate_tile)
        if h == 0:
            g3(wo)
        else:
            spread_wait(up)

    def ends(p, state):
        mult = carry[:, p, :]
        return (state[0] * mult, mult * state[1] + stx[:, EDGE + p, :])

    begin = (jnp.ones((rows, chans), F32), jnp.zeros((rows, chans), F32))
    product, tail = lax.fori_loop(0, here, ends, begin, unroll=8)
    def hand_round(ref, product, tail, slots):
        ref[s, 0:rows] = product
        ref[s, rows : 2 * rows] = tail
        for k in range(1, RING):
            net.put(ref.at[s], ref.at[s], ring_device(ring_to[k]), slots[k])

    def entering(ref, slots, forward):
        for k in range(1, RING):
            net.got(ref.at[ring_from[k]], ring_device(ring_from[k]), slots[k])
        state = jnp.zeros((rows, chans), F32)
        for q in range(RING - 1) if forward else range(RING - 1, 0, -1):
            longer = ref[q, rows : 2 * rows] + ref[q, 0:rows] * state
            state = jnp.where(q < s if forward else q > s, longer, state)
        return state

    hand_round(pre_f, product, tail, pre_slots)
    g1(hi)
    g2(hi)
    g0(up)
    fetch_wait("own_d")
    g0(dn)
    gather_wait(gat)

    for h in range(2):
        got = dot_nn(norm[pl.ds(h * half, half), 0:width], w_one[:, :, gate_side].reshape(width, chans))
        gate_pre[h * GROUP : (h + 1) * GROUP] = got.reshape(GROUP, here, chans)

        def act_tile(q, start, lanes, g):
            span = pl.ds(start, STEP)
            tgx[q, span, lanes] = gelu_parts(gate_pre[q, span, lanes])[0]

        over(h, act_tile)
    state = entering(pre_f, pre_slots, True)
    stx[:, EDGE - 1, :] = state

    def scan(p, state):
        state = carry[:, p, :] * state + stx[:, EDGE + p, :]
        stx[:, EDGE + p, :] = state
        return state

    lax.fori_loop(0, here, scan, state, unroll=8)
    g3(hi)
    gather_wait(wo)

    for h in range(2):
        def mix_tile(q, start, lanes, g):
            act = tgx[q, pl.ds(start, STEP), lanes]
            mix[flat(q, start), lanes] = (stx[q, pl.ds(EDGE + start, STEP), lanes] * act).astype(BF16)

        over(h, mix_tile)
        span = pl.ds(h * half, half)
        part[span, :] = dot_nn(mix[span, :], w_o[...]).astype(BF16)
        merge(part_rows, first_in, out_slots, h)
    for h in range(2):
        merge_relay(part_rows, first_in, second_in, out_slots, h, tiles16, sixteen)
    g1(up)
    for h in range(2):
        merge_end(first_in, second_in, out_slots, h)

        def resid_tile(i, h=h):
            v = own(x, h, i)[...] + merged(h, i)
            own(out, h, i)[...] = v
            sixteen(two_rows(b, h), i)[...] = (v * rms(v) * gain_two).astype(BF16)

        loop(tiles16, resid_tile)
        share(two_rows, two_slots, h)
        if h == 0:
            g2(up)
            g1(dn)
    for h in range(2):
        share(gout_rows, gout_slots, h)
    g3(up)
    g2(dn)
    share_relay(two_rows, two_slots, 0)
    share_relay(two_rows, two_slots, 1)
    gather_wait(hi)
    gather_wait(up)

    for h in range(2):
        share_end(two_rows, two_slots, h)
        span = pl.ds(h * half, half)
        for j in range(hid // 256):
            left = slice(j * 256, j * 256 + 256)
            right = slice(hid + j * 256, hid + j * 256 + 256)
            pre[:, 0:256] = dot_nn(norm_two[span, :], w_hu[:, :, left].reshape(width, 256))
            pre[:, 256:512] = dot_nn(norm_two[span, :], w_hu[:, :, right].reshape(width, 256))

            def tile(i, h=h, j=j):
                rows_t = at(i * STEP, STEP, STEP)
                flat_t = at(h * half + i * STEP, STEP, STEP)
                for g in range(2):
                    first = slice(j * 256 + g * LANES, j * 256 + (g + 1) * LANES)
                    second = slice(hid + j * 256 + g * LANES, hid + j * 256 + (g + 1) * LANES)
                    act, slope = gelu_parts(pre[rows_t, g * LANES : (g + 1) * LANES])
                    upward = pre[rows_t, 256 + g * LANES : 256 + (g + 1) * LANES]
                    prod[flat_t, first] = (act * upward).astype(BF16)
                    ghu[flat_t, first] = (upward * slope).astype(BF16)
                    ghu[flat_t, second] = act.astype(BF16)

            loop(half // STEP, tile)
        share_relay(gout_rows, gout_slots, h)
        if h == 0:
            g3(dn)
    for h in range(2):
        share_end(gout_rows, gout_slots, h)
    for j in range(2):
        cols = slice(j * hid // 2, (j + 1) * hid // 2)
        r["dw_d"][cols, :] = dot_tn(prod[:, cols], gout[...]).astype(BF16)
    sp(dn_sum, 3, 2, 1, 0)
    gather_wait(dn)

    net.flush("part")
    for h in range(2):
        span = pl.ds(h * half, half)
        for j in range(hid // 256):
            left = slice(j * 256, j * 256 + 256)
            right = slice(hid + j * 256, hid + j * 256 + 256)
            back = dot_nt(gout[span, :], w_d[left, :])
            ghu[span, left] = (back * ghu[span, left].astype(F32)).astype(BF16)
            ghu[span, right] = (back * ghu[span, right].astype(F32)).astype(BF16)
        for j in range(2):
            cols = slice(j * width // 2, (j + 1) * width // 2)
            part[span, cols] = dot_nt(ghu[span, :], w_hu[4 * j : 4 * j + 4].reshape(width // 2, 2 * hid)).astype(BF16)
        merge(part_rows, first_in, gnt_slots, h)
    for h in range(2):
        merge_relay(part_rows, first_in, second_in, gnt_slots, h, tiles16, sixteen)

    se(dn_sum, 3)
    net.flush("")
    for j in range(2):
        def grad_hu(i, j=j):
            cols = at(i * 256, 256, LANES)
            side = slice(j * hid, (j + 1) * hid)
            got = dot_tn(norm_two[:, cols], ghu[:, side]).astype(BF16)
            w_hu[pl.ds(2 * i, 2), :, side] = got.reshape(2, GROUP * blk, hid)

        loop(width // 256, grad_hu)
        if j == 0:
            sp(hi, 3, 2, 1, 0)
            se(dn_sum, 2)
        else:
            sp(up, 3)

    for h in range(2):
        merge_end(first_in, second_in, gnt_slots, h)

        def second_norm(i, h=h):
            back = norm_grad(1, own(out, h, i)[...], merged(h, i), gain_two)
            total = own(cot, h, i)[...] + back
            own(gin, h, i)[...] = total
            sixteen(gres_rows(b, h), i)[...] = total.astype(BF16)

        loop(tiles16, second_norm)
        share(gres_rows, gres_slots, h)
        if h == 0:
            sf(dn_sum)
    net.flush("part")
    for h in range(2):
        span = pl.ds(h * half, half)
        part[span, :] = dot_nn(prod[span, :], w_d[...]).astype(BF16)
    share_relay(gres_rows, gres_slots, 0)
    se(hi, 3)
    share_relay(gres_rows, gres_slots, 1)
    se(hi, 2)

    for h in range(2):
        share_end(gres_rows, gres_slots, h)
        if h:
            for k in range(2):
                merge(part_rows, first_in, down_slots, k)
        block = slice(h * GROUP, (h + 1) * GROUP)
        got = dot_nt(gres[pl.ds(h * half, half), :], w_o[...])
        tgx[block, 0:here, 0:chans] = got.reshape(GROUP, here, chans)
        if h:
            for k in range(2):
                merge_relay(part_rows, first_in, second_in, down_slots, k, tiles16, sixteen)

        def mix_back(q, start, lanes, g):
            span = pl.ds(start, STEP)
            act, slope = gelu_parts(gate_pre[q, span, lanes])
            back = tgx[q, span, lanes]
            states = stx[q, pl.ds(EDGE + start, STEP), lanes]
            ggb[flat(q, start), lanes] = (back * states * slope).astype(BF16)
            tgx[q, span, lanes] = back * act

        over(h, mix_back)

    def ends_back(i, state):
        p = here - 1 - i
        mult = carry[:, p, :]
        return (state[0] * mult, mult * (tgx[:, p, 0:chans] + state[1]))

    product, tail = lax.fori_loop(0, here, ends_back, begin, unroll=8)
    hand_round(pre_b, product, tail, back_slots)
    sp(up, 2, 1, 0)

    w_o[...] = dot_tn(mix[...], gres[...]).astype(BF16)
    for j in range(2):
        cols = slice(j * width // 2, (j + 1) * width // 2)
        got = dot_tn(norm[:, cols], ggb[:, gate_side]).astype(BF16)
        r["dw_gate"][4 * j : 4 * j + 4] = got.reshape(4, GROUP * blk, chans)

    state = entering(pre_b, back_slots, False)

    def scan_back(i, state):
        p = here - 1 - i
        total = tgx[:, p, 0:chans] + state
        tgx[:, p, 0:chans] = total
        return carry[:, p, :] * total

    lax.fori_loop(0, here, scan_back, state, unroll=8)

    sp(gat_sum, 3, 2, 1, 0)
    sp(wo, 3, 2, 1, 0)
    thru_cols = lambda q, h: ghu.at[pl.ds(h * half, half), at(q * chans, chans, LANES)]
    thru_first = lambda h, slot: prod.at[pl.ds(h * half, half), pl.ds(slot * chans, chans)]
    thru_second = lambda h: gout.at[pl.ds(h * half, half), pl.ds(0, chans)]
    for h in range(2):
        def gates_back(q, start, lanes, g):
            span = pl.ds(start, STEP)
            total = tgx[q, span, lanes]
            rg, ig, co = (rgate[q, span, lanes], igate[q, span, lanes], conv_out[q, span, lanes])
            before = stx[q, pl.ds(EDGE + start - 1, STEP), lanes]
            rate = vec[7:8, lanes]
            decay = jnp.exp(rg * rate)
            scale = jnp.sqrt(1.0 - decay * decay + FLOOR_TERM)
            grad_decay = total * before * same(q, start, 1) - total * ig * co * decay / scale
            grad_log = grad_decay * decay
            grad_rg = grad_log * rate * rg * (1.0 - rg)
            scaled = total * scale
            grad_ig = scaled * co * ig * (1.0 - ig)
            tgx[q, span, lanes] = scaled * ig
            gri[flat(q, start), lanes] = grad_rg.astype(BF16)
            gri[flat(q, start), slice(chans + g * LANES, chans + (g + 1) * LANES)] = grad_ig.astype(BF16)
            add_to(5, lanes, grad_rg)
            add_to(6, lanes, grad_ig)
            add_to(7, lanes, grad_log * (-DECAY_SCALE * rg))

        over(h, gates_back)
        span = pl.ds(h * half, half)
        for j in range(2):
            pair = slice(2 * j, 2 * j + 2)
            got = dot_nt(gri[span, :], w_ri[pair].reshape(2 * chans, two))
            ghu[span, 2 * j * chans : 2 * (j + 1) * chans] = got.astype(BF16)
        if h:
            for k in range(2):
                merge_end(first_in, second_in, down_slots, k)

                def out_tile(i, k=k):
                    own(out, k, i)[...] = own(out, k, i)[...] + merged(k, i)

                loop(tiles16, out_tile)
        merge(thru_cols, thru_first, thru_slots, h)
        if h == 0:
            sf(hi)
            se(up, 3)
    leave_out = fetch(0, out, out_hbm)
    for h in range(2):
        merge_relay(thru_cols, thru_first, thru_second, thru_slots, h, half // 16, sixteen)

    def grad_ri(i):
        got = dot_tn(conv[:, at(i * chans, chans, LANES)], gri[...])
        w_ri[i] = got.astype(BF16).reshape(RING, cblk, two)

    loop(GROUP, grad_ri)
    sp(ri, 3)
    se(up, 2)
    se(gat_sum, 3, 2)

    for h in range(2):
        merge_end(thru_first, thru_second, thru_slots, h)

        def conv_grad(q, start, lanes, g, h=h):
            span = flat(q, start)
            total = ghu[span, at(b * chans + g * LANES, LANES, LANES)].astype(F32)
            total = total + prod[span, lanes].astype(F32) + gout[span, lanes].astype(F32)
            tgx[q, pl.ds(start, STEP), lanes] += total

        over(h, conv_grad)
        if h == 0:
            sf(up)

    head_out, head_in = edge_copies(tgx, 0, here, halo_back, RING - 1, s > 0, s < RING - 1)
    head_out(lambda one: one.start())
    sp(ri, 2, 1, 0)
    se(ri, 3)
    head_in()
    se(wo, 3, 2)
    net.flush("part")
    for h in range(2):
        def conv_back(q, start, lanes, g):
            now = tgx[q, pl.ds(start, STEP), lanes]
            ids = tgx[q, pl.ds(start, STEP), marks]
            total = vec[0:1, lanes] * now
            add_to(4, lanes, now)
            add_to(0, lanes, now * brx[q, pl.ds(EDGE + start, STEP), lanes])
            for k in range(1, 4):
                later = pl.ds(start + k, STEP)
                match = (tgx[q, later, marks] == ids).astype(F32)
                total = total + vec[k : k + 1, lanes] * tgx[q, later, lanes] * match
                lag = brx[q, pl.ds(EDGE + start - k, STEP), lanes]
                add_to(k, lanes, now * lag * same(q, start, k))
            ggb[flat(q, start), slice(chans + g * LANES, chans + (g + 1) * LANES)] = total.astype(BF16)

        over(h, conv_back)
    for j in range(2):
        cols = slice(j * width // 2, (j + 1) * width // 2)
        got = dot_tn(norm[:, cols], ggb[:, in_side]).astype(BF16)
        r["dw_in"][4 * j : 4 * j + 4] = got.reshape(4, GROUP * blk, chans)
    sp(inp_sum, 3, 2, 1, 0)
    for h in range(2):
        span = pl.ds(h * half, half)
        for j in range(2):
            cols = slice(j * width // 2, (j + 1) * width // 2)
            part[span, cols] = dot_nt(ggb[span, :], w_one[4 * j : 4 * j + 4].reshape(width // 2, two)).astype(BF16)
        merge(part_rows, first_in, gn_slots, h)
    for h in range(2):
        merge_relay(part_rows, first_in, second_in, gn_slots, h, tiles16, sixteen)

    se(ri, 2)
    sf(gat_sum)
    se(inp_sum, 3, 2)

    for h in range(2):
        merge_end(first_in, second_in, gn_slots, h)

        def first_norm(i, h=h):
            back = norm_grad(0, own(x, h, i)[...], merged(h, i), gain_one)
            own(gin, h, i)[...] = own(gin, h, i)[...] + back

        loop(tiles16, first_norm)
    leave_gin = fetch(1, gin, gin_hbm)

    for k in range(8):
        total = jnp.sum(acc[k], axis=0, keepdims=True)
        vs[s, k : k + 1, 0:chans] = total * vec[8:9, :] if k == 7 else total
    piece = width // 4
    for k in range(2):
        total = jnp.sum(gain_acc[k], axis=0, keepdims=True)
        for j in range(4):
            vs[s, 4 * k + j : 4 * k + j + 1, chans : chans + piece] = total[:, j * piece : (j + 1) * piece]
    for k in range(1, RING):
        net.put(vs.at[s], vs.at[s], ring_device(ring_to[k]), vec_slots[k])

    def keep_down(i, total):
        g_d[at(i * 16, 16, 16), :] = total

    def keep_out(i, total):
        g_o[at(i * 16, 16, 16), :] = total

    sf(ri)
    sf(wo)
    sum_end(dn_sum, keep_down)
    sum_end_spread(hi)
    sum_end_spread(up)
    sf(inp_sum)
    sum_end_spread(gat_sum)
    sum_end_spread(ri)
    sum_end(wo, keep_out)
    sum_end_spread(inp_sum)
    for k in range(1, RING):
        net.got(vs.at[ring_from[k]], ring_device(ring_from[k]), vec_slots[k])
    total = vs[0]
    for q in range(1, RING):
        total = total + vs[q]
    vb[b] = total
    for (peer, to), slot in zip(group_peers, last_slots):
        net.put(vb.at[b], vb.at[b], to, slot)
    for (peer, to), slot in zip(group_peers, last_slots):
        net.got(vb.at[peer], to, slot)
    g_vec[:, 0:chans] = total[:, 0:chans]
    summed = vb[0, :, chans : chans + piece]
    for q in range(1, GROUP):
        summed = summed + vb[q, :, chans : chans + piece]
    g_vec[:, chans : chans + piece] = summed
    for c in (hi, up, gat_sum, inp_sum, ri):
        home_wait(c)
    net.flush()
    leave_out.wait()
    leave_gin.wait()

    edge_out(lambda one: one.wait_send())
    head_out(lambda one: one.wait_send())


def finish(names, *refs):
    r = dict(zip(names, refs))
    r["to_o"][...] = r["g_o"][...]
    r["to_d"][...] = r["g_d"][...]
    place = lax.axis_index("seq") * GROUP + lax.axis_index("batch")
    s = lax.axis_index("seq")
    blk, cblk, fblk = (r["to_gate"].shape[0], r["to_recur"].shape[0], r["to_d"].shape[0])
    chans, hid = (RING * cblk, RING * fblk)
    rec = blk + cblk

    def joined(pieces, parts):
        pieces = [piece.astype(F32) for piece in pieces]
        return jnp.concatenate(
            [pieces[q][:, k * parts : (k + 1) * parts] for k in range(RING) for q in range(GROUP)], axis=1
        )

    fin, fin_hu, g_vec = (r["fin"], r["fin_hu"], r["g_vec"])
    for name, first, tall, left in (
        ("to_gate", 0, blk, 0),
        ("to_input", 0, blk, chans),
        ("to_recur", blk, cblk, 0),
        ("to_inject", blk, cblk, chans),
    ):
        spans = [slice(q * rec + first, q * rec + first + tall) for q in range(GROUP)]
        r[name][...] = joined([fin[span, left : left + chans] for span in spans], cblk)
    for name, left in (("to_hidden", 0), ("to_upward", hid)):
        spans = [slice(q * blk, (q + 1) * blk) for q in range(GROUP)]
        r[name][...] = joined([fin_hu[span, left : left + hid] for span in spans], fblk)
    vectors = g_vec[:, 0:chans]
    mine = vectors[:, 0:cblk]
    for k in range(1, RING):
        mine = jnp.where(k == s, vectors[:, k * cblk : (k + 1) * cblk], mine)
    r["to_taps"][...] = mine[0:4]
    for k, name in enumerate(("to_cbias", "to_rbias", "to_ibias", "to_decay")):
        r[name][...] = mine[4 + k]
    piece = g_vec.shape[1] - chans
    for k, name in enumerate(("to_gain_one", "to_gain_two")):
        total = jnp.zeros((1, blk), F32)
        for j in range(4):
            for m in range(piece // blk):
                part = g_vec[4 * k + j : 4 * k + j + 1, chans + m * blk : chans + (m + 1) * blk]
                total = jnp.where(j * (piece // blk) + m == place, part, total)
        r[name][...] = total[0]


def split_block(
    inputs,
    segments,
    w_gate,
    w_input,
    w_recur,
    w_inject,
    w_output,
    w_hidden,
    w_upward,
    w_down,
    gain_one,
    gain_two,
    conv_taps,
    conv_bias,
    recur_bias,
    inject_bias,
    decay_param,
    cotangent,
):
    count, here, width = inputs.shape
    channels = w_gate.shape[1]
    chans, hid = (channels // GROUP, w_hidden.shape[1] // GROUP)
    blk, cblk, fblk = (w_gate.shape[0], w_recur.shape[0], w_down.shape[0])
    tokens = GROUP * count * here
    rows = GROUP * count
    wide = chans + LANES
    operands = {
        "hbm_x": inputs.reshape(count * here, width),
        "hbm_cot": cotangent.reshape(count * here, width),
        "hbm_seg": segments,
        "hbm_w_gate": w_gate,
        "hbm_w_input": w_input,
        "hbm_w_recur": w_recur,
        "hbm_w_inject": w_inject,
        "hbm_w_output": w_output,
        "hbm_w_hidden": w_hidden,
        "hbm_w_upward": w_upward,
        "hbm_w_down": w_down,
        "hbm_gain_one": gain_one,
        "hbm_gain_two": gain_two,
        "hbm_conv_taps": conv_taps,
        "hbm_conv_bias": conv_bias,
        "hbm_recur_bias": recur_bias,
        "hbm_inject_bias": inject_bias,
        "hbm_decay_param": decay_param,
    }
    piece = width // 4
    outputs = {
        "out": ((count * here, width), F32),
        "gin": ((count * here, width), F32),
        "fin": ((GROUP * (blk + cblk), 2 * chans), BF16),
        "fin_hu": ((GROUP * blk, 2 * hid), BF16),
        "g_o": ((cblk, width), F32),
        "g_d": ((fblk, width), F32),
        "g_vec": ((8, chans + piece), F32),
    }
    scratch = {
        "x": ((count * here, width), F32),
        "cot": ((count * here, width), F32),
        "out_own": ((count * here, width), F32),
        "seg": (segments.shape, jnp.int32),
        "gains": ((2, width), F32),
        "taps": (conv_taps.shape, F32),
        "biases": ((4, channels), F32),
        "vecs": ((GROUP, 16, chans), F32),
        "vec": ((16, chans), F32),
        "w_one": ((RING, GROUP * blk, 2 * chans), BF16),
        "dw_gate": ((RING, GROUP * blk, chans), BF16),
        "dw_in": ((RING, GROUP * blk, chans), BF16),
        "dw_d": ((hid, width), BF16),
        "w_ri": ((GROUP, RING, cblk, 2 * chans), BF16),
        "w_o": ((chans, width), BF16),
        "w_hu": ((RING, GROUP * blk, 2 * hid), BF16),
        "w_d": ((hid, width), BF16),
        "norm": ((tokens, width + LANES), BF16),
        "gout": ((tokens, width), BF16),
        "norm_two": ((tokens, width), BF16),
        "gres": ((tokens, width), BF16),
        "conv": ((tokens, channels), BF16),
        "mix": ((tokens, chans), BF16),
        "prod": ((tokens, hid), BF16),
        "ghu": ((tokens, 2 * hid), BF16),
        "ggb": ((tokens, 2 * chans), BF16),
        "gri": ((tokens, 2 * chans), BF16),
        "part": ((tokens, width), BF16),
        "brx": ((rows, EDGE + here, wide), F32),
        "tgx": ((rows, here + EDGE, wide), F32),
        "stx": ((rows, EDGE + here, chans), F32),
        "gate_pre": ((rows, here, chans), F32),
        "conv_out": ((rows, here, chans), F32),
        "rgate": ((rows, here, chans), F32),
        "igate": ((rows, here, chans), F32),
        "carry": ((rows, here, chans), F32),
        "pre": ((GROUP * here, 512), F32),
        "core_in": ((2, 2, here, width), BF16),
        "x_in": ((2, here, width), BF16),
        "pre_f": ((RING, 2 * rows, chans), F32),
        "pre_b": ((RING, 2 * rows, chans), F32),
        "y_ri": ((4, GROUP, cblk, 2 * chans), BF16),
        "z_ri": ((3, GROUP, cblk, 2 * chans), BF16),
        "y_o": ((4 * cblk, width), BF16),
        "z_o": (((3) * cblk, width), BF16),
        "y_h": ((4, GROUP * blk, hid), BF16),
        "z_h": ((3, GROUP * blk, hid), BF16),
        "y_u": ((4, GROUP * blk, hid), BF16),
        "z_u": ((3, GROUP * blk, hid), BF16),
        "y_d": ((4 * fblk, width), BF16),
        "z_d": (((3) * fblk, width), BF16),
        "acc": ((8, 8, chans), F32),
        "gain_acc": ((2, 8, width), F32),
        "vs": ((RING, 8, chans + piece), F32),
        "vb": ((GROUP, 8, chans + piece), F32),
    }
    names = [*operands, *outputs, *scratch, "send", "recv", "local"]
    in_vmem = pl.BlockSpec(memory_space=pltpu.VMEM)
    in_hbm = pl.BlockSpec(memory_space=pl.ANY)
    shapes = lambda specs: [jax.ShapeDtypeStruct(shape, kind) for shape, kind in specs.values()]
    got = pl.pallas_call(
        functools.partial(fused, names),
        out_shape=shapes(outputs),
        in_specs=[in_hbm] * len(operands),
        out_specs=[in_hbm] * 2 + [in_vmem] * (len(outputs) - 2),
        scratch_shapes=[pltpu.VMEM(shape, kind) for shape, kind in scratch.values()]
        + [pltpu.SemaphoreType.DMA((SLOTS,))] * 2
        + [pltpu.SemaphoreType.DMA((20,))],
        compiler_params=pltpu.CompilerParams(
            collective_id=0, has_side_effects=True, vmem_limit_bytes=VMEM_BYTES
        ),
        name="block",
    )(*operands.values())
    finals = {
        "to_gate": ((blk, channels), F32),
        "to_input": ((blk, channels), F32),
        "to_recur": ((cblk, channels), F32),
        "to_inject": ((cblk, channels), F32),
        "to_o": ((cblk, width), F32),
        "to_hidden": ((blk, GROUP * hid), F32),
        "to_upward": ((blk, GROUP * hid), F32),
        "to_d": ((fblk, width), F32),
        "to_gain_one": ((blk,), F32),
        "to_gain_two": ((blk,), F32),
        "to_taps": ((4, cblk), F32),
        "to_cbias": ((cblk,), F32),
        "to_rbias": ((cblk,), F32),
        "to_ibias": ((cblk,), F32),
        "to_decay": ((cblk,), F32),
    }
    done = pl.pallas_call(
        functools.partial(finish, [*list(outputs)[2:], *finals]),
        out_shape=shapes(finals),
        in_specs=[in_vmem] * (len(outputs) - 2),
        out_specs=[in_vmem] * len(finals),
        name="finish",
    )(*got[2:])
    return (
        got[0].reshape(count, here, width),
        got[1].reshape(count, here, width),
        *done,
    )


def solution(mesh):
    fits = dict(mesh.shape) == {"seq": RING, "batch": GROUP}
    return jax.shard_map(
        split_block if fits else gathered_block,
        mesh=mesh,
        in_specs=(
            P("batch", "seq", None),
            P("batch", "seq"),
            P(("seq", "batch"), None),
            P(("seq", "batch"), None),
            P(("seq", "batch"), None),
            P(("seq", "batch"), None),
            P(("seq", "batch"), None),
            P(("seq", "batch"), None),
            P(("seq", "batch"), None),
            P(("seq", "batch"), None),
            P(),
            P(),
            P(),
            P(),
            P(),
            P(),
            P(),
            P("batch", "seq", None),
        ),
        out_specs=(
            P("batch", "seq", None),
            P("batch", "seq", None),
            P(("seq", "batch"), None),
            P(("seq", "batch"), None),
            P(("seq", "batch"), None),
            P(("seq", "batch"), None),
            P(("seq", "batch"), None),
            P(("seq", "batch"), None),
            P(("seq", "batch"), None),
            P(("seq", "batch"), None),
            P(("seq", "batch")),
            P(("seq", "batch")),
            P(None, ("seq", "batch")),
            P(("seq", "batch")),
            P(("seq", "batch")),
            P(("seq", "batch")),
            P(("seq", "batch")),
        ),
        check_vma=False,
    )
```

```python
import functools

import jax
import jax.numpy as jnp
from jax import lax
from jax.experimental import pallas as pl
from jax.experimental.pallas import tpu as pltpu
from jax.sharding import PartitionSpec as P

EPSILON = 1e-06
DECAY_SCALE = 8.0
FLOOR_TERM = 0.01
SLOTS = 390
VMEM_BYTES = 63 << 20


def shifted(array, axis, by):
    peers = lax.axis_size(axis)
    pairs = [(i, i + by) for i in range(peers) if 0 <= i + by < peers]
    return lax.ppermute(array, axis, pairs)


def prefix(value, axis, join, neutral, backward):
    count, mine = (lax.axis_size(axis), lax.axis_index(axis))
    pieces = jax.tree.map(lambda part: lax.all_gather(part, axis), value)
    if backward:
        pieces = jax.tree.map(lambda part: part[::-1], pieces)
        mine = count - 1 - mine
    so_far = jax.tree.map(
        lambda part, zero: jnp.full_like(part, 0) + jnp.asarray(zero, part.dtype), value, neutral
    )

    def turn(position, so_far):
        longer = join(so_far, jax.tree.map(lambda part: part[position], pieces))
        return jax.tree.map(lambda new, old: jnp.where(position < mine, new, old), longer, so_far)

    return lax.fori_loop(0, count - 1, turn, so_far)


def shortened(array):
    return jax.tree.map(lambda a: a.astype(jnp.bfloat16) if a.dtype == jnp.float32 else a, array)


def combine(earlier, later):
    return (earlier[0] * later[0], later[1] + later[0] * earlier[1])


def matmul_plain(left, right):
    return jnp.dot(left, right, preferred_element_type=jnp.float32)


def matmul_tleft(left, right):
    return jnp.einsum("ta,tb->ab", left, right, preferred_element_type=jnp.float32)


def matmul_tright(left, right):
    return jnp.einsum("ta,ba->tb", left, right, preferred_element_type=jnp.float32)


def norm_forward(values, gain):
    scaler = lax.rsqrt(jnp.mean(values * values, axis=-1, keepdims=True) + EPSILON)
    return (values * scaler * gain, scaler)


def norm_back(values, scaler, gain, incoming):
    scaled = incoming * gain
    grad_gain = jnp.sum(incoming * values * scaler, axis=0)
    inner = jnp.mean(scaled * values, axis=-1, keepdims=True)
    return (scaler * (scaled - values * scaler * scaler * inner), grad_gain)


def gathered_block(
    inputs,
    segments,
    w_gate,
    w_input,
    w_recur,
    w_inject,
    w_output,
    w_hidden,
    w_upward,
    w_down,
    gain_one,
    gain_two,
    conv_taps,
    conv_bias,
    recur_bias,
    inject_bias,
    decay_param,
    cotangent,
):
    row_count, positions, features = inputs.shape
    (
        gate_full,
        input_full,
        recur_full,
        inject_full,
        output_full,
        hidden_full,
        upward_full,
        down_full,
    ) = (
        lax.all_gather(w_gate, ("seq", "batch"), axis=0, tiled=True),
        lax.all_gather(w_input, ("seq", "batch"), axis=0, tiled=True),
        lax.all_gather(w_recur, ("seq", "batch"), axis=0, tiled=True),
        lax.all_gather(w_inject, ("seq", "batch"), axis=0, tiled=True),
        lax.all_gather(w_output, ("seq", "batch"), axis=0, tiled=True),
        lax.all_gather(w_hidden, ("seq", "batch"), axis=0, tiled=True),
        lax.all_gather(w_upward, ("seq", "batch"), axis=0, tiled=True),
        lax.all_gather(w_down, ("seq", "batch"), axis=0, tiled=True),
    )
    channels = gate_full.shape[1]
    tokens_here = row_count * positions
    flat_in = inputs.reshape(tokens_here, features)
    normed, scale_one = norm_forward(flat_in, gain_one)
    normed_low = normed.astype(jnp.bfloat16)
    gate_pre = matmul_plain(normed_low, gate_full)
    gate_act, gate_pull = jax.vjp(jax.nn.gelu, gate_pre)
    branch = matmul_plain(normed_low, input_full).reshape(row_count, positions, channels)
    seg_marks = segments.astype(jnp.float32) + 1.0
    prior_branch, prior_marks = shifted(
        (branch[:, positions - 3 :], seg_marks[:, positions - 3 :]), "seq", 1
    )
    ext_branch = jnp.concatenate([prior_branch, branch], axis=1)
    ext_marks = jnp.concatenate([prior_marks, seg_marks], axis=1)
    sames = []
    lagged = []
    for offset in range(4):
        sames.append(
            (ext_marks[:, 3 - offset : 3 - offset + positions] == seg_marks).astype(jnp.float32)[
                :, :, None
            ]
        )
        lagged.append(ext_branch[:, 3 - offset : 3 - offset + positions])
    conv_out = conv_bias + conv_taps[0] * branch
    for offset in range(1, 4):
        conv_out = conv_out + conv_taps[offset] * lagged[offset] * sames[offset]
    conv_low = conv_out.reshape(tokens_here, channels).astype(jnp.bfloat16)
    recur_gate = jax.nn.sigmoid(matmul_plain(conv_low, recur_full) + recur_bias).reshape(
        row_count, positions, channels
    )
    inject_gate = jax.nn.sigmoid(matmul_plain(conv_low, inject_full) + inject_bias).reshape(
        row_count, positions, channels
    )
    base_rate = jax.nn.softplus(decay_param)
    decays = jnp.exp(-DECAY_SCALE * recur_gate * base_rate)
    carry_mult = decays * sames[1]
    normalizer = jnp.sqrt(1.0 - decays * decays + FLOOR_TERM)
    injected = normalizer * inject_gate * conv_out
    cumul, local_state = lax.associative_scan(combine, (carry_mult, injected), axis=1)
    ones_rows = jnp.ones((row_count, channels), jnp.float32)
    zeros_rows = jnp.zeros((row_count, channels), jnp.float32)
    entry = prefix(
        (cumul[:, -1], local_state[:, -1]), "seq", combine, (ones_rows, zeros_rows), False
    )[1]
    states = local_state + cumul * entry[:, None]
    states_before = jnp.concatenate([entry[:, None], states[:, :-1]], axis=1)
    states_flat = states.reshape(tokens_here, channels)
    mixed = (states_flat * gate_act).astype(jnp.bfloat16)
    resid = flat_in + matmul_plain(mixed, output_full)
    normed_two, scale_two = norm_forward(resid, gain_two)
    normed_two_low = normed_two.astype(jnp.bfloat16)
    hidden_pre = matmul_plain(normed_two_low, hidden_full)
    upward_pre = matmul_plain(normed_two_low, upward_full)
    hidden_act, hidden_pull = jax.vjp(jax.nn.gelu, hidden_pre)
    product = (hidden_act * upward_pre).astype(jnp.bfloat16)
    output = resid + matmul_plain(product, down_full)
    grad_out = cotangent.reshape(tokens_here, features)
    grad_out_low = grad_out.astype(jnp.bfloat16)
    grad_down = matmul_tleft(product, grad_out_low)
    grad_product = matmul_tright(grad_out_low, down_full)
    grad_hidden_pre = hidden_pull(grad_product * upward_pre)[0].astype(jnp.bfloat16)
    grad_upward_pre = (grad_product * hidden_act).astype(jnp.bfloat16)
    grad_hidden = matmul_tleft(normed_two_low, grad_hidden_pre)
    grad_upward = matmul_tleft(normed_two_low, grad_upward_pre)
    grad_normed_two = matmul_tright(grad_hidden_pre, hidden_full) + matmul_tright(
        grad_upward_pre, upward_full
    )
    grad_resid_norm, grad_gain_two = norm_back(resid, scale_two, gain_two, grad_normed_two)
    grad_resid = grad_out + grad_resid_norm
    grad_resid_low = grad_resid.astype(jnp.bfloat16)
    grad_output = matmul_tleft(mixed, grad_resid_low)
    grad_mixed = matmul_tright(grad_resid_low, output_full)
    grad_gate_pre = gate_pull(grad_mixed * states_flat)[0].astype(jnp.bfloat16)
    grad_states = (grad_mixed * gate_act).reshape(row_count, positions, channels)
    next_mult = jnp.concatenate([carry_mult[:, 1:], jnp.ones_like(carry_mult[:, :1])], axis=1)
    tail_prod, local_grad = lax.associative_scan(
        combine, (next_mult, grad_states), axis=1, reverse=True
    )
    incoming = prefix(
        (cumul[:, -1], carry_mult[:, 0] * local_grad[:, 0]),
        "seq",
        combine,
        (ones_rows, zeros_rows),
        True,
    )[1]
    total_grad = local_grad + tail_prod * incoming[:, None]
    grad_decays = (
        total_grad * states_before * sames[1]
        - total_grad * inject_gate * conv_out * decays / normalizer
    )
    grad_log = grad_decays * decays
    grad_recur_pre = grad_log * (-DECAY_SCALE * base_rate) * recur_gate * (1.0 - recur_gate)
    grad_decay_param = jnp.sum(
        grad_log * (-DECAY_SCALE * recur_gate), axis=(0, 1)
    ) * jax.nn.sigmoid(decay_param)
    grad_inject_pre = total_grad * normalizer * conv_out * inject_gate * (1.0 - inject_gate)
    grad_recur_bias = jnp.sum(grad_recur_pre, axis=(0, 1))
    grad_inject_bias = jnp.sum(grad_inject_pre, axis=(0, 1))
    grad_recur_low = grad_recur_pre.reshape(tokens_here, channels).astype(jnp.bfloat16)
    grad_inject_low = grad_inject_pre.reshape(tokens_here, channels).astype(jnp.bfloat16)
    grad_recur = matmul_tleft(conv_low, grad_recur_low)
    grad_inject = matmul_tleft(conv_low, grad_inject_low)
    through_gates = matmul_tright(grad_recur_low, recur_full) + matmul_tright(
        grad_inject_low, inject_full
    )
    grad_conv = total_grad * normalizer * inject_gate + through_gates.reshape(
        row_count, positions, channels
    )
    grad_conv_bias = jnp.sum(grad_conv, axis=(0, 1))
    taps_by_channel = jnp.stack(
        [jnp.sum(grad_conv * lagged[offset] * sames[offset], axis=(0, 1)) for offset in range(4)],
        axis=1,
    )
    later_grad, later_marks = (
        shifted(shortened(grad_conv[:, :3]), "seq", -1),
        shifted(seg_marks[:, :3].astype(jnp.bfloat16), "seq", -1).astype(jnp.float32),
    )
    ext_grad = jnp.concatenate([grad_conv, later_grad], axis=1)
    ext_after = jnp.concatenate([seg_marks, later_marks], axis=1)
    grad_branch = conv_taps[0] * grad_conv
    for offset in range(1, 4):
        match = (ext_after[:, offset : offset + positions] == seg_marks).astype(jnp.float32)[
            :, :, None
        ]
        grad_branch = (
            grad_branch + conv_taps[offset] * ext_grad[:, offset : offset + positions] * match
        )
    grad_branch_low = grad_branch.reshape(tokens_here, channels).astype(jnp.bfloat16)
    grad_input = matmul_tleft(normed_low, grad_branch_low)
    grad_gate = matmul_tleft(normed_low, grad_gate_pre)
    grad_normed = matmul_tright(grad_gate_pre, gate_full) + matmul_tright(
        grad_branch_low, input_full
    )
    grad_first_norm, grad_gain_one = norm_back(flat_in, scale_one, gain_one, grad_normed)
    grad_inputs = (grad_resid + grad_first_norm).reshape(row_count, positions, features)
    every = (
        lax.psum_scatter(grad_gate, ("seq", "batch"), scatter_dimension=0, tiled=True),
        lax.psum_scatter(grad_input, ("seq", "batch"), scatter_dimension=0, tiled=True),
        lax.psum_scatter(grad_recur, ("seq", "batch"), scatter_dimension=0, tiled=True),
        lax.psum_scatter(grad_inject, ("seq", "batch"), scatter_dimension=0, tiled=True),
        lax.psum_scatter(grad_output, ("seq", "batch"), scatter_dimension=0, tiled=True),
        lax.psum_scatter(grad_hidden, ("seq", "batch"), scatter_dimension=0, tiled=True),
        lax.psum_scatter(grad_upward, ("seq", "batch"), scatter_dimension=0, tiled=True),
        lax.psum_scatter(grad_down, ("seq", "batch"), scatter_dimension=0, tiled=True),
        lax.psum_scatter(grad_gain_one, ("seq", "batch"), scatter_dimension=0, tiled=True),
        lax.psum_scatter(grad_gain_two, ("seq", "batch"), scatter_dimension=0, tiled=True),
        lax.psum_scatter(taps_by_channel, ("seq", "batch"), scatter_dimension=0, tiled=True),
        lax.psum_scatter(grad_conv_bias, ("seq", "batch"), scatter_dimension=0, tiled=True),
        lax.psum_scatter(grad_recur_bias, ("seq", "batch"), scatter_dimension=0, tiled=True),
        lax.psum_scatter(grad_inject_bias, ("seq", "batch"), scatter_dimension=0, tiled=True),
        lax.psum_scatter(grad_decay_param, ("seq", "batch"), scatter_dimension=0, tiled=True),
    )
    summed = (
        every[0],
        every[1],
        every[2],
        every[3],
        every[4],
        every[5],
        every[6],
        every[7],
        every[8],
        every[9],
        every[10].T,
        every[11],
        every[12],
        every[13],
        every[14],
    )
    return (
        output.reshape(row_count, positions, features),
        grad_inputs,
        summed[0],
        summed[1],
        summed[2],
        summed[3],
        summed[4],
        summed[5],
        summed[6],
        summed[7],
        summed[8],
        summed[9],
        summed[10],
        summed[11],
        summed[12],
        summed[13],
        summed[14],
    )


MESH = pl.DeviceIdType.MESH
PLAN = {
    "f1": ["wait inp", "g0 inp 012"],
    "f2": ["wait gat", "g0 gat 012"],
    "f3": ["g1 inp", "g2 inp"],
    "f4": ["g1 gat", "g3 inp"],
    "f5": ["wait ra", "g0 ra 012", "wait rb", "g0 rb 01", "g2 gat"],
    "f91": ["g0 rb 2", "g1 ra", "g3 gat"],
    "conv0": ["g1 rb", "g2 ra"],
    "conv1": ["g2 rb", "g3 ra", "g3 rb", "g0 wo 012"],
    "f10": ["g1 wo", "g2 wo", "wait hi", "g0 hi 012"],
    "f11": ["g3 wo"],
    "gate1": ["wait up"],
    "f12": ["g1 hi", "g2 hi", "g0 up 012", "g0 dn 012"],
    "f14": ["g3 hi", "g1 up"],
    "resid0": ["g2 up", "g1 dn"],
    "f15": ["g3 up", "g2 dn"],
    "hid0": ["g3 dn"],
    "f18": ["sp dn 3210"],
    "b2": ["se dn 3"],
    "grad0": ["sp hi 3210", "se dn 2"],
    "grad1": ["sp up 3"],
    "norm0": ["sf dn"],
    "b4": ["se hi 3"],
    "b5": ["se hi 2"],
    "b6": ["sp up 210"],
    "b8": ["sp gat 3210", "sp wo 3210"],
    "thru0": ["sf hi", "se up 3"],
    "b10": ["se up 2", "se gat 32"],
    "edge0": ["sp ra 32", "sp rb 32", "sf up"],
    "edge1": ["sp ra 10", "sp rb 10", "se ra 32", "se rb 3"],
    "taps1": ["se wo 32"],
    "b13": ["sp inp 3210"],
    "b14": ["se rb 2", "sf ra"],
    "first0": ["sf rb"],
    "t0": ["se inp 32", "sf gat", "sf wo", "end dn", "end hi", "end up", "sf inp", "end gat", "end ra", "end rb"],
    "t1": ["end wo", "end inp"],
}
F32, BF16 = (jnp.float32, jnp.bfloat16)
LANES = 128
EDGE = 8
STEP = 32
GROUP, RING = (4, 8)


def dot_nn(left, right):
    return lax.dot_general(left, right, (((1,), (0,)), ((), ())), preferred_element_type=F32)


def dot_nt(left, right):
    return lax.dot_general(left, right, (((1,), (1,)), ((), ())), preferred_element_type=F32)


def dot_tn(left, right):
    return lax.dot_general(left, right, (((0,), (0,)), ((), ())), preferred_element_type=F32)


def gelu_parts(value):
    rate = 0.7978845608028654
    square = value * value
    bent = jnp.tanh(rate * (value + 0.044715 * square * value))
    act = 0.5 * value * (1.0 + bent)
    slope = 0.5 * (1.0 + bent) + 0.5 * rate * value * (1.0 - bent * bent) * (1.0 + 0.134145 * square)
    return (act, slope)


def at(start, size, of):
    return pl.ds(pl.multiple_of(start, of), size)


def loop(count, body):
    def turn(i, nothing):
        body(i)
        return nothing

    lax.fori_loop(0, count, turn, 0)


class Net:
    def __init__(self, send, recv):
        self.send, self.recv, self.used, self.open = (send, recv, 0, {})

    def slots(self, count):
        first = self.used
        self.used += count
        return list(range(first, first + count))

    def put(self, src, dst, to, slot, tag=""):
        copy = pltpu.make_async_remote_copy(
            src_ref=src,
            dst_ref=dst,
            send_sem=self.send.at[slot],
            recv_sem=self.recv.at[slot],
            device_id=to,
            device_id_type=MESH,
        )
        copy.start()
        self.open.setdefault(tag, []).append(copy)

    def got(self, dst, to, slot):
        pltpu.make_async_remote_copy(
            src_ref=dst,
            dst_ref=dst,
            send_sem=self.send.at[slot],
            recv_sem=self.recv.at[slot],
            device_id=to,
            device_id_type=MESH,
        ).wait_recv()

    def flush(self, *tags):
        for tag in tags or list(self.open):
            for copy in self.open.pop(tag, []):
                copy.wait_send()


def fused(names, *refs):
    r = dict(zip(names, refs))
    out_hbm, gin_hbm, fin, fin_hu, g_o, g_d, g_vec = (
        r[k] for k in ("out", "gin", "fin", "fin_hu", "g_o", "g_d", "g_vec")
    )
    x, cot, out, gin, vec, gains = (r[k] for k in ("x", "cot", "out_own", "cot", "vec", "gains"))
    w_one, w_ri, w_o, w_hu, w_d = (r[k] for k in ("w_one", "w_ri", "w_o", "w_hu", "w_d"))
    norm, gout, norm_two, gres, conv, mix = (
        r[k] for k in ("norm", "gout", "norm_two", "gres", "conv", "mix")
    )
    prod, ghu, ggb, gri, part = (r[k] for k in ("prod", "ghu", "ggb", "gri", "part"))
    brx, tgx, stx, gate_pre, conv_out = (r[k] for k in ("brx", "tgx", "stx", "gate_pre", "conv_out"))
    rgate, igate, carry, pre = (r[k] for k in ("rgate", "igate", "carry", "pre"))
    core_in, x_in, pre_f, pre_b = (r[k] for k in ("core_in", "x_in", "pre_f", "pre_b"))
    acc, gain_acc, vs, vb = (r[k] for k in ("acc", "gain_acc", "vs", "vb"))
    net = Net(r["send"], r["recv"])

    width = x.shape[1]
    here = carry.shape[1]
    chans = carry.shape[2]
    hid = prod.shape[1]
    rows = 2 * GROUP
    half = GROUP * here
    blk, cblk, fblk = (width // (RING * GROUP), chans // RING, hid // RING)
    groups = [slice(g * LANES, (g + 1) * LANES) for g in range(chans // LANES)]
    marks = slice(chans, chans + LANES)

    s, b = (lax.axis_index("seq"), lax.axis_index("batch"))
    mate, across = (b + 1 - 2 * (b % 2), b + 2 - 4 * (b // 2))
    corner = across + 1 - 2 * (b % 2)
    to_mate, to_across, to_corner = ((s, mate), (s, across), (s, corner))
    group_peers = [(mate, to_mate), (across, to_across), (corner, to_corner)]
    flips = {"h": 4 - 8 * (s // 4), "l": 2 - 4 * (s // 2 % 2), "y": 1 - 2 * (s % 2)}

    def turned(axes):
        place = s
        for axis in axes:
            place = place + flips[axis]
        return place

    def reach(axes):
        return (turned(axes), b)

    ring_to = [lax.rem(s + k, RING) for k in range(RING)]
    ring_from = [lax.rem(s + RING - k, RING) for k in range(RING)]

    def ring_device(q):
        return (q, b)

    def fetch(slot, src, dst):
        copy = pltpu.make_async_copy(src, dst, r["local"].at[slot])
        copy.start()
        return copy

    raw = ghu
    sides = (slice(0, raw.shape[1]), slice(raw.shape[1], 2 * raw.shape[1]))
    spots, place = ({}, 0)
    fetched = {}
    for name, tall in (("w_gate", blk), ("w_input", blk), ("w_recur", cblk), ("w_inject", cblk)):
        spots[name] = place
        fetched[name] = [fetch(len(fetched), r["hbm_" + name], raw.at[pl.ds(place, tall)])]
        place += tall
    fetched["x"] = [fetch(4, r["hbm_x"], x)]
    fetched["seg"] = [fetch(5, r["hbm_seg"], r["seg"])]
    for k, name in enumerate(("gain_one", "gain_two")):
        fetched[name] = [fetch(6 + k, r["hbm_" + name], gains.at[k])]
    for k, name in enumerate(("w_hidden", "w_upward")):
        spots[name] = place
        fetched[name] = [
            fetch(8 + 2 * k + j, r["hbm_" + name].at[:, side], raw.at[pl.ds(place + j * blk, blk)])
            for j, side in enumerate(sides)
        ]
        place += 2 * blk
    fetched["own_o"] = [fetch(12, r["hbm_w_output"], w_o.at[at(s * cblk, cblk, 16)])]
    fetched["own_d"] = [fetch(13, r["hbm_w_down"], w_d.at[at(s * fblk, fblk, 16)])]
    fetched["vec"] = [fetch(14, r["hbm_conv_taps"], r["taps"])] + [
        fetch(15 + k, r["hbm_" + name], r["biases"].at[k])
        for k, name in enumerate(("conv_bias", "recur_bias", "inject_bias", "decay_param"))
    ]
    fetched["cot"] = [fetch(19, r["hbm_cot"], cot)]

    def fetch_wait(*which):
        for name in which:
            for copy in fetched[name]:
                copy.wait()

    barrier = pltpu.get_barrier_semaphore()
    for _, to in group_peers:
        pl.semaphore_signal(barrier, inc=1, device_id=to, device_id_type=MESH)
    for k in range(1, RING):
        pl.semaphore_signal(barrier, inc=1, device_id=ring_device(ring_to[k]), device_id_type=MESH)

    class Chunk:
        pass

    def chunk(axes, block, piece, pieces, first_sum, later_sum):
        c = Chunk()
        c.axes, c.back, c.block, c.piece, c.pieces = (axes[:3], axes[-3:], block, piece, pieces)
        c.first_sum, c.later_sum = (first_sum, later_sum)
        c.gather, c.sums = (net.slots(7), net.slots(7))
        c.spread, c.home = (net.slots(3), net.slots(3))
        return c

    def tall_chunk(axes, ref, size, first_ref, later_ref):
        return chunk(
            axes,
            lambda q: ref.at[at(q * size, size, 16)],
            lambda q, i: ref.at[at(q * size + i * 16, 16, 16)],
            size // 16,
            lambda k: first_ref.at[pl.ds(k * size, size)],
            lambda k: later_ref.at[pl.ds(k * size, size)],
        )

    def wide_chunk(axes, ref, cols, first_ref, later_ref):
        return chunk(
            axes,
            lambda q: ref.at[q, :, cols],
            lambda q, i: ref.at[q, at(i * 16, 16, 16), cols],
            GROUP * blk // 16,
            lambda k: first_ref.at[k],
            lambda k: later_ref.at[k],
        )

    class Late:
        def __init__(self, first, cols):
            self.first, self.cols, self.at = (first, cols, self)

        def __getitem__(self, k):
            size = GROUP * blk
            return norm_two.at[pl.ds((self.first + k) * size, size), self.cols]

    tokens = rows * here
    two = 2 * chans
    gate_side, in_side = (slice(0, chans), slice(chans, two))
    gat = wide_chunk("hly", w_one, gate_side, None, None)
    gat_sum = wide_chunk("hyl", r["dw_gate"], gate_side, Late(0, gate_side), Late(4, gate_side))
    inp = wide_chunk("hly", w_one, in_side, None, None)
    inp_sum = wide_chunk("hly", r["dw_in"], gate_side, Late(0, in_side), Late(4, in_side))
    def gate_chunk(axes, cols, first_ref, later_ref):
        return chunk(
            axes,
            lambda q: w_ri.at[:, q, :, cols],
            lambda q, i: w_ri.at[i, q, :, cols],
            GROUP,
            lambda k: first_ref.at[k],
            lambda k: later_ref.at[k],
        )

    ra = gate_chunk("hly hyl", gate_side, r["y_ra"], r["z_ra"])
    rb = gate_chunk("hyl hly", in_side, r["y_rb"], r["z_rb"])
    wo = tall_chunk("hly", w_o, cblk, r["y_o"], r["z_o"])
    hi = wide_chunk("hly", w_hu, slice(0, hid), r["y_h"], r["z_h"])
    up = wide_chunk("hly", w_hu, slice(hid, 2 * hid), r["y_u"], r["z_u"])
    dn = tall_chunk("hyl", w_d, fblk, None, None)
    dn_sum = tall_chunk("hyl", r["dw_d"], fblk, r["y_d"], r["z_d"])

    def cube_place(ref, cols):
        return lambda q: ref.at[s, at(q * blk, blk, 16), cols]

    rec = blk + cblk
    xhu = gri.at[pl.ds(GROUP * rec, 2 * GROUP * blk)]
    gat.source = lambda q: gri.at[at(q * rec, blk, 16), gate_side]
    gat.place = cube_place(w_one, gate_side)
    gat_sum.place = cube_place(r["dw_gate"], gate_side)
    gat_sum.result = lambda q: fin.at[at(q * rec, blk, 16), gate_side]
    inp.source = lambda q: gri.at[at(q * rec, blk, 16), in_side]
    inp.place = cube_place(w_one, in_side)
    inp_sum.place = cube_place(r["dw_in"], gate_side)
    inp_sum.result = lambda q: fin.at[at(q * rec, blk, 16), in_side]
    for c, cols in ((ra, gate_side), (rb, in_side)):
        c.source = lambda q, cols=cols: gri.at[at(q * rec + blk, cblk, 16), cols]
        c.place = lambda q, cols=cols: w_ri.at[q, s, :, cols]
        c.result = lambda q, cols=cols: fin.at[at(q * rec + blk, cblk, 16), cols]
    hi.source = lambda q: xhu.at[at(q * blk, blk, 16)]
    hi.place = cube_place(w_hu, slice(0, hid))
    hi.result = lambda q: fin_hu.at[at(q * blk, blk, 16), slice(0, hid)]
    up.source = lambda q: xhu.at[at((GROUP + q) * blk, blk, 16)]
    up.place = cube_place(w_hu, slice(hid, 2 * hid))
    up.result = lambda q: fin_hu.at[at(q * blk, blk, 16), slice(hid, 2 * hid)]

    def member_cols(array, q, parts):
        pieces = [array[:, parts * (GROUP * k + q) : parts * (GROUP * k + q + 1)] for k in range(RING)]
        return jnp.concatenate(pieces, axis=1)

    def prepare(c, tall, parts, *names):
        for q in range(GROUP):
            for k, name in enumerate(names):
                array = raw[spots[name] : spots[name] + tall, :]
                if array.shape[1] < RING * GROUP * parts:
                    array = jnp.concatenate([array, raw[spots[name] + tall : spots[name] + 2 * tall, :]], axis=1)
                c.source(q)[:, k * RING * parts : (k + 1) * RING * parts] = member_cols(array, q, parts)

    def spread(c):
        for (peer, to), slot in zip(group_peers, c.spread):
            net.put(c.source(peer), c.place(b), to, slot)
        c.place(b)[...] = c.source(b)[...]

    def spread_wait(c):
        for (peer, to), slot in zip(group_peers, c.spread):
            net.got(c.place(peer), to, slot)

    def g0(c, *which):
        for slot in which or range(3):
            axis = c.axes[slot]
            net.put(c.block(s), c.block(s), reach(axis), c.gather[slot])

    def g1(c):
        i, j, k = c.axes
        net.got(c.block(turned(i)), reach(i), c.gather[0])
        net.put(c.block(turned(i)), c.block(turned(i)), reach(j), c.gather[3])
        net.put(c.block(turned(i)), c.block(turned(i)), reach(k), c.gather[4])

    def g2(c):
        i, j, k = c.axes
        net.got(c.block(turned(j)), reach(j), c.gather[1])
        net.put(c.block(turned(j)), c.block(turned(j)), reach(k), c.gather[5])

    def g3(c):
        i, j, k = c.axes
        net.got(c.block(turned(i + j)), reach(j), c.gather[3])
        net.put(c.block(turned(i + j)), c.block(turned(i + j)), reach(k), c.gather[6])

    def gather_wait(c):
        i, j, k = c.axes
        for slot, axes in ((2, k), (4, i + k), (5, j + k), (6, i + j + k)):
            net.got(c.block(turned(axes)), reach(k), c.gather[slot])

    def sp(c, *which):
        i, j, k = c.back
        for slot in which:
            axes = ("", i, j, i + j)[slot]
            net.put(c.block(turned(axes + k)), c.first_sum(slot), reach(k), c.sums[slot], "sum")

    def added(c, axes, parts, keep):
        def add(i):
            total = c.piece(turned(axes), i)[...].astype(F32)
            for ref in parts:
                total = total + part_of(c, ref, i).astype(F32)
            keep(i, total)

        loop(c.pieces, add)

    def part_of(c, ref, i):
        if len(ref.shape) == 2:
            return ref[at(i * 16, 16, 16), :]
        return ref[i]

    def back_to(c, axes):
        def keep(i, total):
            c.piece(turned(axes), i)[...] = total.astype(BF16)

        return keep

    def se(c, *which):
        i, j, k = c.back
        for slot in which:
            axes = {2: j, 3: i + j}[slot]
            net.got(c.first_sum(slot), reach(k), c.sums[slot])
            added(c, axes, [c.first_sum(slot)], back_to(c, axes))
            net.put(c.block(turned(axes)), c.later_sum(slot - 2), reach(j), c.sums[slot + 2], "sum")

    def sf(c):
        i, j, k = c.back
        net.got(c.first_sum(1), reach(k), c.sums[1])
        net.got(c.later_sum(1), reach(j), c.sums[5])
        added(c, i, [c.first_sum(1), c.later_sum(1)], back_to(c, i))
        net.put(c.block(turned(i)), c.later_sum(2), reach(i), c.sums[6], "sum")

    def sum_end(c, keep):
        i, j, k = c.back
        net.got(c.first_sum(0), reach(k), c.sums[0])
        net.got(c.later_sum(0), reach(j), c.sums[4])
        net.got(c.later_sum(2), reach(i), c.sums[6])
        added(c, "", [c.first_sum(0), c.later_sum(0), c.later_sum(2)], keep)

    def sum_end_spread(c):
        sum_end(c, back_to(c, ""))
        for (peer, to), slot in zip(group_peers, c.home):
            net.put(c.place(peer), c.result(b), to, slot)
        c.result(b)[...] = c.place(b)[...]

    def home_wait(c):
        for (peer, to), slot in zip(group_peers, c.home):
            net.got(c.result(peer), to, slot)

    def share(view, slots, h):
        net.put(view(b, h), view(b, h), to_across, slots[3 * h])
        net.put(view(b, h), view(b, h), to_mate, slots[3 * h + 1])

    def share_relay(view, slots, h):
        net.got(view(across, h), to_across, slots[3 * h])
        net.put(view(across, h), view(across, h), to_mate, slots[3 * h + 2])

    def share_end(view, slots, h):
        net.got(view(mate, h), to_mate, slots[3 * h + 1])
        net.got(view(corner, h), to_mate, slots[3 * h + 2])

    def token_rows(ref):
        return lambda q, h: ref.at[at((h * GROUP + q) * here, here, 16)]

    def merge(view, first, slots, h, tag="part"):
        net.put(view(corner, h), first(h, 1), to_mate, slots[3 * h], tag)
        net.put(view(mate, h), first(h, 0), to_mate, slots[3 * h + 1], tag)

    def merge_relay(view, first, second, slots, h, parts, tile, tag="part"):
        net.got(first(h, 1), to_mate, slots[3 * h])

        def add(i):
            v = tile(view(across, h), i)
            v[...] = (v[...].astype(F32) + tile(first(h, 1), i)[...].astype(F32)).astype(BF16)

        loop(parts, add)
        net.put(view(across, h), second(h), to_across, slots[3 * h + 2], tag)

    def merge_end(first, second, slots, h):
        net.got(first(h, 0), to_mate, slots[3 * h + 1])
        net.got(second(h), to_across, slots[3 * h + 2])

    def sixteen(ref, i):
        return ref.at[at(i * 16, 16, 16)]

    first_in = lambda h, slot: core_in.at[h, slot]
    second_in = lambda h: x_in.at[h]
    part_rows = token_rows(part)

    def merged(h, i):
        total = sixteen(part_rows(b, h), i)[...].astype(F32)
        return total + core_in[h, 0, at(i * 16, 16, 16)].astype(F32) + x_in[h, at(i * 16, 16, 16)].astype(F32)

    def own(ref, h, i):
        return ref.at[at(h * here + i * 16, 16, 16)]

    tiles16 = here // 16

    def rms(values):
        return lax.rsqrt(jnp.mean(values * values, axis=-1, keepdims=True) + EPSILON)

    def norm_grad(index, values, incoming, gain):
        scaler = rms(values)
        scaled = incoming * gain
        inner = jnp.mean(scaled * values, axis=-1, keepdims=True)
        term = incoming * values * scaler
        gain_acc[index] += term[0:8] + term[8:16]
        return scaler * (scaled - values * (scaler * scaler * inner))

    def over(h, body, starts=range(0, here, STEP)):
        def row(i):
            q = h * GROUP + i
            for start in starts:
                for g, lanes in enumerate(groups):
                    body(q, start, lanes, g)

        loop(GROUP, row)

    def flat(q, start):
        return at(q * here + start, STEP, STEP)

    def add_to(index, lanes, values):
        total = values[0:8]
        for k in range(8, STEP, 8):
            total = total + values[k : k + 8]
        acc[index, :, lanes] += total

    def same(q, start, k):
        now = brx[q, pl.ds(EDGE + start, STEP), marks]
        return (now == brx[q, pl.ds(EDGE + start - k, STEP), marks]).astype(F32)

    def keep_down(i, total):
        g_d[at(i * 16, 16, 16), :] = total

    def keep_out(i, total):
        g_o[at(i * 16, 16, 16), :] = total

    def finish_sum(c):
        if c is dn:
            sum_end(dn_sum, keep_down)
        elif c is wo:
            sum_end(wo, keep_out)
        else:
            sum_end_spread(summing.get(c, c))

    moved = {"inp": inp, "gat": gat, "ra": ra, "rb": rb, "wo": wo, "hi": hi, "up": up, "dn": dn}
    summing = {gat: gat_sum, inp: inp_sum, dn: dn_sum}
    acts = {
        "wait": spread_wait,
        "g0": g0,
        "g1": g1,
        "g2": g2,
        "g3": g3,
        "sp": lambda c, *which: sp(summing.get(c, c), *which),
        "se": lambda c, *which: se(summing.get(c, c), *which),
        "sf": lambda c: sf(summing.get(c, c)),
        "end": finish_sum,
    }

    def tick(name):
        for event in PLAN.get(name, ()):
            act, which, *slots = event.split()
            acts[act](moved[which], *map(int, "".join(slots)))

    norm_slots, gout_slots, conv_slots = (net.slots(6), net.slots(6), net.slots(6))
    two_slots, gres_slots = (net.slots(6), net.slots(6))
    out_slots, gnt_slots, down_slots, thru_slots, gn_slots = (net.slots(6) for _ in range(5))
    halo_slots, halo_back = (net.slots(2), net.slots(2))
    pre_slots, back_slots, vec_slots, last_slots = (
        net.slots(RING),
        net.slots(RING),
        net.slots(RING),
        net.slots(3),
    )
    norm_rows, gout_rows, two_rows, gres_rows = (token_rows(ref) for ref in (norm, gout, norm_two, gres))
    conv_cols = lambda q, h: conv.at[pl.ds(h * half, half), at(q * chans, chans, LANES)]

    fetch_wait("w_input", "own_o")
    prepare(inp, blk, cblk, "w_input")
    fetch_wait("x", "seg", "gain_one", "gain_two")
    gain_one, gain_two = (gains[0:1], gains[1:2])
    pl.semaphore_wait(barrier, 3 + RING - 1)
    spread(inp)

    def norm_half(h):
        ids = r["seg"][h : h + 1, :].astype(F32)
        norm[at((h * GROUP + b) * here, here, 16), width : width + LANES] = jnp.transpose(
            jnp.broadcast_to(ids, (here, here))
        ).astype(BF16)

        def norm_tile(i):
            v = own(x, h, i)[...]
            sixteen(norm_rows(b, h), i)[:, 0:width] = (v * rms(v) * gain_one).astype(BF16)

        loop(tiles16, norm_tile)

    fetch_wait("w_gate")
    prepare(gat, blk, cblk, "w_gate")
    spread(gat)
    fetch_wait("w_recur")
    prepare(ra, cblk, cblk, "w_recur")
    spread(ra)
    fetch_wait("w_inject")
    prepare(rb, cblk, cblk, "w_inject")
    spread(rb)
    tick("f1")
    norm_half(0)
    share(norm_rows, norm_slots, 0)
    tick("f2")
    norm_half(1)
    share(norm_rows, norm_slots, 1)
    tick("f3")
    fetch_wait("w_hidden")
    prepare(hi, blk, fblk, "w_hidden")
    tick("f4")
    spread(hi)
    tick("f5")
    fetch_wait("w_upward")
    prepare(up, blk, fblk, "w_upward")
    spread(up)
    tick("f6")

    fetch_wait("vec")
    log_of = lambda grown: jnp.log(grown)
    biases = jnp.concatenate([r["biases"][k].reshape(1, -1) for k in range(4)], axis=0)
    small = jnp.exp(biases[3:4])
    grown = 1.0 + small
    rate = jnp.where(grown == 1.0, small, log_of(grown) * small / jnp.where(grown == 1.0, 1.0, grown - 1.0))
    sources = jnp.concatenate([r["taps"][...], biases[0:3], -DECAY_SCALE * rate], axis=0)
    for q in range(GROUP):
        r["vecs"][q, 0:8] = member_cols(sources, q, cblk)
        r["vecs"][q, 8:16] = member_cols(jnp.broadcast_to(jax.nn.sigmoid(biases[3:4]), (8, GROUP * chans)), q, cblk)
    vec[...] = r["vecs"][b]
    acc[...] = jnp.zeros_like(acc)
    gain_acc[...] = jnp.zeros_like(gain_acc)

    @pl.when(s == 0)
    def _():
        brx[:, 0:EDGE, :] = jnp.full((rows, EDGE, chans + LANES), -1.0, F32)

    @pl.when(s == RING - 1)
    def _():
        tgx[:, here : here + EDGE, :] = jnp.full((rows, EDGE, chans + LANES), -1.0, F32)

    share_relay(norm_rows, norm_slots, 0)
    tick("f7")
    fetch_wait("cot", "own_d")
    for h in range(2):
        def low_tile(i, h=h):
            sixteen(gout_rows(b, h), i)[...] = own(cot, h, i)[...].astype(BF16)

        loop(tiles16, low_tile)
    tick("f8")
    gather_wait(inp)
    share_end(norm_rows, norm_slots, 0)

    def edge_copies(ref, src, dst, slots, step, gives, takes):
        def copy(h, where):
            block = pl.ds(h * GROUP, GROUP)
            return pltpu.make_async_remote_copy(
                src_ref=ref.at[block, pl.ds(src, EDGE)],
                dst_ref=ref.at[block, pl.ds(dst, EDGE)],
                send_sem=net.send.at[slots[h]],
                recv_sem=net.recv.at[slots[h]],
                device_id=(where, b),
                device_id_type=MESH,
            )

        def out(h):
            @pl.when(gives)
            def _():
                copy(h, lax.rem(s + step, RING)).start()

        def arrive(h):
            @pl.when(takes)
            def _():
                copy(h, lax.rem(s + RING - step, RING)).wait_recv()

        def left():
            @pl.when(gives)
            def _():
                for h in range(2):
                    copy(h, lax.rem(s + step, RING)).wait_send()

        return (out, arrive, left)


    edge_out, edge_in, edge_left = edge_copies(brx, here, 0, halo_slots, 1, s < RING - 1, s > 0)
    for h in range(2):
        if h:
            share_relay(norm_rows, norm_slots, h)
            share_end(norm_rows, norm_slots, h)
        span = pl.ds(h * half, half)
        block = slice(h * GROUP, (h + 1) * GROUP)
        got = dot_nn(norm[span, 0:width], w_one[:, :, in_side].reshape(width, chans))
        brx[block, EDGE : EDGE + here, 0:chans] = got.reshape(GROUP, here, chans)
        ids = norm[span, width : width + LANES].astype(F32).reshape(GROUP, here, LANES)
        brx[block, EDGE : EDGE + here, marks] = ids
        tgx[block, 0:here, marks] = ids
        edge_out(h)
        tick(f"f9{h}")

    def conv_tile(q, start, lanes, g):
        total = vec[4:5, lanes] + vec[0:1, lanes] * brx[q, pl.ds(EDGE + start, STEP), lanes]
        for k in range(1, 4):
            lag = brx[q, pl.ds(EDGE + start - k, STEP), lanes]
            total = total + vec[k : k + 1, lanes] * lag * same(q, start, k)
        conv_out[q, pl.ds(start, STEP), lanes] = total
        conv[flat(q, start), at(b * chans + g * LANES, LANES, LANES)] = total.astype(BF16)

    for h in range(2):
        over(h, conv_tile, range(STEP, here, STEP))
    for h in range(2):
        edge_in(h)
        over(h, conv_tile, [0])
        share(conv_cols, conv_slots, h)
        tick(f"conv{h}")
    share_relay(conv_cols, conv_slots, 0)
    tick("f10")
    share_relay(conv_cols, conv_slots, 1)
    tick("f11")
    share_end(conv_cols, conv_slots, 0)
    gather_wait(ra)
    gather_wait(rb)

    for h in range(2):
        if h:
            share_end(conv_cols, conv_slots, h)
        block = slice(h * GROUP, (h + 1) * GROUP)
        got = dot_nn(conv[pl.ds(h * half, half), :], w_ri[...].reshape(GROUP * chans, two))
        got = got.reshape(GROUP, here, two)
        rgate[block] = got[:, :, 0:chans]
        igate[block] = got[:, :, chans:two]

        def gate_tile(q, start, lanes, g):
            span = pl.ds(start, STEP)
            rg = jax.nn.sigmoid(rgate[q, span, lanes] + vec[5:6, lanes])
            ig = jax.nn.sigmoid(igate[q, span, lanes] + vec[6:7, lanes])
            rgate[q, span, lanes] = rg
            igate[q, span, lanes] = ig
            decay = jnp.exp(rg * vec[7:8, lanes])
            carry[q, span, lanes] = decay * same(q, start, 1)
            scale = jnp.sqrt(1.0 - decay * decay + FLOOR_TERM)
            stx[q, pl.ds(EDGE + start, STEP), lanes] = scale * ig * conv_out[q, span, lanes]

        over(h, gate_tile)
        tick(f"gate{h}")

    def ends(p, state):
        mult = carry[:, p, :]
        return (state[0] * mult, mult * state[1] + stx[:, EDGE + p, :])

    begin = (jnp.ones((rows, chans), F32), jnp.zeros((rows, chans), F32))
    product, tail = lax.fori_loop(0, here, ends, begin, unroll=8)
    def hand_round(ref, product, tail, slots):
        ref[s, 0:rows] = product
        ref[s, rows : 2 * rows] = tail
        for k in range(1, RING):
            net.put(ref.at[s], ref.at[s], ring_device(ring_to[k]), slots[k])

    def entering(ref, slots, forward):
        for k in range(1, RING):
            net.got(ref.at[ring_from[k]], ring_device(ring_from[k]), slots[k])
        state = jnp.zeros((rows, chans), F32)
        for q in range(RING - 1) if forward else range(RING - 1, 0, -1):
            longer = ref[q, rows : 2 * rows] + ref[q, 0:rows] * state
            state = jnp.where(q < s if forward else q > s, longer, state)
        return state

    hand_round(pre_f, product, tail, pre_slots)
    tick("f12")
    gather_wait(gat)

    for h in range(2):
        got = dot_nn(norm[pl.ds(h * half, half), 0:width], w_one[:, :, gate_side].reshape(width, chans))
        gate_pre[h * GROUP : (h + 1) * GROUP] = got.reshape(GROUP, here, chans)

        def act_tile(q, start, lanes, g):
            span = pl.ds(start, STEP)
            tgx[q, span, lanes] = gelu_parts(gate_pre[q, span, lanes])[0]

        over(h, act_tile)
        tick(f"act{h}")
    state = entering(pre_f, pre_slots, True)
    stx[:, EDGE - 1, :] = state

    def scan(p, state):
        state = carry[:, p, :] * state + stx[:, EDGE + p, :]
        stx[:, EDGE + p, :] = state
        return state

    lax.fori_loop(0, here, scan, state, unroll=8)
    tick("f13")
    gather_wait(wo)

    for h in range(2):
        def mix_tile(q, start, lanes, g):
            act = tgx[q, pl.ds(start, STEP), lanes]
            mix[flat(q, start), lanes] = (stx[q, pl.ds(EDGE + start, STEP), lanes] * act).astype(BF16)

        over(h, mix_tile)
        span = pl.ds(h * half, half)
        part[span, :] = dot_nn(mix[span, :], w_o[...]).astype(BF16)
        merge(part_rows, first_in, out_slots, h)
        tick(f"mix{h}")
    for h in range(2):
        merge_relay(part_rows, first_in, second_in, out_slots, h, tiles16, sixteen)
    tick("f14")
    for h in range(2):
        merge_end(first_in, second_in, out_slots, h)

        def resid_tile(i, h=h):
            v = own(x, h, i)[...] + merged(h, i)
            own(out, h, i)[...] = v
            sixteen(two_rows(b, h), i)[...] = (v * rms(v) * gain_two).astype(BF16)

        loop(tiles16, resid_tile)
        share(two_rows, two_slots, h)
        tick(f"resid{h}")
    for h in range(2):
        share(gout_rows, gout_slots, h)
    tick("f15")
    share_relay(two_rows, two_slots, 0)
    tick("f16")
    share_relay(two_rows, two_slots, 1)
    tick("f17")
    gather_wait(hi)
    gather_wait(up)

    for h in range(2):
        share_end(two_rows, two_slots, h)
        span = pl.ds(h * half, half)
        for j in range(hid // 256):
            left = slice(j * 256, j * 256 + 256)
            right = slice(hid + j * 256, hid + j * 256 + 256)
            pre[:, 0:256] = dot_nn(norm_two[span, :], w_hu[:, :, left].reshape(width, 256))
            pre[:, 256:512] = dot_nn(norm_two[span, :], w_hu[:, :, right].reshape(width, 256))

            def tile(i, h=h, j=j):
                rows_t = at(i * STEP, STEP, STEP)
                flat_t = at(h * half + i * STEP, STEP, STEP)
                for g in range(2):
                    first = slice(j * 256 + g * LANES, j * 256 + (g + 1) * LANES)
                    second = slice(hid + j * 256 + g * LANES, hid + j * 256 + (g + 1) * LANES)
                    act, slope = gelu_parts(pre[rows_t, g * LANES : (g + 1) * LANES])
                    upward = pre[rows_t, 256 + g * LANES : 256 + (g + 1) * LANES]
                    prod[flat_t, first] = (act * upward).astype(BF16)
                    ghu[flat_t, first] = (upward * slope).astype(BF16)
                    ghu[flat_t, second] = act.astype(BF16)

            loop(half // STEP, tile)
        share_relay(gout_rows, gout_slots, h)
        tick(f"hid{h}")
    for h in range(2):
        share_end(gout_rows, gout_slots, h)
    for j in range(2):
        cols = slice(j * hid // 2, (j + 1) * hid // 2)
        r["dw_d"][cols, :] = dot_tn(prod[:, cols], gout[...]).astype(BF16)
    tick("f18")
    gather_wait(dn)

    net.flush("part")
    for h in range(2):
        span = pl.ds(h * half, half)
        for j in range(hid // 256):
            left = slice(j * 256, j * 256 + 256)
            right = slice(hid + j * 256, hid + j * 256 + 256)
            back = dot_nt(gout[span, :], w_d[left, :])
            ghu[span, left] = (back * ghu[span, left].astype(F32)).astype(BF16)
            ghu[span, right] = (back * ghu[span, right].astype(F32)).astype(BF16)
        for j in range(2):
            cols = slice(j * width // 2, (j + 1) * width // 2)
            part[span, cols] = dot_nt(ghu[span, :], w_hu[4 * j : 4 * j + 4].reshape(width // 2, 2 * hid)).astype(BF16)
        merge(part_rows, first_in, gnt_slots, h)
        tick(f"back{h}")
    for h in range(2):
        merge_relay(part_rows, first_in, second_in, gnt_slots, h, tiles16, sixteen)
    tick("b2")

    net.flush("")
    for j in range(2):
        def grad_hu(i, j=j):
            cols = at(i * 256, 256, LANES)
            side = slice(j * hid, (j + 1) * hid)
            got = dot_tn(norm_two[:, cols], ghu[:, side]).astype(BF16)
            w_hu[pl.ds(2 * i, 2), :, side] = got.reshape(2, GROUP * blk, hid)

        loop(width // 256, grad_hu)
        tick(f"grad{j}")

    for h in range(2):
        merge_end(first_in, second_in, gnt_slots, h)

        def second_norm(i, h=h):
            back = norm_grad(1, own(out, h, i)[...], merged(h, i), gain_two)
            total = own(cot, h, i)[...] + back
            own(gin, h, i)[...] = total
            sixteen(gres_rows(b, h), i)[...] = total.astype(BF16)

        loop(tiles16, second_norm)
        share(gres_rows, gres_slots, h)
        tick(f"norm{h}")
    net.flush("part")
    for h in range(2):
        span = pl.ds(h * half, half)
        part[span, :] = dot_nn(prod[span, :], w_d[...]).astype(BF16)
    tick("b3")
    share_relay(gres_rows, gres_slots, 0)
    tick("b4")
    share_relay(gres_rows, gres_slots, 1)
    tick("b5")

    for h in range(2):
        share_end(gres_rows, gres_slots, h)
        if h:
            for k in range(2):
                merge(part_rows, first_in, down_slots, k)
        block = slice(h * GROUP, (h + 1) * GROUP)
        got = dot_nt(gres[pl.ds(h * half, half), :], w_o[...])
        tgx[block, 0:here, 0:chans] = got.reshape(GROUP, here, chans)
        if h:
            for k in range(2):
                merge_relay(part_rows, first_in, second_in, down_slots, k, tiles16, sixteen)

        def mix_back(q, start, lanes, g):
            span = pl.ds(start, STEP)
            act, slope = gelu_parts(gate_pre[q, span, lanes])
            back = tgx[q, span, lanes]
            states = stx[q, pl.ds(EDGE + start, STEP), lanes]
            ggb[flat(q, start), lanes] = (back * states * slope).astype(BF16)
            tgx[q, span, lanes] = back * act

        over(h, mix_back)
        tick(f"mixb{h}")

    def ends_back(i, state):
        p = here - 1 - i
        mult = carry[:, p, :]
        return (state[0] * mult, mult * (tgx[:, p, 0:chans] + state[1]))

    product, tail = lax.fori_loop(0, here, ends_back, begin, unroll=8)
    hand_round(pre_b, product, tail, back_slots)
    tick("b6")

    w_o[...] = dot_tn(mix[...], gres[...]).astype(BF16)
    for j in range(2):
        cols = slice(j * width // 2, (j + 1) * width // 2)
        got = dot_tn(norm[:, cols], ggb[:, gate_side]).astype(BF16)
        r["dw_gate"][4 * j : 4 * j + 4] = got.reshape(4, GROUP * blk, chans)

    tick("b7")
    state = entering(pre_b, back_slots, False)

    def scan_back(i, state):
        p = here - 1 - i
        total = tgx[:, p, 0:chans] + state
        tgx[:, p, 0:chans] = total
        return carry[:, p, :] * total

    lax.fori_loop(0, here, scan_back, state, unroll=8)

    tick("b8")
    thru_cols = lambda q, h: ghu.at[pl.ds(h * half, half), at(q * chans, chans, LANES)]
    thru_first = lambda h, slot: prod.at[pl.ds(h * half, half), pl.ds(slot * chans, chans)]
    thru_second = lambda h: gout.at[pl.ds(h * half, half), pl.ds(0, chans)]
    for h in range(2):
        def gates_back(q, start, lanes, g):
            span = pl.ds(start, STEP)
            total = tgx[q, span, lanes]
            rg, ig, co = (rgate[q, span, lanes], igate[q, span, lanes], conv_out[q, span, lanes])
            before = stx[q, pl.ds(EDGE + start - 1, STEP), lanes]
            rate = vec[7:8, lanes]
            decay = jnp.exp(rg * rate)
            scale = jnp.sqrt(1.0 - decay * decay + FLOOR_TERM)
            grad_decay = total * before * same(q, start, 1) - total * ig * co * decay / scale
            grad_log = grad_decay * decay
            grad_rg = grad_log * rate * rg * (1.0 - rg)
            scaled = total * scale
            grad_ig = scaled * co * ig * (1.0 - ig)
            tgx[q, span, lanes] = scaled * ig
            gri[flat(q, start), lanes] = grad_rg.astype(BF16)
            gri[flat(q, start), slice(chans + g * LANES, chans + (g + 1) * LANES)] = grad_ig.astype(BF16)
            add_to(5, lanes, grad_rg)
            add_to(6, lanes, grad_ig)
            add_to(7, lanes, grad_log * (-DECAY_SCALE * rg))

        over(h, gates_back)
        span = pl.ds(h * half, half)
        for j in range(2):
            pair = slice(2 * j, 2 * j + 2)
            got = dot_nt(gri[span, :], w_ri[pair].reshape(2 * chans, two))
            ghu[span, 2 * j * chans : 2 * (j + 1) * chans] = got.astype(BF16)
        if h == 0:
            for k in range(2):
                merge_end(first_in, second_in, down_slots, k)

                def out_tile(i, k=k):
                    own(out, k, i)[...] = own(out, k, i)[...] + merged(k, i)

                loop(tiles16, out_tile)
        merge(thru_cols, thru_first, thru_slots, h, "thru")
        tick(f"thru{h}")
    leave_out = fetch(0, out, out_hbm)
    for h in range(2):
        merge_relay(thru_cols, thru_first, thru_second, thru_slots, h, half // 16, sixteen, "thru")
    tick("b9")

    def grad_ri(i):
        got = dot_tn(conv[:, at(i * chans, chans, LANES)], gri[...])
        w_ri[i] = got.astype(BF16).reshape(RING, cblk, two)

    loop(GROUP, grad_ri)
    tick("b10")

    head_out, head_in, head_left = edge_copies(tgx, 0, here, halo_back, RING - 1, s > 0, s < RING - 1)

    def conv_grad(q, start, lanes, g):
        span = flat(q, start)
        total = ghu[span, at(b * chans + g * LANES, LANES, LANES)].astype(F32)
        total = total + prod[span, lanes].astype(F32) + gout[span, lanes].astype(F32)
        tgx[q, pl.ds(start, STEP), lanes] += total

    def conv_back(q, start, lanes, g):
        now = tgx[q, pl.ds(start, STEP), lanes]
        ids = tgx[q, pl.ds(start, STEP), marks]
        total = vec[0:1, lanes] * now
        add_to(4, lanes, now)
        add_to(0, lanes, now * brx[q, pl.ds(EDGE + start, STEP), lanes])
        for k in range(1, 4):
            later = pl.ds(start + k, STEP)
            match = (tgx[q, later, marks] == ids).astype(F32)
            total = total + vec[k : k + 1, lanes] * tgx[q, later, lanes] * match
            lag = brx[q, pl.ds(EDGE + start - k, STEP), lanes]
            add_to(k, lanes, now * lag * same(q, start, k))
        ggb[flat(q, start), slice(chans + g * LANES, chans + (g + 1) * LANES)] = total.astype(BF16)

    net.flush("part")
    for h in range(2):
        merge_end(thru_first, thru_second, thru_slots, h)
        over(h, conv_grad)
        head_out(h)
        tick(f"edge{h}")
        over(h, conv_back, range(0, here - STEP, STEP))
        head_in(h)
        over(h, conv_back, [here - STEP])
        tick(f"taps{h}")
        span = pl.ds(h * half, half)
        for j in range(2):
            cols = slice(j * width // 2, (j + 1) * width // 2)
            part[span, cols] = dot_nt(ggb[span, :], w_one[4 * j : 4 * j + 4].reshape(width // 2, two)).astype(BF16)
        merge(part_rows, first_in, gn_slots, h)
        tick(f"gain{h}")
        if h == 0:
            merge_relay(part_rows, first_in, second_in, gn_slots, h, tiles16, sixteen)
    for j in range(2):
        cols = slice(j * width // 2, (j + 1) * width // 2)
        got = dot_tn(norm[:, cols], ggb[:, in_side]).astype(BF16)
        r["dw_in"][4 * j : 4 * j + 4] = got.reshape(4, GROUP * blk, chans)
    tick("b13")
    merge_relay(part_rows, first_in, second_in, gn_slots, 1, tiles16, sixteen)
    tick("b14")


    for h in range(2):
        merge_end(first_in, second_in, gn_slots, h)

        def first_norm(i, h=h):
            back = norm_grad(0, own(x, h, i)[...], merged(h, i), gain_one)
            own(gin, h, i)[...] = own(gin, h, i)[...] + back

        loop(tiles16, first_norm)
        tick(f"first{h}")
    leave_gin = fetch(1, gin, gin_hbm)

    for k in range(8):
        total = jnp.sum(acc[k], axis=0, keepdims=True)
        vs[s, k : k + 1, 0:chans] = total * vec[8:9, :] if k == 7 else total
    piece = width // 4
    for k in range(2):
        total = jnp.sum(gain_acc[k], axis=0, keepdims=True)
        for j in range(4):
            vs[s, 4 * k + j : 4 * k + j + 1, chans : chans + piece] = total[:, j * piece : (j + 1) * piece]
    for k in range(1, RING):
        net.put(vs.at[s], vs.at[s], ring_device(ring_to[k]), vec_slots[k])

    tick("t0")
    for k in range(1, RING):
        net.got(vs.at[ring_from[k]], ring_device(ring_from[k]), vec_slots[k])
    total = vs[0]
    for q in range(1, RING):
        total = total + vs[q]
    vb[b] = total
    for (peer, to), slot in zip(group_peers, last_slots):
        net.put(vb.at[b], vb.at[b], to, slot)
    tick("t1")
    for (peer, to), slot in zip(group_peers, last_slots):
        net.got(vb.at[peer], to, slot)
    g_vec[:, 0:chans] = total[:, 0:chans]
    summed = vb[0, :, chans : chans + piece]
    for q in range(1, GROUP):
        summed = summed + vb[q, :, chans : chans + piece]
    g_vec[:, chans : chans + piece] = summed
    for c in (hi, up, gat_sum, ra, rb, inp_sum):
        home_wait(c)
    net.flush()
    leave_out.wait()
    leave_gin.wait()

    edge_left()
    head_left()


def finish(names, *refs):
    r = dict(zip(names, refs))
    r["to_o"][...] = r["g_o"][...]
    r["to_d"][...] = r["g_d"][...]
    place = lax.axis_index("seq") * GROUP + lax.axis_index("batch")
    s = lax.axis_index("seq")
    blk, cblk, fblk = (r["to_gate"].shape[0], r["to_recur"].shape[0], r["to_d"].shape[0])
    chans, hid = (RING * cblk, RING * fblk)
    rec = blk + cblk

    def joined(pieces, parts):
        pieces = [piece.astype(F32) for piece in pieces]
        return jnp.concatenate(
            [pieces[q][:, k * parts : (k + 1) * parts] for k in range(RING) for q in range(GROUP)], axis=1
        )

    fin, fin_hu, g_vec = (r["fin"], r["fin_hu"], r["g_vec"])
    for name, first, tall, left in (
        ("to_gate", 0, blk, 0),
        ("to_input", 0, blk, chans),
        ("to_recur", blk, cblk, 0),
        ("to_inject", blk, cblk, chans),
    ):
        spans = [slice(q * rec + first, q * rec + first + tall) for q in range(GROUP)]
        r[name][...] = joined([fin[span, left : left + chans] for span in spans], cblk)
    for name, left in (("to_hidden", 0), ("to_upward", hid)):
        spans = [slice(q * blk, (q + 1) * blk) for q in range(GROUP)]
        r[name][...] = joined([fin_hu[span, left : left + hid] for span in spans], fblk)
    vectors = g_vec[:, 0:chans]
    mine = vectors[:, 0:cblk]
    for k in range(1, RING):
        mine = jnp.where(k == s, vectors[:, k * cblk : (k + 1) * cblk], mine)
    r["to_taps"][...] = mine[0:4]
    for k, name in enumerate(("to_cbias", "to_rbias", "to_ibias", "to_decay")):
        r[name][...] = mine[4 + k]
    piece = g_vec.shape[1] - chans
    for k, name in enumerate(("to_gain_one", "to_gain_two")):
        total = jnp.zeros((1, blk), F32)
        for j in range(4):
            for m in range(piece // blk):
                part = g_vec[4 * k + j : 4 * k + j + 1, chans + m * blk : chans + (m + 1) * blk]
                total = jnp.where(j * (piece // blk) + m == place, part, total)
        r[name][...] = total[0]


def split_block(
    inputs,
    segments,
    w_gate,
    w_input,
    w_recur,
    w_inject,
    w_output,
    w_hidden,
    w_upward,
    w_down,
    gain_one,
    gain_two,
    conv_taps,
    conv_bias,
    recur_bias,
    inject_bias,
    decay_param,
    cotangent,
):
    count, here, width = inputs.shape
    channels = w_gate.shape[1]
    chans, hid = (channels // GROUP, w_hidden.shape[1] // GROUP)
    blk, cblk, fblk = (w_gate.shape[0], w_recur.shape[0], w_down.shape[0])
    tokens = GROUP * count * here
    rows = GROUP * count
    wide = chans + LANES
    operands = {
        "hbm_x": inputs.reshape(count * here, width),
        "hbm_cot": cotangent.reshape(count * here, width),
        "hbm_seg": segments,
        "hbm_w_gate": w_gate,
        "hbm_w_input": w_input,
        "hbm_w_recur": w_recur,
        "hbm_w_inject": w_inject,
        "hbm_w_output": w_output,
        "hbm_w_hidden": w_hidden,
        "hbm_w_upward": w_upward,
        "hbm_w_down": w_down,
        "hbm_gain_one": gain_one,
        "hbm_gain_two": gain_two,
        "hbm_conv_taps": conv_taps,
        "hbm_conv_bias": conv_bias,
        "hbm_recur_bias": recur_bias,
        "hbm_inject_bias": inject_bias,
        "hbm_decay_param": decay_param,
    }
    piece = width // 4
    outputs = {
        "out": ((count * here, width), F32),
        "gin": ((count * here, width), F32),
        "fin": ((GROUP * (blk + cblk), 2 * chans), BF16),
        "fin_hu": ((GROUP * blk, 2 * hid), BF16),
        "g_o": ((cblk, width), F32),
        "g_d": ((fblk, width), F32),
        "g_vec": ((8, chans + piece), F32),
    }
    scratch = {
        "x": ((count * here, width), F32),
        "cot": ((count * here, width), F32),
        "out_own": ((count * here, width), F32),
        "seg": (segments.shape, jnp.int32),
        "gains": ((2, width), F32),
        "taps": (conv_taps.shape, F32),
        "biases": ((4, channels), F32),
        "vecs": ((GROUP, 16, chans), F32),
        "vec": ((16, chans), F32),
        "w_one": ((RING, GROUP * blk, 2 * chans), BF16),
        "dw_gate": ((RING, GROUP * blk, chans), BF16),
        "dw_in": ((RING, GROUP * blk, chans), BF16),
        "dw_d": ((hid, width), BF16),
        "w_ri": ((GROUP, RING, cblk, 2 * chans), BF16),
        "w_o": ((chans, width), BF16),
        "w_hu": ((RING, GROUP * blk, 2 * hid), BF16),
        "w_d": ((hid, width), BF16),
        "norm": ((tokens, width + LANES), BF16),
        "gout": ((tokens, width), BF16),
        "norm_two": ((tokens, width), BF16),
        "gres": ((tokens, width), BF16),
        "conv": ((tokens, channels), BF16),
        "mix": ((tokens, chans), BF16),
        "prod": ((tokens, hid), BF16),
        "ghu": ((tokens, 2 * hid), BF16),
        "ggb": ((tokens, 2 * chans), BF16),
        "gri": ((tokens, 2 * chans), BF16),
        "part": ((tokens, width), BF16),
        "brx": ((rows, EDGE + here, wide), F32),
        "tgx": ((rows, here + EDGE, wide), F32),
        "stx": ((rows, EDGE + here, chans), F32),
        "gate_pre": ((rows, here, chans), F32),
        "conv_out": ((rows, here, chans), F32),
        "rgate": ((rows, here, chans), F32),
        "igate": ((rows, here, chans), F32),
        "carry": ((rows, here, chans), F32),
        "pre": ((GROUP * here, 512), F32),
        "core_in": ((2, 2, here, width), BF16),
        "x_in": ((2, here, width), BF16),
        "pre_f": ((RING, 2 * rows, chans), F32),
        "pre_b": ((RING, 2 * rows, chans), F32),
        "y_ra": ((4, GROUP, cblk, chans), BF16),
        "z_ra": ((3, GROUP, cblk, chans), BF16),
        "y_rb": ((4, GROUP, cblk, chans), BF16),
        "z_rb": ((3, GROUP, cblk, chans), BF16),
        "y_o": ((4 * cblk, width), BF16),
        "z_o": (((3) * cblk, width), BF16),
        "y_h": ((4, GROUP * blk, hid), BF16),
        "z_h": ((3, GROUP * blk, hid), BF16),
        "y_u": ((4, GROUP * blk, hid), BF16),
        "z_u": ((3, GROUP * blk, hid), BF16),
        "y_d": ((4 * fblk, width), BF16),
        "z_d": (((3) * fblk, width), BF16),
        "acc": ((8, 8, chans), F32),
        "gain_acc": ((2, 8, width), F32),
        "vs": ((RING, 8, chans + piece), F32),
        "vb": ((GROUP, 8, chans + piece), F32),
    }
    names = [*operands, *outputs, *scratch, "send", "recv", "local"]
    in_vmem = pl.BlockSpec(memory_space=pltpu.VMEM)
    in_hbm = pl.BlockSpec(memory_space=pl.ANY)
    shapes = lambda specs: [jax.ShapeDtypeStruct(shape, kind) for shape, kind in specs.values()]
    got = pl.pallas_call(
        functools.partial(fused, names),
        out_shape=shapes(outputs),
        in_specs=[in_hbm] * len(operands),
        out_specs=[in_hbm] * 2 + [in_vmem] * (len(outputs) - 2),
        scratch_shapes=[pltpu.VMEM(shape, kind) for shape, kind in scratch.values()]
        + [pltpu.SemaphoreType.DMA((SLOTS,))] * 2
        + [pltpu.SemaphoreType.DMA((20,))],
        compiler_params=pltpu.CompilerParams(
            collective_id=0, has_side_effects=True, vmem_limit_bytes=VMEM_BYTES
        ),
        name="block",
    )(*operands.values())
    finals = {
        "to_gate": ((blk, channels), F32),
        "to_input": ((blk, channels), F32),
        "to_recur": ((cblk, channels), F32),
        "to_inject": ((cblk, channels), F32),
        "to_o": ((cblk, width), F32),
        "to_hidden": ((blk, GROUP * hid), F32),
        "to_upward": ((blk, GROUP * hid), F32),
        "to_d": ((fblk, width), F32),
        "to_gain_one": ((blk,), F32),
        "to_gain_two": ((blk,), F32),
        "to_taps": ((4, cblk), F32),
        "to_cbias": ((cblk,), F32),
        "to_rbias": ((cblk,), F32),
        "to_ibias": ((cblk,), F32),
        "to_decay": ((cblk,), F32),
    }
    done = pl.pallas_call(
        functools.partial(finish, [*list(outputs)[2:], *finals]),
        out_shape=shapes(finals),
        in_specs=[in_vmem] * (len(outputs) - 2),
        out_specs=[in_vmem] * len(finals),
        name="finish",
    )(*got[2:])
    return (
        got[0].reshape(count, here, width),
        got[1].reshape(count, here, width),
        *done,
    )


def solution(mesh):
    fits = dict(mesh.shape) == {"seq": RING, "batch": GROUP}
    return jax.shard_map(
        split_block if fits else gathered_block,
        mesh=mesh,
        in_specs=(
            P("batch", "seq", None),
            P("batch", "seq"),
            P(("seq", "batch"), None),
            P(("seq", "batch"), None),
            P(("seq", "batch"), None),
            P(("seq", "batch"), None),
            P(("seq", "batch"), None),
            P(("seq", "batch"), None),
            P(("seq", "batch"), None),
            P(("seq", "batch"), None),
            P(),
            P(),
            P(),
            P(),
            P(),
            P(),
            P(),
            P("batch", "seq", None),
        ),
        out_specs=(
            P("batch", "seq", None),
            P("batch", "seq", None),
            P(("seq", "batch"), None),
            P(("seq", "batch"), None),
            P(("seq", "batch"), None),
            P(("seq", "batch"), None),
            P(("seq", "batch"), None),
            P(("seq", "batch"), None),
            P(("seq", "batch"), None),
            P(("seq", "batch"), None),
            P(("seq", "batch")),
            P(("seq", "batch")),
            P(None, ("seq", "batch")),
            P(("seq", "batch")),
            P(("seq", "batch")),
            P(("seq", "batch")),
            P(("seq", "batch")),
        ),
        check_vma=False,
    )
```
